128 devices in a mesh: rep: 16 (over y, x_lo, core), shard: 8 (over x_hi, z).
Axes of the slice: x: 4 (x_hi: 2, x_lo: 2; x = x_hi * 2 + x_lo), y: 4, z: 4, core: 2. Of those that a mesh axis runs over, the one named last changes fastest.
Arguments:
- resid: float32 [32768, 1536], P(('rep', 'shard')), may hold values from -6 to 6
- cotangent: float32 [32768, 1536], P(('rep', 'shard')), may hold values from -6 to 6
- first_length: int32 [16], P('rep'), may hold values from 128 to 1920, as said below
- norm_gain: float32 [1, 1536], replicated, may hold values from 0.5 to 1.5
- in_weight: bfloat16 [1, 1536, 6448], P(None, 'shard'), may hold values from -0.15625 to 0.15625
- conv_weight: float32 [1, 4, 3328], replicated, may hold values from -3 to 3
- conv_bias: float32 [1, 3328], replicated, may hold values from -2 to 2
- dt_bias: float32 [1, 48], replicated, may hold values from -1 to 1
- a_log: float32 [1, 48], replicated, may hold values from -6.2 to -2.8
- skip: float32 [1, 48], replicated, may hold values from 0.5 to 1.5
- gate_gain: float32 [1, 3072], replicated, may hold values from 0.5 to 1.5
- out_weight: bfloat16 [1, 3072, 1536], P(None, 'shard'), may hold values from -0.109375 to 0.109375
Outputs:
- mixed: float32 [32768, 1536], P(('rep', 'shard'))
- resid_grad: float32 [32768, 1536], P(('rep', 'shard'))
- norm_gain_grad: float32 [1, 1536], replicated
- in_weight_grad: float32 [1, 1536, 6448], P(None, 'shard')
- conv_weight_grad: float32 [1, 4, 3328], replicated
- conv_bias_grad: float32 [1, 3328], replicated
- dt_bias_grad: float32 [1, 48], replicated
- a_log_grad: float32 [1, 48], replicated
- skip_grad: float32 [1, 48], replicated
- gate_gain_grad: float32 [1, 3072], replicated
- out_weight_grad: float32 [1, 3072, 1536], P(None, 'shard')
The draws below stay inside these ranges and needn't reach their ends.
Inputs may be any that keep to these rules, and one draw needn't show every extreme that they name: `first_length`: each group's first sequence is either shorter than 256 tokens or longer than 1792, so one of its two sequences covers every device of the group.
All inputs are finite; a program needn't handle non-finite values.
Results may differ from the reference program's by a relative error of at most 0.0095.
Values may be sent and summed in bfloat16 or wider, within the bound.
A program may use at most 256 MiB of HBM per device.

```python
import jax
import jax.numpy as jnp
from jax import lax

D = 1536
HEADS = 48
HEAD_DIM = 64
STATE = 128
CONV = 4
LAYERS = 1
TOK_DEV = 256
INNER = 3072
CONVCH = 3328
PROJ = 6448
GROUP_TOK = 2048
GROUPS = 16
TOKENS = 32768
SPAN = 256


def draw_first_length(key, part):
    key = jax.random.fold_in(key, 11)
    key_short, key_side = jax.random.split(key)
    short_len = jax.random.randint(key_short, (GROUPS,), TOK_DEV // 2, TOK_DEV)
    side_pick = jax.random.randint(key_side, (GROUPS,), 0, 2)
    return jnp.where(side_pick == 1, GROUP_TOK - short_len, short_len).astype(jnp.int32)


def levels(rng, dims, shards, low, top_value):
    gain = 1.0
    for position, parts in shards:
        heights = jax.random.uniform(jax.random.fold_in(jax.random.fold_in(rng, 6), position), (parts,), jnp.float32, low / len(shards), top_value / len(shards))
        gain = gain * jnp.repeat(jnp.exp(heights), dims[position] // parts).reshape((-1,) + (1,) * (len(dims) - 1 - position))
    return gain


def scatter_about(stream_key, extent, width, limit, pieces=(), kind=jnp.bfloat16):
    drawn = width * jax.random.normal(stream_key, extent, jnp.float32)
    if pieces:
        drawn = drawn * levels(stream_key, extent, pieces, -0.22, 0.18)
    return jnp.clip(drawn, -limit, limit).astype(kind)


def setup_inputs(seed: int = 0) -> dict:
    key_of = jax.random.split(jax.random.key(seed), 13)
    resid = scatter_about(key_of[0], (TOKENS, D), 1.0, 6.0, ((0, 128),), jnp.float32)
    cotangent = scatter_about(key_of[1], (TOKENS, D), 1.0, 6.0, ((0, 128),), jnp.float32)
    first_length = draw_first_length(jax.random.fold_in(key_of[12], 71), 0)
    norm_gain = jnp.clip(1.0 + 0.1 * jax.random.normal(key_of[3], (LAYERS, D), jnp.float32), 0.5, 1.5)
    in_weight = scatter_about(key_of[4], (LAYERS, D, PROJ), D ** -0.5, 0.15625, ((1, 8),))
    conv_weight = scatter_about(key_of[5], (LAYERS, CONV, CONVCH), 0.5, 3.0, (), jnp.float32)
    conv_bias = scatter_about(key_of[6], (LAYERS, CONVCH), 0.3, 2.0, (), jnp.float32)
    dt_bias = jnp.clip(jax.random.uniform(key_of[7], (LAYERS, HEADS), jnp.float32, -1.0, 1.0), -1.0, 1.0)
    a_log = jnp.clip(jax.random.uniform(key_of[8], (LAYERS, HEADS), jnp.float32, -6.2, -2.8), -6.2, -2.8)
    skip = jnp.clip(jax.random.uniform(key_of[9], (LAYERS, HEADS), jnp.float32, 0.5, 1.5), 0.5, 1.5)
    gate_gain = jnp.clip(1.0 + 0.1 * jax.random.normal(key_of[10], (LAYERS, INNER), jnp.float32), 0.5, 1.5)
    out_weight = scatter_about(key_of[11], (LAYERS, INNER, D), INNER ** -0.5, 0.109375, ((1, 8),))
    return dict(resid=resid, cotangent=cotangent, first_length=first_length, norm_gain=norm_gain, in_weight=in_weight, conv_weight=conv_weight, conv_bias=conv_bias, dt_bias=dt_bias, a_log=a_log, skip=skip, gate_gain=gate_gain, out_weight=out_weight)


epsilon = 1e-05
highest = lax.Precision.HIGHEST

@jax.custom_vjp
def low(v):
    return lax.optimization_barrier(v.astype(jnp.bfloat16)).astype(jnp.float32)

@jax.custom_vjp
def low_back(v):
    return v

def low_keep(v):
    return (low(v), None)

def low_pass(kept, grad):
    return (grad,)

def back_keep(v):
    return (v, None)

def back_low(kept, grad):
    return (low(grad),)
low.defvjp(low_keep, low_pass)
low_back.defvjp(back_keep, back_low)

def rms_scale(stream, gain_vec):
    inv_scale = lax.rsqrt(lax.optimization_barrier(jnp.mean(stream * stream, axis=-1, keepdims=True)) + epsilon)
    return stream * inv_scale * gain_vec[None, :]

def pre_mix(projected, rim_rows, taps, conv_shift, step_bias, segment, rim_segment):
    length = projected.shape[0]
    gate_part = projected[:, :INNER]
    conv_input = projected[:, INNER:INNER + CONVCH]
    raw_step = projected[:, INNER + CONVCH:]
    padded = jnp.concatenate([rim_rows, conv_input], axis=0)
    all_segments = jnp.concatenate([rim_segment, segment], axis=0)
    convolved = jnp.zeros((length, CONVCH), jnp.float32) + conv_shift[None, :]
    for offset in range(CONV):
        same_seq = (all_segments[offset:offset + length] == segment).astype(jnp.float32)
        convolved = convolved + taps[offset][None, :] * padded[offset:offset + length] * same_seq[:, None]
    activated = jax.nn.silu(convolved)
    head_input = activated[:, :INNER].reshape(length, HEADS, HEAD_DIM)
    b_proj = activated[:, INNER:INNER + STATE]
    c_proj = activated[:, INNER + STATE:]
    step_size = jax.nn.softplus(raw_step + step_bias[None, :])
    return (gate_part, head_input, step_size, b_proj, c_proj)

def block_terms(head_input, step_size, b_proj, c_proj, rate_log, segment, segment_before):
    length = segment.shape[0]
    log_decay = -step_size * jnp.exp(rate_log)[None, :]
    cum_decay = jnp.cumsum(log_decay, axis=0)
    row_index = lax.broadcasted_iota(jnp.int32, (length, length), 0)
    col_index = lax.broadcasted_iota(jnp.int32, (length, length), 1)
    causal_mask = (row_index >= col_index) & (segment[:, None] == segment[None, :])
    decay_rows = cum_decay.T
    gap_decay = decay_rows[:, :, None] - decay_rows[:, None, :]
    weights_in = jnp.where(causal_mask[None], jnp.exp(jnp.where(causal_mask[None], gap_decay, 0.0)), 0.0)
    intersection = jnp.dot(c_proj, b_proj.T, precision=highest)
    scaled_input = head_input * step_size[:, :, None]
    local_out = jnp.einsum('hij,jhp->ihp', weights_in * intersection[None], scaled_input, precision=highest)
    valid = (segment == segment_before).astype(jnp.float32)
    state_weight = jnp.exp(cum_decay) * valid[:, None]
    last_seg = segment[length - 1]
    tail = jnp.exp(cum_decay[length - 1][None, :] - cum_decay) * (segment == last_seg).astype(jnp.float32)[:, None]
    end_state = jnp.einsum('jh,jhp,jn->hpn', tail, scaled_input, b_proj, precision=highest)
    decay_total = jnp.exp(cum_decay[length - 1]) * (last_seg == segment_before).astype(jnp.float32)
    return (local_out, state_weight, end_state, decay_total)

def apply_state(local_out, state_weight, c_proj, state_in):
    return local_out + state_weight[:, :, None] * jnp.einsum('hpn,in->ihp', state_in, c_proj, precision=highest)

def post_mix(mixer_out, head_input, gate_part, skip_vec, gain_vec):
    length = mixer_out.shape[0]
    with_skip = (mixer_out + skip_vec[None, :, None] * head_input).reshape(length, INNER)
    gated_out = with_skip * jax.nn.silu(gate_part)
    inv_scale = lax.rsqrt(lax.optimization_barrier(jnp.mean(gated_out * gated_out, axis=1, keepdims=True)) + epsilon)
    return gated_out * inv_scale * gain_vec[None, :]

def group_ssd(head_input, step_size, b_proj, c_proj, rate_log, segment):
    blocks = GROUP_TOK // SPAN

    def one_block(carried, inputs):
        state_in, segment_before = carried
        block_x, block_step, block_b, block_c, block_seg = inputs
        local_out, state_weight, end_state, decay_total = block_terms(block_x, block_step, block_b, block_c, rate_log, block_seg, segment_before)
        mixer_out = apply_state(local_out, state_weight, block_c, state_in)
        return ((end_state + decay_total[:, None, None] * state_in, block_seg[SPAN - 1]), mixer_out)
    start = (jnp.zeros((HEADS, HEAD_DIM, STATE), jnp.float32), jnp.zeros((), jnp.int32))
    inputs = (head_input.reshape(blocks, SPAN, HEADS, HEAD_DIM), step_size.reshape(blocks, SPAN, HEADS), b_proj.reshape(blocks, SPAN, STATE), c_proj.reshape(blocks, SPAN, STATE), segment.reshape(blocks, SPAN))
    unused, outputs = lax.scan(jax.checkpoint(one_block), start, inputs)
    return outputs.reshape(GROUP_TOK, HEADS, HEAD_DIM)

def two_layers(token_rows, params, segment):
    norm_gain, in_weight, conv_weight, conv_bias, dt_bias, a_log, skip, gate_gain, out_weight = params
    rim_rows = jnp.zeros((CONV - 1, CONVCH), jnp.float32)
    rim_segment = jnp.full((CONV - 1,), -1, jnp.int32)
    stream = token_rows
    for layer_index in range(LAYERS):
        normed_in = low(rms_scale(stream, norm_gain[layer_index]))
        projected = low_back(low(jnp.dot(normed_in, in_weight[layer_index], precision=highest)))
        gate_part, head_input, step_size, b_proj, c_proj = pre_mix(projected, rim_rows, conv_weight[layer_index], conv_bias[layer_index], dt_bias[layer_index], segment, rim_segment)
        mixer_out = group_ssd(head_input, step_size, b_proj, c_proj, a_log[layer_index], segment)
        normed_out = low(post_mix(mixer_out, head_input, gate_part, skip[layer_index], gate_gain[layer_index]))
        stream = stream + low_back(jnp.dot(normed_out, out_weight[layer_index], precision=highest))
    return stream

def reference(resid, cotangent, first_length, norm_gain, in_weight, conv_weight, conv_bias, dt_bias, a_log, skip, gate_gain, out_weight):
    params = (norm_gain.astype(jnp.float32), in_weight.astype(jnp.float32), conv_weight.astype(jnp.float32), conv_bias.astype(jnp.float32), dt_bias.astype(jnp.float32), a_log.astype(jnp.float32), skip.astype(jnp.float32), gate_gain.astype(jnp.float32), out_weight.astype(jnp.float32))
    group_rows = resid.astype(jnp.float32).reshape(GROUPS, GROUP_TOK, D)
    group_cots = cotangent.astype(jnp.float32).reshape(GROUPS, GROUP_TOK, D)

    def one_group(summed, inputs):
        token_rows, group_cot, first_len = inputs
        segment = (jnp.arange(GROUP_TOK, dtype=jnp.int32) >= first_len).astype(jnp.int32)

        def forward(rows_in, params_in):
            return two_layers(rows_in, params_in, segment)
        output, pullback = jax.vjp(forward, token_rows, params)
        rows_grad, params_grad = pullback(group_cot)
        summed = jax.tree.map(lambda left, right: left + right, summed, params_grad)
        return (summed, (output, rows_grad))
    zeros_start = jax.tree.map(jnp.zeros_like, params)
    summed, results = lax.scan(one_group, zeros_start, (group_rows, group_cots, first_length))
    outputs, rows_grads = results
    g_norm, g_in, g_conv, g_bias, g_step, g_rate, g_skip, g_gate, g_out = summed
    return (outputs.reshape(TOKENS, D), rows_grads.reshape(TOKENS, D), g_norm, g_in, g_conv, g_bias, g_step, g_rate, g_skip, g_gate, g_out)
```

```python
import jax
import jax.numpy as jnp
from jax import lax
from jax.experimental import pallas as pl
from jax.experimental.pallas import tpu as pltpu
from jax.sharding import PartitionSpec as P

HEADS = 48
HEAD_DIM = 64
STATE = 128
CONV = 4
INNER = 3072
CONVCH = 3328
MODEL = 1536
SHARDS = 8
OWN = HEADS // SHARDS
CH = OWN * HEAD_DIM
XBC = CH + 2 * STATE
COLS = 2 * CH + 2 * STATE + 128
TOK = 256
GROUP = TOK * SHARDS
L = 128
NB = GROUP // L
HALO = 16
RESET = -200.0

epsilon = 1e-05
F32 = jnp.float32
BF = jnp.bfloat16


def mm(a, b, dims=((1,), (0,))):
    return lax.dot_general(a, b, (dims, ((), ())), preferred_element_type=F32)


def split(v, parts):
    out = []
    for _ in range(parts):
        piece = v.astype(BF)
        out.append(piece)
        v = v - piece.astype(F32)
    return out


def mm_left(ones, v, parts):
    return sum(mm(ones, piece) for piece in split(v, parts))


def mm_right(v, ones, parts):
    return sum(mm(piece, ones) for piece in split(v, parts))


def iota2(shape, dim):
    return lax.broadcasted_iota(jnp.int32, shape, dim)


def head_columns():
    return (iota2((CH, 128), 0) // HEAD_DIM == iota2((CH, 128), 1)).astype(BF)


def spread(per_head):
    lane = iota2((per_head.shape[0], 128), 1)
    tiles = []
    for pair in range(OWN // 2):
        left = per_head[:, 2 * pair : 2 * pair + 1]
        right = per_head[:, 2 * pair + 1 : 2 * pair + 2]
        tiles.append(jnp.where(lane < HEAD_DIM, left, right))
    return jnp.concatenate(tiles, axis=1)


def head_rows(cum_rows, at):
    pieces = [
        jnp.broadcast_to(cum_rows[h : h + 1, at : at + 1], (HEAD_DIM, 1)) for h in range(OWN)
    ]
    return jnp.exp(jnp.concatenate(pieces, axis=0))


def tap_mask(row, first_len, back):
    past = row - first_len
    return jnp.where((past >= 0) & (past < back), 0.0, 1.0)


def block_front(rows, r0, first_len, taps, shift, step_bias, rate_log):
    xbc = rows[:, CH : CH + XBC].astype(F32)
    row = r0 + iota2((L, 1), 0)
    conv = jnp.broadcast_to(shift, (L, XBC))
    for k in range(CONV):
        back = CONV - 1 - k
        term = taps[k : k + 1] * xbc[HALO - back : HALO - back + L]
        if back:
            term = term * tap_mask(row, first_len, back)
        conv = conv + term
    gate = rows[HALO:, :CH].astype(F32)
    raw = rows[HALO:, CH + XBC :].astype(F32) + step_bias
    step = jnp.maximum(raw, 0.0) + jnp.log1p(jnp.exp(-jnp.abs(raw)))
    log_decay = -step * jnp.exp(rate_log)
    with_reset = log_decay + jnp.where(row == first_len, RESET, 0.0)
    lower = (iota2((L, L), 0) >= iota2((L, L), 1)).astype(BF)
    cum = mm_left(lower, with_reset, 3)
    return gate, xbc, conv, raw, step, log_decay, cum


def sigmoid(v):
    return 1.0 / (1.0 + jnp.exp(-v))


def pair_mix(weights, value, dims=((1,), (0,))):
    lane = iota2((L, 128), 1)
    tiles = []
    for pair in range(OWN // 2):
        part = value[:, 128 * pair : 128 * pair + 128]
        tiles.append(
            jnp.where(
                lane < HEAD_DIM,
                mm(weights[2 * pair], part, dims),
                mm(weights[2 * pair + 1], part, dims),
            )
        )
    return jnp.concatenate(tiles, axis=1)


def decay_weights(cum, cum_rows):
    causal = iota2((L, L), 0) >= iota2((L, L), 1)
    out = []
    for h in range(OWN):
        gap = cum[:, h : h + 1] - cum_rows[h : h + 1, :]
        out.append(jnp.exp(jnp.where(causal, gap, -1e30)))
    return out


def to_row(column):
    return jnp.transpose(jnp.broadcast_to(column, (L, L)))[0:1]


def to_column(row):
    return jnp.transpose(jnp.broadcast_to(row, (L, L)))


def forward_kernel(
    first_ref, proj, d_normed, taps, shift, step_bias, rate_log, skip, gain, y_out, states, sums, carry
):
    first_len = first_ref[0]
    carry[...] = jnp.zeros_like(carry)

    def block(b, unused):
        r0 = pl.multiple_of(b * L, L)
        rows = proj[pl.ds(r0, HALO + L), :]
        gate, xbc, conv, raw, step, log_decay, cum = block_front(
            rows, r0, first_len, taps[...], shift[...], step_bias[...], rate_log[...]
        )
        act = conv * sigmoid(conv)
        x = act[:, :CH]
        b_low = act[:, CH : CH + STATE].astype(BF)
        c_low = act[:, CH + STATE :].astype(BF)
        cum_rows = jnp.transpose(cum)
        scores = mm(c_low, b_low, ((1,), (1,)))
        scaled = x * spread(step)
        scaled_low = scaled.astype(BF)
        weights = [(w * scores).astype(BF) for w in decay_weights(cum, cum_rows)]
        state = carry[...]
        states[b] = state
        y = pair_mix(weights, scaled_low)
        y = y + jnp.exp(spread(cum)) * mm(c_low, state.astype(BF), ((1,), (1,)))
        tail = jnp.exp(spread(cum[L - 1 : L] - cum))
        carry[...] = head_rows(cum_rows, L - 1) * state + mm(
            (tail * scaled).astype(BF), b_low, ((0,), (0,))
        )
        y = y + skip[...] * x
        y_out[pl.ds(r0, L), :] = y
        gated = y * (gate * sigmoid(gate))
        normed = gain[...] * d_normed[pl.ds(r0, L), :]
        sums[0, pl.ds(b, 1), :] = to_row(jnp.sum(gated * gated, axis=1, keepdims=True))
        sums[1, pl.ds(b, 1), :] = to_row(jnp.sum(gated * normed, axis=1, keepdims=True))
        return unused

    lax.fori_loop(0, NB, block, 0)
    states[NB] = carry[...]


def backward_kernel(
    first_ref,
    proj,
    d_normed,
    taps,
    shift,
    step_bias,
    rate_log,
    skip,
    gain,
    y_in,
    states,
    sums,
    d_proj,
    small,
    heads,
    carry,
    late,
):
    first_len = first_ref[0]
    carry[...] = jnp.zeros_like(carry)
    late[...] = jnp.zeros_like(late)
    small[...] = jnp.zeros_like(small)
    heads[...] = jnp.zeros_like(heads)
    upper = (iota2((L, L), 1) >= iota2((L, L), 0)).astype(BF)
    columns = head_columns()

    def block(at, unused):
        b = NB - 1 - at
        r0 = pl.multiple_of(b * L, L)
        rows = proj[pl.ds(r0, HALO + L), :]
        gate, xbc, conv, raw, step, log_decay, cum = block_front(
            rows, r0, first_len, taps[...], shift[...], step_bias[...], rate_log[...]
        )
        sig = sigmoid(conv)
        act = conv * sig
        x = act[:, :CH]
        b_low = act[:, CH : CH + STATE].astype(BF)
        c_low = act[:, CH + STATE :].astype(BF)
        cum_rows = jnp.transpose(cum)
        scores = mm(c_low, b_low, ((1,), (1,)))
        step_wide = spread(step)
        scaled = x * step_wide
        scaled_low = scaled.astype(BF)
        decays = decay_weights(cum, cum_rows)

        y = y_in[pl.ds(r0, L), :]
        sig_gate = sigmoid(gate)
        silu_gate = gate * sig_gate
        gated = y * silu_gate
        inv = lax.rsqrt(sums[0, pl.ds(b, 1), :] * (1.0 / INNER) + epsilon)
        back = inv * inv * inv * sums[1, pl.ds(b, 1), :] * (1.0 / INNER)
        inv = jnp.concatenate([to_column(inv)] * (CH // 128), axis=1)
        back = jnp.concatenate([to_column(back)] * (CH // 128), axis=1)
        dn = d_normed[pl.ds(r0, L), :]
        d_gated = inv * gain[...] * dn - gated * back
        dy = d_gated * silu_gate
        d_gate = d_gated * y * (sig_gate + silu_gate * (1.0 - sig_gate))
        dy_low = dy.astype(BF)

        state = states[b]
        end_state = states[b + 1]
        d_state = carry[...]
        state_low = state.astype(BF)
        d_state_low = d_state.astype(BF)
        enter = jnp.exp(spread(cum))
        tail = jnp.exp(spread(cum[L - 1 : L] - cum))
        lane = iota2((L, 128), 1)
        d_scores = jnp.zeros((L, L), F32)
        weights = []
        for h in range(OWN):
            part = slice(128 * (h // 2), 128 * (h // 2) + 128)
            mine = (lane < HEAD_DIM) if h % 2 == 0 else (lane >= HEAD_DIM)
            d_weight = mm(
                dy_low[:, part],
                jnp.where(mine, scaled[:, part], 0.0).astype(BF),
                ((1,), (1,)),
            )
            d_scores = d_scores + d_weight * decays[h]
            weights.append((decays[h] * scores).astype(BF))
        d_scores_low = d_scores.astype(BF)
        d_scaled = pair_mix(weights, dy_low, ((0,), (0,)))
        d_scaled = d_scaled + tail * mm(b_low, d_state_low, ((1,), (1,)))
        enter_dy = (enter * dy).astype(BF)
        d_c = mm(d_scores_low, b_low) + mm(enter_dy, state_low)
        d_b = mm(d_scores_low, c_low, ((0,), (0,))) + mm((tail * scaled).astype(BF), d_state_low)

        ssm = y - skip[...] * x
        d_cum = mm_right(
            dy_low.astype(F32) * ssm - scaled_low.astype(F32) * d_scaled, columns, 3
        )
        through = jnp.zeros((1, 128), F32)
        for piece in split(end_state * d_state, 3):
            through = through + jnp.sum(
                mm(piece, columns, ((0,), (0,))), axis=0, keepdims=True
            )
        d_cum = d_cum + jnp.where(iota2((L, 1), 0) == L - 1, through, 0.0)
        d_log = mm_left(upper, d_cum, 3)
        rate = jnp.exp(rate_log[...])
        d_step = mm_right(d_scaled * x, columns, 3) - rate * d_log
        d_raw = d_step * sigmoid(raw)
        d_x = d_scaled * step_wide + skip[...] * dy

        carry[...] = head_rows(cum_rows, L - 1) * d_state + mm(enter_dy, c_low, ((0,), (0,)))

        d_act = jnp.concatenate([d_x, d_b, d_c], axis=1)
        d_conv = d_act * (sig + act * (1.0 - sig))
        row = r0 + iota2((L + 8, 1), 0)
        longer = jnp.concatenate([d_conv, late[...]], axis=0)
        late[...] = d_conv[:8]
        d_xbc = jnp.zeros((L, XBC), F32)
        for k in range(CONV):
            ahead = CONV - 1 - k
            masked = longer
            if ahead:
                masked = longer * tap_mask(row, first_len, ahead)
            d_xbc = d_xbc + taps[k : k + 1, :] * masked[ahead : ahead + L]
            small[k : k + 1, :] += jnp.sum(
                masked[:L] * xbc[HALO - ahead : HALO - ahead + L], axis=0, keepdims=True
            )
        small[4:5, :] += jnp.sum(d_conv, axis=0, keepdims=True)
        small[5:6, :CH] += jnp.sum(dy * x, axis=0, keepdims=True)
        small[6:7, :CH] += jnp.sum(dn * gated * inv, axis=0, keepdims=True)
        heads[0:1, :] += jnp.sum(d_raw, axis=0, keepdims=True)
        heads[1:2, :] += jnp.sum(d_log * log_decay, axis=0, keepdims=True)
        d_proj[pl.ds(r0, L), :] = jnp.concatenate([d_gate, d_xbc, d_raw], axis=1).astype(BF)
        return unused

    lax.fori_loop(0, NB, block, 0)


VM = pl.BlockSpec(memory_space=pltpu.VMEM)
SM = pl.BlockSpec(memory_space=pltpu.SMEM)
LIMIT = 56 << 20


def rms_scale(stream, gain_vec):
    inv_scale = lax.rsqrt(jnp.mean(stream * stream, axis=-1, keepdims=True) + epsilon)
    return stream * inv_scale * gain_vec[None, :]


def own_lanes(vector, begin, count, width):
    part = lax.dynamic_slice(vector, (begin,), (count,))
    return jnp.pad(part, (0, width - count))[None]


def local(
    resid,
    cotangent,
    first_length,
    norm_gain,
    in_weight,
    conv_weight,
    conv_bias,
    dt_bias,
    a_log,
    skip,
    gate_gain,
    out_weight,
):
    me = lax.axis_index("shard")
    w = in_weight[0]
    rows = w.shape[0]
    normed_in = rms_scale(resid, norm_gain[0]).astype(BF)
    out_low = cotangent.astype(BF)
    wide = jnp.concatenate(
        [w[:, :INNER].reshape(rows, SHARDS, CH), w[:, INNER : 2 * INNER].reshape(rows, SHARDS, CH)],
        axis=2,
    ).transpose(1, 0, 2)
    wide = lax.all_to_all(wide, "shard", 0, 0).reshape(MODEL, 2 * CH)
    narrow = lax.all_gather(w[:, 2 * INNER :], "shard", axis=0, tiled=True)
    w_step = lax.dynamic_slice(narrow, (0, 2 * STATE + me * OWN), (MODEL, OWN))
    w_in = jnp.concatenate(
        [wide, narrow[:, : 2 * STATE], jnp.pad(w_step, ((0, 0), (0, 128 - OWN)))], axis=1
    )
    w_out = out_weight[0]
    all_in = lax.all_gather(normed_in, "shard", axis=0, tiled=True)
    all_low = lax.all_gather(out_low, "shard", axis=0, tiled=True)
    proj = jnp.dot(all_in, w_in, preferred_element_type=F32).astype(BF)
    proj = jnp.pad(proj, ((HALO, 0), (0, 0)))
    d_normed = mm(all_low, w_out, ((1,), (1,)))

    taps = jnp.concatenate(
        [lax.dynamic_slice(conv_weight[0], (0, me * CH), (CONV, CH)), conv_weight[0][:, INNER:]],
        axis=1,
    )
    shift = jnp.concatenate(
        [lax.dynamic_slice(conv_bias[0], (me * CH,), (CH,)), conv_bias[0][INNER:]]
    )[None]
    step_bias = own_lanes(dt_bias[0], me * OWN, OWN, 128)
    rate_log = own_lanes(a_log[0], me * OWN, OWN, 128)
    skip_wide = jnp.repeat(lax.dynamic_slice(skip[0], (me * OWN,), (OWN,)), HEAD_DIM)[None]
    gain = lax.dynamic_slice(gate_gain[0], (me * CH,), (CH,))[None]
    params = (taps, shift, step_bias, rate_log, skip_wide, gain)

    y, states, sums = pl.pallas_call(
        forward_kernel,
        out_shape=(
            jax.ShapeDtypeStruct((GROUP, CH), F32),
            jax.ShapeDtypeStruct((NB + 1, CH, STATE), F32),
            jax.ShapeDtypeStruct((2, NB, L), F32),
        ),
        in_specs=[SM] + [VM] * 8,
        out_specs=(VM,) * 3,
        scratch_shapes=[pltpu.VMEM((CH, STATE), F32)],
        compiler_params=pltpu.CompilerParams(vmem_limit_bytes=LIMIT),
    )(first_length, proj, d_normed, *params)
    sums = lax.psum(sums, "shard")

    inv = lax.rsqrt(sums[0].reshape(GROUP, 1) * (1.0 / INNER) + epsilon)
    normed_out = (y * jax.nn.silu(proj[HALO:, :CH].astype(F32)) * inv * gain).astype(BF)
    mixed_part = mm(normed_out, w_out).astype(BF)
    mixed = resid + lax.psum_scatter(mixed_part, "shard", scatter_dimension=0, tiled=True).astype(F32)
    out_part = mm(normed_out, all_low, ((0,), (0,)))

    d_proj, small, heads = pl.pallas_call(
        backward_kernel,
        out_shape=(
            jax.ShapeDtypeStruct((GROUP, COLS), BF),
            jax.ShapeDtypeStruct((8, XBC), F32),
            jax.ShapeDtypeStruct((8, 128), F32),
        ),
        in_specs=[SM] + [VM] * 11,
        out_specs=(VM,) * 3,
        scratch_shapes=[pltpu.VMEM((CH, STATE), F32), pltpu.VMEM((8, XBC), F32)],
        compiler_params=pltpu.CompilerParams(vmem_limit_bytes=LIMIT),
    )(first_length, proj, d_normed, *params, y, states, sums)

    in_part = mm(all_in, d_proj, ((0,), (0,)))
    d_in_part = mm(d_proj, w_in, ((1,), (1,))).astype(BF)
    d_in = lax.psum_scatter(d_in_part, "shard", scatter_dimension=0, tiled=True).astype(F32)
    unused, norm_pull = jax.vjp(rms_scale, resid, norm_gain[0])
    d_stream, d_norm_gain = norm_pull(d_in)
    grad = cotangent + d_stream

    wide_part = in_part[:, : 2 * CH].astype(BF).reshape(SHARDS, rows, 2 * CH)
    wide_sum = lax.all_to_all(wide_part, "shard", 0, 0).transpose(1, 0, 2)
    narrow_part = jnp.zeros((MODEL, 2 * STATE + HEADS), F32)
    narrow_part = narrow_part.at[:, : 2 * STATE].set(in_part[:, 2 * CH : 2 * CH + 2 * STATE])
    narrow_part = lax.dynamic_update_slice(
        narrow_part, in_part[:, 2 * CH + 2 * STATE :][:, :OWN], (0, 2 * STATE + me * OWN)
    ).astype(BF)
    narrow_sum = lax.psum_scatter(narrow_part, "shard", scatter_dimension=0, tiled=True)
    in_share = jnp.concatenate(
        [wide_sum[:, :, :CH].reshape(rows, INNER), wide_sum[:, :, CH:].reshape(rows, INNER), narrow_sum],
        axis=1,
    )
    in_grad, out_grad = lax.psum((in_share, out_part.astype(BF)), "rep")

    def place(own, rest, total):
        full = jnp.zeros((own.shape[0], total), F32)
        full = lax.dynamic_update_slice(full, own, (0, me * own.shape[1]))
        return full if rest is None else full.at[:, total - rest.shape[1] :].set(rest)

    conv_parts = place(small[:5, :CH], small[:5, CH:], CONVCH)
    skip_part = jnp.sum(small[5, :CH].reshape(OWN, HEAD_DIM), axis=1)[None]
    per_head = place(jnp.concatenate([heads[:2, :OWN], skip_part], axis=0), None, HEADS)
    gain_part = place(small[6:7, :CH], None, INNER)
    g_conv, g_head, g_gain, g_norm = lax.psum(
        (conv_parts, per_head, gain_part, d_norm_gain[None]), ("rep", "shard")
    )
    return (
        mixed,
        grad,
        g_norm,
        in_grad.astype(F32)[None],
        g_conv[:CONV][None],
        g_conv[4:5],
        g_head[0:1],
        g_head[1:2],
        g_head[2:3],
        g_gain,
        out_grad.astype(F32)[None],
    )


def solution(mesh):
    rows = P(("rep", "shard"), None)
    weight = P(None, "shard", None)
    return jax.shard_map(
        local,
        mesh=mesh,
        in_specs=(rows, rows, P("rep"), P(), weight, P(), P(), P(), P(), P(), P(), weight),
        out_specs=(rows, rows, P(), weight, P(), P(), P(), P(), P(), P(), weight),
        check_vma=False,
    )
```

```python
import jax
import jax.numpy as jnp
from jax import lax
from jax.experimental import pallas as pl
from jax.experimental.pallas import tpu as pltpu
from jax.sharding import PartitionSpec as P

HEADS = 48
HEAD_DIM = 64
STATE = 128
CONV = 4
INNER = 3072
CONVCH = 3328
MODEL = 1536
SHARDS = 8
OWN = HEADS // SHARDS
CH = OWN * HEAD_DIM
XBC = CH + 2 * STATE
HALF = 640
COLS = 2 * CH + 2 * STATE + 128
BC = 2 * STATE
TOK = 256
GROUP = TOK * SHARDS
L = 128
NB = GROUP // L
HALO = 16
PIECE = 48
MESH = pl.DeviceIdType.MESH
RESET = -200.0

epsilon = 1e-05
F32 = jnp.float32
BF = jnp.bfloat16


def mm(a, b, dims=((1,), (0,))):
    return lax.dot_general(a, b, (dims, ((), ())), preferred_element_type=F32)


def split(v, parts):
    out = []
    for _ in range(parts):
        piece = v.astype(BF)
        out.append(piece)
        v = v - piece.astype(F32)
    return out


def mm_left(ones, v, parts):
    return sum(mm(ones, piece) for piece in split(v, parts))


def mm_right(v, ones, parts):
    return sum(mm(piece, ones) for piece in split(v, parts))


def iota2(shape, dim):
    return lax.broadcasted_iota(jnp.int32, shape, dim)


def head_columns():
    return (iota2((CH, 128), 0) // HEAD_DIM == iota2((CH, 128), 1)).astype(BF)


def spread(per_head):
    lane = iota2((per_head.shape[0], 128), 1)
    tiles = []
    for pair in range(OWN // 2):
        left = per_head[:, 2 * pair : 2 * pair + 1]
        right = per_head[:, 2 * pair + 1 : 2 * pair + 2]
        tiles.append(jnp.where(lane < HEAD_DIM, left, right))
    return jnp.concatenate(tiles, axis=1)


def head_rows(cum_rows, at):
    pieces = [
        jnp.broadcast_to(cum_rows[h : h + 1, at : at + 1], (HEAD_DIM, 1)) for h in range(OWN)
    ]
    return jnp.exp(jnp.concatenate(pieces, axis=0))


def tap_mask(row, first_len, back):
    past = row - first_len
    return jnp.where((past >= 0) & (past < back), 0.0, 1.0)


def block_front(rows, r0, first_len, taps, shift, step_bias, rate_log):
    xbc = rows[:, CH : CH + XBC].astype(F32)
    row = r0 + iota2((L, 1), 0)
    conv = jnp.broadcast_to(shift, (L, XBC))
    for k in range(CONV):
        back = CONV - 1 - k
        term = taps[k : k + 1] * xbc[HALO - back : HALO - back + L]
        if back:
            term = term * tap_mask(row, first_len, back)
        conv = conv + term
    gate = rows[HALO:, :CH].astype(F32)
    raw = rows[HALO:, CH + XBC :].astype(F32) + step_bias
    step = jnp.maximum(raw, 0.0) + jnp.log1p(jnp.exp(-jnp.abs(raw)))
    log_decay = -step * jnp.exp(rate_log)
    with_reset = log_decay + jnp.where(row == first_len, RESET, 0.0)
    lower = (iota2((L, L), 0) >= iota2((L, L), 1)).astype(BF)
    cum = mm_left(lower, with_reset, 3)
    return gate, xbc, conv, raw, step, log_decay, cum


def sigmoid(v):
    return 1.0 / (1.0 + jnp.exp(-v))


def pair_mix(weights, value, dims=((1,), (0,))):
    lane = iota2((L, 128), 1)
    tiles = []
    for pair in range(OWN // 2):
        part = value[:, 128 * pair : 128 * pair + 128]
        tiles.append(
            jnp.where(
                lane < HEAD_DIM,
                mm(weights[2 * pair], part, dims),
                mm(weights[2 * pair + 1], part, dims),
            )
        )
    return jnp.concatenate(tiles, axis=1)


def decay_weights(cum, cum_rows):
    causal = iota2((L, L), 0) >= iota2((L, L), 1)
    out = []
    for h in range(OWN):
        gap = cum[:, h : h + 1] - cum_rows[h : h + 1, :]
        out.append(jnp.exp(jnp.where(causal, gap, -1e30)))
    return out


def to_row(column):
    return jnp.transpose(jnp.broadcast_to(column, (L, L)))[0:1]


def to_column(row):
    return jnp.transpose(jnp.broadcast_to(row, (L, L)))


def forward_block(b, first_len, proj, taps, shift, step_bias, rate_log, skip, y_out, states, sums, carry):
    r0 = pl.multiple_of(b * L, L)
    rows = proj[pl.ds(r0, HALO + L), :]
    gate, xbc, conv, raw, step, log_decay, cum = block_front(
        rows, r0, first_len, taps, shift, step_bias, rate_log
    )
    act = conv * sigmoid(conv)
    x = act[:, BC:]
    b_low = act[:, :STATE].astype(BF)
    c_low = act[:, STATE:BC].astype(BF)
    cum_rows = jnp.transpose(cum)
    scores = mm(c_low, b_low, ((1,), (1,)))
    scaled = x * spread(step)
    scaled_low = scaled.astype(BF)
    weights = [(w * scores).astype(BF) for w in decay_weights(cum, cum_rows)]
    state = carry[...]
    states[b] = state
    y = pair_mix(weights, scaled_low)
    y = y + jnp.exp(spread(cum)) * mm(c_low, state.astype(BF), ((1,), (1,)))
    tail = jnp.exp(spread(cum[L - 1 : L] - cum))
    carry[...] = head_rows(cum_rows, L - 1) * state + mm(
        (tail * scaled).astype(BF), b_low, ((0,), (0,))
    )
    y = y + skip * x
    y_out[pl.ds(r0, L), :] = y
    gated = y * (gate * sigmoid(gate))
    sums[pl.ds(b, 1), :] = to_row(jnp.sum(gated * gated, axis=1, keepdims=True))


def place_of():
    rep, me = lax.axis_index("rep"), lax.axis_index("shard")
    hi, z = me // 4, lax.rem(me, 4)
    left = hi * 4 + lax.rem(z + 3, 4)
    right = hi * 4 + lax.rem(z + 1, 4)
    far = hi * 4 + lax.rem(z + 2, 4)
    across = lax.rem(me + 4, 8)
    return rep, me, left, right, far, across


def other_side(block):
    return lax.rem(block + 4, 8)


def enter(rep, me):
    barrier = pltpu.get_barrier_semaphore()
    peers = [(rep, lax.rem(me + o, SHARDS)) for o in range(1, SHARDS)]
    peers += [(lax.rem(rep + 4 * o, 16), me) for o in range(1, 4)]
    peers.append((rep + 1 - 2 * lax.rem(rep, 2), me))
    for peer in peers:
        pl.semaphore_signal(barrier, inc=1, device_id=peer, device_id_type=MESH)
    pl.semaphore_wait(barrier, len(peers))


class Gather:
    def __init__(self, blocks, send, recv):
        self.blocks, self.send, self.recv = blocks, send, recv
        self.rep, self.me, self.left, self.right, self.far, self.across = place_of()

    def move(self, channel, block, to, rows=None):
        ref = self.blocks.at[block] if rows is None else self.blocks.at[block, pl.ds(rows, TOK // 2)]
        return pltpu.make_async_remote_copy(
            src_ref=ref,
            dst_ref=ref,
            send_sem=self.send.at[channel],
            recv_sem=self.recv.at[channel],
            device_id=(self.rep, to),
            device_id_type=MESH,
        )

    def outgoing(self, channel):
        me, left, right, across = self.me, self.left, self.right, self.across
        return (
            lambda: self.move(0, me, right),
            lambda: self.move(1, me, left),
            lambda: self.move(2, me, across),
            lambda: self.move(3, left, right, 0),
            lambda: self.move(4, right, left, TOK // 2),
            lambda: self.move(5, across, right),
            lambda: self.move(6, across, left),
            lambda: self.move(7, self.far, across, 0),
            lambda: self.move(8, self.far, across, TOK // 2),
        )[channel]()

    def incoming(self, channel):
        left, right, far, across = self.left, self.right, self.far, self.across
        return (
            lambda: self.move(0, left, left),
            lambda: self.move(1, right, right),
            lambda: self.move(2, across, across),
            lambda: self.move(3, far, left, 0),
            lambda: self.move(4, far, right, TOK // 2),
            lambda: self.move(5, other_side(left), left),
            lambda: self.move(6, other_side(right), right),
            lambda: self.move(7, other_side(far), across, 0),
            lambda: self.move(8, other_side(far), across, TOK // 2),
        )[channel]()

    def start(self, *channels):
        for channel in channels:
            self.outgoing(channel).start()

    def arrived(self, *channels):
        for channel in channels:
            self.incoming(channel).wait_recv()

    def sent(self):
        for channel in range(9):
            self.outgoing(channel).wait_send()


def own_heads(vector, me):
    pick = (iota2((HEADS, 128), 0) == iota2((HEADS, 128), 1) + me * OWN) & (
        iota2((HEADS, 128), 1) < OWN
    )
    wide = jnp.broadcast_to(vector, (8, HEADS))
    return mm_right(wide, pick.astype(BF), 3)[0:1]


def own_channels(vector, me):
    pick = iota2((HEADS, CH), 0) == iota2((HEADS, CH), 1) // HEAD_DIM + me * OWN
    wide = jnp.broadcast_to(vector, (8, HEADS))
    return mm_right(wide, pick.astype(BF), 3)[0:1]


def own_slices(me, conv_weight, conv_bias):
    own = pl.ds(pl.multiple_of(me * CH, 128), CH)
    taps = jnp.concatenate([conv_weight[:, INNER:], conv_weight[:, own]], axis=1)
    shift = jnp.concatenate([conv_bias[:, INNER:], conv_bias[:, own]], axis=1)
    return taps, shift


def front_kernel(
    first_ref, resid, cotangent, w_in, narrow, w_out, norm_gain, conv_weight, conv_bias, dt_bias,
    a_log, skip, gate_gain, x_out, low_out, w_all_out, proj_out, y_out, states_out, normed_out, sums_out,
    x_all, low_all, w_all, proj, y, states, d_normed, sums, carry, stage, taps, shift,
    x_send, x_recv, low_send, low_recv, piece_send, piece_recv, y_send, y_recv, core_send, core_recv,
    sum_send, sum_recv, here,
):
    rep, me, left, right, far, across = place_of()
    core = lax.rem(rep, 2)
    along_y = rep // 4
    first_len = first_ref[0]
    load_resid = pltpu.make_async_copy(resid, stage.at[0], here.at[0])
    load_cot = pltpu.make_async_copy(cotangent, stage.at[1], here.at[1])
    load_resid.start()
    load_cot.start()
    enter(rep, me)

    own_rows = pl.ds(pl.multiple_of(along_y * PIECE, 16), PIECE)

    def landing(block):
        return pl.ds(pl.multiple_of(block * 192 + along_y * PIECE, 16), PIECE)

    def weight_pieces(to, make):
        wide = pl.ds(pl.multiple_of(core * INNER + to * CH, 128), CH)
        half = pl.ds(pl.multiple_of(core * BC, 128), BC)
        make(w_in.at[own_rows, wide], w_all.at[core, landing(me), pl.ds(0, CH)])
        make(narrow.at[own_rows, half], w_all.at[core, landing(me), pl.ds(CH, BC)])

    for o in range(1, SHARDS):
        to = lax.rem(me + o, SHARDS)
        weight_pieces(
            to,
            lambda src, dst: pltpu.make_async_remote_copy(
                src_ref=src, dst_ref=dst, send_sem=piece_send.at[o], recv_sem=piece_recv.at[o],
                device_id=(rep, to), device_id_type=MESH,
            ).start(),
        )
    weight_pieces(me, lambda src, dst: pltpu.make_async_copy(src, dst, here.at[2]).start())

    load_resid.wait()
    rows = stage[0]
    scale = lax.rsqrt(jnp.mean(rows * rows, axis=1, keepdims=True) + epsilon)
    x_all[me] = (rows * scale * norm_gain[...]).astype(BF)
    gather_x = Gather(x_all, x_send, x_recv)
    gather_x.start(0, 1, 2)
    load_cot.wait()
    low_all[me] = stage[1].astype(BF)
    gather_low = Gather(low_all, low_send, low_recv)

    taps_now, shift_now = own_slices(me, conv_weight, conv_bias)
    taps[...] = taps_now
    shift[...] = shift_now
    proj[pl.ds(0, HALO), :] = jnp.zeros((HALO, COLS), BF)
    carry[...] = jnp.zeros_like(carry)

    pltpu.make_async_copy(
        w_all.at[core, landing(me)], w_all.at[core, landing(me)], here.at[2]
    ).wait()
    for o in range(1, SHARDS):
        source = lax.rem(me + SHARDS - o, SHARDS)
        piece = w_all.at[core, landing(source)]
        pltpu.make_async_remote_copy(
            src_ref=piece, dst_ref=piece, send_sem=piece_send.at[o], recv_sem=piece_recv.at[o],
            device_id=(rep, source), device_id_type=MESH,
        ).wait()
    for o in range(1, 4):
        for block in range(SHARDS):
            piece = w_all.at[core, landing(block)]
            pltpu.make_async_remote_copy(
                src_ref=piece, dst_ref=piece, send_sem=y_send.at[o], recv_sem=y_recv.at[o],
                device_id=(lax.rem(rep + 4 * o, 16), me), device_id_type=MESH,
            ).start()
    gather_x.arrived(0)
    gather_x.start(3)
    gather_x.arrived(1)
    gather_x.start(4)
    gather_x.arrived(2)
    gather_x.start(5, 6)
    gather_x.arrived(3)
    gather_x.start(7)
    gather_x.arrived(4)
    gather_x.start(8)
    gather_low.start(0, 1, 2)
    for o in range(1, 4):
        quarter = w_all.at[core, pl.ds(0, SHARDS * PIECE)]
        pltpu.make_async_remote_copy(
            src_ref=quarter, dst_ref=quarter, send_sem=y_send.at[o], recv_sem=y_recv.at[o],
            device_id=(lax.rem(rep + 4 * o, 16), me), device_id_type=MESH,
        ).wait()

    def halves(which):
        return pltpu.make_async_remote_copy(
            src_ref=w_all.at[which], dst_ref=w_all.at[which], send_sem=core_send.at[0],
            recv_sem=core_recv.at[0], device_id=(rep + 1 - 2 * core, me), device_id_type=MESH,
        )

    halves(core).start()
    halves(1 - core).wait_recv()
    halves(core).wait_send()
    pick = (iota2((128, 128), 0) == iota2((128, 128), 1) + me * OWN) & (iota2((128, 128), 1) < OWN)
    w_all[1, :, CH : CH + 128] = mm(w_all[1, :, CH : CH + 128], pick.astype(BF)).astype(BF)

    side = (me // 4) * 4

    def project(at, unused):
        rows = x_all[at]
        begin = pl.multiple_of(HALO + at * TOK, 16)
        proj[pl.ds(begin, TOK), :HALF] = mm(rows, w_all[0]).astype(BF)
        proj[pl.ds(begin, TOK), HALF:] = mm(rows, w_all[1, :, : CH + 128]).astype(BF)
        return unused

    lax.fori_loop(side, side + 4, project, 0)
    gather_low.arrived(0)
    gather_low.start(3)
    gather_low.arrived(1)
    gather_low.start(4)
    gather_x.arrived(5, 6, 7, 8)
    lax.fori_loop(4 - side, 8 - side, project, 0)
    gather_low.arrived(2)
    gather_low.start(5, 6)

    step_bias = own_heads(dt_bias[...], me)
    rate_log = own_heads(a_log[...], me)
    skip_wide = own_channels(skip[...], me)

    def scan(b, unused):
        @pl.when(b == 6)
        def relay_a():
            gather_low.arrived(3)
            gather_low.start(7)

        @pl.when(b == 8)
        def relay_b():
            gather_low.arrived(4)
            gather_low.start(8)

        forward_block(
            b, first_len, proj, taps[...], shift[...], step_bias, rate_log, skip_wide, y, states,
            sums.at[me, 0], carry,
        )
        return unused

    lax.fori_loop(0, NB, scan, 0)
    states[NB] = carry[...]

    gain = gate_gain[:, pl.ds(pl.multiple_of(me * CH, 128), CH)]

    def normed(at, unused):
        begin = pl.multiple_of(at * TOK, TOK)
        dn = mm(low_all[at], w_out[...], ((1,), (1,)))
        d_normed[pl.ds(begin, TOK), :] = dn
        gate = proj[pl.ds(HALO + begin, TOK), :CH].astype(F32)
        gated = y[pl.ds(begin, TOK), :] * (gate * sigmoid(gate))
        both = jnp.sum(gated * gain * dn, axis=1, keepdims=True)
        sums[me, 1, pl.ds(2 * at, 1), :] = to_row(both[:L])
        sums[me, 1, pl.ds(2 * at + 1, 1), :] = to_row(both[L:])
        return unused

    lax.fori_loop(side, side + 4, normed, 0)
    gather_low.arrived(5, 6, 7, 8)
    lax.fori_loop(4 - side, 8 - side, normed, 0)

    def sum_copy(o, slot, to):
        return pltpu.make_async_remote_copy(
            src_ref=sums.at[slot], dst_ref=sums.at[slot], send_sem=sum_send.at[o],
            recv_sem=sum_recv.at[o], device_id=(rep, to), device_id_type=MESH,
        )

    for o in range(1, SHARDS):
        sum_copy(o, me, lax.rem(me + o, SHARDS)).start()
    for o in range(1, SHARDS):
        source = lax.rem(me + SHARDS - o, SHARDS)
        sum_copy(o, source, source).wait_recv()
    for o in range(1, SHARDS):
        sum_copy(o, me, lax.rem(me + o, SHARDS)).wait_send()
    total = sums[0]
    for slot in range(1, SHARDS):
        total = total + sums[slot]
    sums_out[...] = total
    gather_x.sent()
    gather_low.sent()
    keep = (
        (x_all, x_out), (low_all, low_out), (w_all, w_all_out), (proj, proj_out), (y, y_out),
        (states, states_out), (d_normed, normed_out),
    )
    for at, (src, dst) in enumerate(keep):
        pltpu.make_async_copy(src, dst, here.at[3 + at]).start()
    for at, (src, dst) in enumerate(keep):
        pltpu.make_async_copy(src, dst, here.at[3 + at]).wait()


def backward_kernel(
    first_ref,
    proj,
    d_normed,
    taps,
    shift,
    step_bias,
    rate_log,
    skip,
    gain,
    y_in,
    states,
    sums,
    d_proj,
    small,
    heads,
    carry,
    late,
):
    first_len = first_ref[0]
    carry[...] = jnp.zeros_like(carry)
    late[...] = jnp.zeros_like(late)
    small[...] = jnp.zeros_like(small)
    heads[...] = jnp.zeros_like(heads)
    upper = (iota2((L, L), 1) >= iota2((L, L), 0)).astype(BF)
    columns = head_columns()

    def block(at, unused):
        b = NB - 1 - at
        r0 = pl.multiple_of(b * L, L)
        rows = proj[pl.ds(r0, HALO + L), :]
        gate, xbc, conv, raw, step, log_decay, cum = block_front(
            rows, r0, first_len, taps[...], shift[...], step_bias[...], rate_log[...]
        )
        sig = sigmoid(conv)
        act = conv * sig
        x = act[:, BC:]
        b_low = act[:, :STATE].astype(BF)
        c_low = act[:, STATE:BC].astype(BF)
        cum_rows = jnp.transpose(cum)
        scores = mm(c_low, b_low, ((1,), (1,)))
        step_wide = spread(step)
        scaled = x * step_wide
        scaled_low = scaled.astype(BF)
        decays = decay_weights(cum, cum_rows)

        y = y_in[pl.ds(r0, L), :]
        sig_gate = sigmoid(gate)
        silu_gate = gate * sig_gate
        gated = y * silu_gate
        inv = lax.rsqrt(sums[0, pl.ds(b, 1), :] * (1.0 / INNER) + epsilon)
        back = inv * inv * inv * sums[1, pl.ds(b, 1), :] * (1.0 / INNER)
        inv = jnp.concatenate([to_column(inv)] * (CH // 128), axis=1)
        back = jnp.concatenate([to_column(back)] * (CH // 128), axis=1)
        dn = d_normed[pl.ds(r0, L), :]
        d_gated = inv * gain[...] * dn - gated * back
        dy = d_gated * silu_gate
        d_gate = d_gated * y * (sig_gate + silu_gate * (1.0 - sig_gate))
        dy_low = dy.astype(BF)

        state = states[b]
        end_state = states[b + 1]
        d_state = carry[...]
        state_low = state.astype(BF)
        d_state_low = d_state.astype(BF)
        enter = jnp.exp(spread(cum))
        tail = jnp.exp(spread(cum[L - 1 : L] - cum))
        lane = iota2((L, 128), 1)
        d_scores = jnp.zeros((L, L), F32)
        weights = []
        for h in range(OWN):
            part = slice(128 * (h // 2), 128 * (h // 2) + 128)
            mine = (lane < HEAD_DIM) if h % 2 == 0 else (lane >= HEAD_DIM)
            d_weight = mm(
                dy_low[:, part],
                jnp.where(mine, scaled[:, part], 0.0).astype(BF),
                ((1,), (1,)),
            )
            d_scores = d_scores + d_weight * decays[h]
            weights.append((decays[h] * scores).astype(BF))
        d_scores_low = d_scores.astype(BF)
        d_scaled = pair_mix(weights, dy_low, ((0,), (0,)))
        d_scaled = d_scaled + tail * mm(b_low, d_state_low, ((1,), (1,)))
        enter_dy = (enter * dy).astype(BF)
        d_c = mm(d_scores_low, b_low) + mm(enter_dy, state_low)
        d_b = mm(d_scores_low, c_low, ((0,), (0,))) + mm((tail * scaled).astype(BF), d_state_low)

        ssm = y - skip[...] * x
        d_cum = mm_right(
            dy_low.astype(F32) * ssm - scaled_low.astype(F32) * d_scaled, columns, 3
        )
        through = jnp.zeros((1, 128), F32)
        for piece in split(end_state * d_state, 3):
            through = through + jnp.sum(
                mm(piece, columns, ((0,), (0,))), axis=0, keepdims=True
            )
        d_cum = d_cum + jnp.where(iota2((L, 1), 0) == L - 1, through, 0.0)
        d_log = mm_left(upper, d_cum, 3)
        rate = jnp.exp(rate_log[...])
        d_step = mm_right(d_scaled * x, columns, 3) - rate * d_log
        d_raw = d_step * sigmoid(raw)
        d_x = d_scaled * step_wide + skip[...] * dy

        carry[...] = head_rows(cum_rows, L - 1) * d_state + mm(enter_dy, c_low, ((0,), (0,)))

        d_act = jnp.concatenate([d_b, d_c, d_x], axis=1)
        d_conv = d_act * (sig + act * (1.0 - sig))
        row = r0 + iota2((L + 8, 1), 0)
        longer = jnp.concatenate([d_conv, late[...]], axis=0)
        late[...] = d_conv[:8]
        d_xbc = jnp.zeros((L, XBC), F32)
        for k in range(CONV):
            ahead = CONV - 1 - k
            masked = longer
            if ahead:
                masked = longer * tap_mask(row, first_len, ahead)
            d_xbc = d_xbc + taps[k : k + 1, :] * masked[ahead : ahead + L]
            small[k : k + 1, :] += jnp.sum(
                masked[:L] * xbc[HALO - ahead : HALO - ahead + L], axis=0, keepdims=True
            )
        small[4:5, :] += jnp.sum(d_conv, axis=0, keepdims=True)
        small[5:6, :CH] += jnp.sum(dy * x, axis=0, keepdims=True)
        small[6:7, :CH] += jnp.sum(dn * gated * inv, axis=0, keepdims=True)
        heads[0:1, :] += jnp.sum(d_raw, axis=0, keepdims=True)
        heads[1:2, :] += jnp.sum(d_log * log_decay, axis=0, keepdims=True)
        d_proj[pl.ds(r0, L), :] = jnp.concatenate([d_gate, d_xbc, d_raw], axis=1).astype(BF)
        return unused

    lax.fori_loop(0, NB, block, 0)


VM = pl.BlockSpec(memory_space=pltpu.VMEM)
SM = pl.BlockSpec(memory_space=pltpu.SMEM)
ANY = pl.BlockSpec(memory_space=pl.ANY)
LIMIT = 56 << 20


def rms_scale(stream, gain_vec):
    inv_scale = lax.rsqrt(jnp.mean(stream * stream, axis=-1, keepdims=True) + epsilon)
    return stream * inv_scale * gain_vec[None, :]


def own_lanes(vector, begin, count, width):
    part = lax.dynamic_slice(vector, (begin,), (count,))
    return jnp.pad(part, (0, width - count))[None]


def local(
    resid,
    cotangent,
    first_length,
    norm_gain,
    in_weight,
    conv_weight,
    conv_bias,
    dt_bias,
    a_log,
    skip,
    gate_gain,
    out_weight,
):
    me = lax.axis_index("shard")
    w = in_weight[0]
    rows = w.shape[0]
    narrow = jnp.pad(w[:, 2 * INNER :], ((0, 0), (0, 4 * 128 - BC - HEADS)))
    w_out = out_weight[0]
    shapes = (
        ((SHARDS, TOK, MODEL), BF), ((SHARDS, TOK, MODEL), BF), ((2, MODEL, HALF), BF),
        ((HALO + GROUP, COLS), BF), ((GROUP, CH), F32), ((NB + 1, CH, STATE), F32), ((GROUP, CH), F32),
    )
    dma = pltpu.SemaphoreType.DMA
    x_all, low_all, w_all, proj, y, states, d_normed, sums = pl.pallas_call(
        front_kernel,
        out_shape=tuple(jax.ShapeDtypeStruct(*shape) for shape in shapes)
        + (jax.ShapeDtypeStruct((2, NB, L), F32),),
        in_specs=[SM, ANY, ANY, ANY, ANY] + [VM] * 8,
        out_specs=(ANY,) * 7 + (VM,),
        scratch_shapes=[pltpu.VMEM(*shape) for shape in shapes]
        + [
            pltpu.VMEM((SHARDS, 2, NB, L), F32),
            pltpu.VMEM((CH, STATE), F32),
            pltpu.VMEM((2, TOK, MODEL), F32),
            pltpu.VMEM((CONV, XBC), F32),
            pltpu.VMEM((1, XBC), F32),
        ]
        + [dma((9,))] * 4 + [dma((SHARDS,))] * 2 + [dma((4,))] * 2 + [dma((1,))] * 2
        + [dma((SHARDS,))] * 2 + [dma((10,))],
        compiler_params=pltpu.CompilerParams(
            vmem_limit_bytes=LIMIT, collective_id=0, has_side_effects=True
        ),
    )(
        first_length, resid, cotangent, w, narrow, w_out, norm_gain, conv_weight[0], conv_bias, dt_bias,
        a_log, skip, gate_gain,
    )
    all_in = x_all.reshape(GROUP, MODEL)
    all_low = low_all.reshape(GROUP, MODEL)
    w_in = jnp.concatenate([w_all[0], w_all[1][:, : CH + 128]], axis=1)
    taps = jnp.concatenate(
        [conv_weight[0][:, INNER:], lax.dynamic_slice(conv_weight[0], (0, me * CH), (CONV, CH))],
        axis=1,
    )
    shift = jnp.concatenate(
        [conv_bias[0][INNER:], lax.dynamic_slice(conv_bias[0], (me * CH,), (CH,))]
    )[None]
    step_bias = own_lanes(dt_bias[0], me * OWN, OWN, 128)
    rate_log = own_lanes(a_log[0], me * OWN, OWN, 128)
    skip_wide = jnp.repeat(lax.dynamic_slice(skip[0], (me * OWN,), (OWN,)), HEAD_DIM)[None]
    gain = lax.dynamic_slice(gate_gain[0], (me * CH,), (CH,))[None]
    params = (taps, shift, step_bias, rate_log, skip_wide, gain)

    inv = lax.rsqrt(sums[0].reshape(GROUP, 1) * (1.0 / INNER) + epsilon)
    normed_out = (y * jax.nn.silu(proj[HALO:, :CH].astype(F32)) * inv * gain).astype(BF)
    mixed_part = mm(normed_out, w_out).astype(BF)
    mixed = resid + lax.psum_scatter(mixed_part, "shard", scatter_dimension=0, tiled=True).astype(F32)
    out_part = mm(normed_out, all_low, ((0,), (0,)))

    d_proj, small, heads = pl.pallas_call(
        backward_kernel,
        out_shape=(
            jax.ShapeDtypeStruct((GROUP, COLS), BF),
            jax.ShapeDtypeStruct((8, XBC), F32),
            jax.ShapeDtypeStruct((8, 128), F32),
        ),
        in_specs=[SM] + [VM] * 11,
        out_specs=(VM,) * 3,
        scratch_shapes=[pltpu.VMEM((CH, STATE), F32), pltpu.VMEM((8, XBC), F32)],
        compiler_params=pltpu.CompilerParams(vmem_limit_bytes=LIMIT),
    )(first_length, proj, d_normed, *params, y, states, sums)

    in_part = mm(all_in, d_proj, ((0,), (0,)))
    d_in_part = mm(d_proj, w_in, ((1,), (1,))).astype(BF)
    d_in = lax.psum_scatter(d_in_part, "shard", scatter_dimension=0, tiled=True).astype(F32)
    unused, norm_pull = jax.vjp(rms_scale, resid, norm_gain[0])
    d_stream, d_norm_gain = norm_pull(d_in)
    grad = cotangent + d_stream

    wide_part = jnp.concatenate([in_part[:, :CH], in_part[:, HALF : HALF + CH]], axis=1)
    wide_part = wide_part.astype(BF).reshape(SHARDS, rows, 2 * CH)
    wide_sum = lax.all_to_all(wide_part, "shard", 0, 0).transpose(1, 0, 2)
    narrow_part = jnp.zeros((MODEL, 2 * STATE + HEADS), F32)
    narrow_part = narrow_part.at[:, : 2 * STATE].set(in_part[:, CH : CH + BC])
    narrow_part = lax.dynamic_update_slice(
        narrow_part, in_part[:, HALF + CH :][:, :OWN], (0, 2 * STATE + me * OWN)
    ).astype(BF)
    narrow_sum = lax.psum_scatter(narrow_part, "shard", scatter_dimension=0, tiled=True)
    in_share = jnp.concatenate(
        [wide_sum[:, :, :CH].reshape(rows, INNER), wide_sum[:, :, CH:].reshape(rows, INNER), narrow_sum],
        axis=1,
    )
    in_grad, out_grad = lax.psum((in_share, out_part.astype(BF)), "rep")

    def place(own, rest, total):
        full = jnp.zeros((own.shape[0], total), F32)
        full = lax.dynamic_update_slice(full, own, (0, me * own.shape[1]))
        return full if rest is None else full.at[:, total - rest.shape[1] :].set(rest)

    conv_parts = place(small[:5, BC:], small[:5, :BC], CONVCH)
    skip_part = jnp.sum(small[5, :CH].reshape(OWN, HEAD_DIM), axis=1)[None]
    per_head = place(jnp.concatenate([heads[:2, :OWN], skip_part], axis=0), None, HEADS)
    gain_part = place(small[6:7, :CH], None, INNER)
    g_conv, g_head, g_gain, g_norm = lax.psum(
        (conv_parts, per_head, gain_part, d_norm_gain[None]), ("rep", "shard")
    )
    return (
        mixed,
        grad,
        g_norm,
        in_grad.astype(F32)[None],
        g_conv[:CONV][None],
        g_conv[4:5],
        g_head[0:1],
        g_head[1:2],
        g_head[2:3],
        g_gain,
        out_grad.astype(F32)[None],
    )


def solution(mesh):
    rows = P(("rep", "shard"), None)
    weight = P(None, "shard", None)
    return jax.shard_map(
        local,
        mesh=mesh,
        in_specs=(rows, rows, P("rep"), P(), weight, P(), P(), P(), P(), P(), P(), weight),
        out_specs=(rows, rows, P(), weight, P(), P(), P(), P(), P(), P(), weight),
        check_vma=False,
    )
```

```python
import jax
import jax.numpy as jnp
from jax import lax
from jax.experimental import pallas as pl
from jax.experimental.pallas import tpu as pltpu
from jax.sharding import PartitionSpec as P

HEADS = 48
HEAD_DIM = 64
STATE = 128
CONV = 4
INNER = 3072
CONVCH = 3328
MODEL = 1536
SHARDS = 8
OWN = HEADS // SHARDS
CH = OWN * HEAD_DIM
XBC = CH + 2 * STATE
HALF = 640
COLS = 2 * CH + 2 * STATE + 128
BC = 2 * STATE
TOK = 256
GROUP = TOK * SHARDS
L = 128
NB = GROUP // L
HALO = 16
PIECE = 48
MESH = pl.DeviceIdType.MESH
ROWS = MODEL // SHARDS
QUARTER = SHARDS * PIECE
TAIL = 8 * 256 + 128
CHUNK = 16
HALF_OUT = MODEL // 2
WIDE = 512
OUT_PART = pl.ds(MODEL, CH)
RESET = -200.0

epsilon = 1e-05
F32 = jnp.float32
BF = jnp.bfloat16


def mm(a, b, dims=((1,), (0,))):
    return lax.dot_general(a, b, (dims, ((), ())), preferred_element_type=F32)


def split(v, parts):
    out = []
    for _ in range(parts):
        piece = v.astype(BF)
        out.append(piece)
        v = v - piece.astype(F32)
    return out


def mm_left(ones, v, parts):
    return sum(mm(ones, piece) for piece in split(v, parts))


def mm_right(v, ones, parts):
    return sum(mm(piece, ones) for piece in split(v, parts))


def iota2(shape, dim):
    return lax.broadcasted_iota(jnp.int32, shape, dim)


def head_columns():
    return (iota2((CH, 128), 0) // HEAD_DIM == iota2((CH, 128), 1)).astype(BF)


def spread(per_head):
    lane = iota2((per_head.shape[0], 128), 1)
    tiles = []
    for pair in range(OWN // 2):
        left = per_head[:, 2 * pair : 2 * pair + 1]
        right = per_head[:, 2 * pair + 1 : 2 * pair + 2]
        tiles.append(jnp.where(lane < HEAD_DIM, left, right))
    return jnp.concatenate(tiles, axis=1)


def head_rows(cum_rows, at):
    pieces = [
        jnp.broadcast_to(cum_rows[h : h + 1, at : at + 1], (HEAD_DIM, 1)) for h in range(OWN)
    ]
    return jnp.exp(jnp.concatenate(pieces, axis=0))


def tap_mask(row, first_len, back):
    past = row - first_len
    return jnp.where((past >= 0) & (past < back), 0.0, 1.0)


def block_front(rows, r0, first_len, taps, shift, step_bias, rate_log):
    xbc = rows[:, CH : CH + XBC].astype(F32)
    row = r0 + iota2((L, 1), 0)
    conv = jnp.broadcast_to(shift, (L, XBC))
    for k in range(CONV):
        back = CONV - 1 - k
        term = taps[k : k + 1] * xbc[HALO - back : HALO - back + L]
        if back:
            term = term * tap_mask(row, first_len, back)
        conv = conv + term
    gate = rows[HALO:, :CH].astype(F32)
    raw = rows[HALO:, CH + XBC :].astype(F32) + step_bias
    step = jnp.maximum(raw, 0.0) + jnp.log1p(jnp.exp(-jnp.abs(raw)))
    log_decay = -step * jnp.exp(rate_log)
    with_reset = log_decay + jnp.where(row == first_len, RESET, 0.0)
    lower = (iota2((L, L), 0) >= iota2((L, L), 1)).astype(BF)
    cum = mm_left(lower, with_reset, 3)
    return gate, xbc, conv, raw, step, log_decay, cum


def sigmoid(v):
    return 1.0 / (1.0 + jnp.exp(-v))


def pair_mix(weights, value, dims=((1,), (0,))):
    lane = iota2((L, 128), 1)
    tiles = []
    for pair in range(OWN // 2):
        part = value[:, 128 * pair : 128 * pair + 128]
        tiles.append(
            jnp.where(
                lane < HEAD_DIM,
                mm(weights[2 * pair], part, dims),
                mm(weights[2 * pair + 1], part, dims),
            )
        )
    return jnp.concatenate(tiles, axis=1)


def decay_weights(cum, cum_rows):
    causal = iota2((L, L), 0) >= iota2((L, L), 1)
    out = []
    for h in range(OWN):
        gap = cum[:, h : h + 1] - cum_rows[h : h + 1, :]
        out.append(jnp.exp(jnp.where(causal, gap, -1e30)))
    return out


def to_row(column):
    return jnp.transpose(jnp.broadcast_to(column, (L, L)))[0:1]


def to_column(row):
    return jnp.transpose(jnp.broadcast_to(row, (L, L)))


def forward_block(b, first_len, proj, taps, shift, step_bias, rate_log, skip, y_out, states, sums, carry):
    r0 = pl.multiple_of(b * L, L)
    rows = proj[pl.ds(r0, HALO + L), :]
    gate, xbc, conv, raw, step, log_decay, cum = block_front(
        rows, r0, first_len, taps, shift, step_bias, rate_log
    )
    act = conv * sigmoid(conv)
    x = act[:, BC:]
    b_low = act[:, :STATE].astype(BF)
    c_low = act[:, STATE:BC].astype(BF)
    cum_rows = jnp.transpose(cum)
    scores = mm(c_low, b_low, ((1,), (1,)))
    scaled = x * spread(step)
    scaled_low = scaled.astype(BF)
    weights = [(w * scores).astype(BF) for w in decay_weights(cum, cum_rows)]
    state = carry[...]
    states[b] = state
    y = pair_mix(weights, scaled_low)
    y = y + jnp.exp(spread(cum)) * mm(c_low, state.astype(BF), ((1,), (1,)))
    tail = jnp.exp(spread(cum[L - 1 : L] - cum))
    carry[...] = head_rows(cum_rows, L - 1) * state + mm(
        (tail * scaled).astype(BF), b_low, ((0,), (0,))
    )
    y = y + skip * x
    y_out[pl.ds(r0, L), :] = y
    gated = y * (gate * sigmoid(gate))
    sums[pl.ds(b, 1), :] = to_row(jnp.sum(gated * gated, axis=1, keepdims=True))


def place_of():
    rep, me = lax.axis_index("rep"), lax.axis_index("shard")
    hi, z = me // 4, lax.rem(me, 4)
    left = hi * 4 + lax.rem(z + 3, 4)
    right = hi * 4 + lax.rem(z + 1, 4)
    far = hi * 4 + lax.rem(z + 2, 4)
    across = lax.rem(me + 4, 8)
    return rep, me, left, right, far, across


def sibling(rep, me):
    return rep + 1 - 2 * lax.rem(rep, 2), me


def beside(rep, me):
    return rep + 2 - 4 * lax.rem(rep // 2, 2), me


def other_side(block):
    return lax.rem(block + 4, 8)


def enter(rep, me):
    barrier = pltpu.get_barrier_semaphore()
    peers = [(rep, lax.rem(me + o, SHARDS)) for o in range(1, SHARDS)]
    peers += [(lax.rem(rep + o, 16), me) for o in range(1, 16)]
    for peer in peers:
        pl.semaphore_signal(barrier, inc=1, device_id=peer, device_id_type=MESH)
    return lambda: pl.semaphore_wait(barrier, len(peers))


def block_rows(block, half=None):
    if half is None:
        return pl.ds(pl.multiple_of(block * TOK, TOK), TOK)
    return pl.ds(pl.multiple_of(block * TOK + half, TOK // 2), TOK // 2)


class Gather:
    def __init__(self, blocks, send, recv):
        self.blocks, self.send, self.recv = blocks, send, recv
        self.rep, self.me, self.left, self.right, self.far, self.across = place_of()

    def move(self, channel, block, to, rows=None):
        ref = self.blocks.at[block_rows(block, rows)]
        return pltpu.make_async_remote_copy(
            src_ref=ref,
            dst_ref=ref,
            send_sem=self.send.at[channel],
            recv_sem=self.recv.at[channel],
            device_id=(self.rep, to),
            device_id_type=MESH,
        )

    def outgoing(self, channel):
        me, left, right, across = self.me, self.left, self.right, self.across
        return (
            lambda: self.move(0, me, right),
            lambda: self.move(1, me, left),
            lambda: self.move(2, me, across),
            lambda: self.move(3, left, right, 0),
            lambda: self.move(4, right, left, TOK // 2),
            lambda: self.move(5, across, right),
            lambda: self.move(6, across, left),
            lambda: self.move(7, self.far, across, 0),
            lambda: self.move(8, self.far, across, TOK // 2),
        )[channel]()

    def incoming(self, channel):
        left, right, far, across = self.left, self.right, self.far, self.across
        return (
            lambda: self.move(0, left, left),
            lambda: self.move(1, right, right),
            lambda: self.move(2, across, across),
            lambda: self.move(3, far, left, 0),
            lambda: self.move(4, far, right, TOK // 2),
            lambda: self.move(5, other_side(left), left),
            lambda: self.move(6, other_side(right), right),
            lambda: self.move(7, other_side(far), across, 0),
            lambda: self.move(8, other_side(far), across, TOK // 2),
        )[channel]()

    def start(self, *channels):
        for channel in channels:
            self.outgoing(channel).start()

    def arrived(self, *channels):
        for channel in channels:
            self.incoming(channel).wait_recv()

    def sent(self):
        for channel in range(9):
            self.outgoing(channel).wait_send()


class Scatter:
    SLOTS = ((0, None), (1, None), (2, None), (3, 0), (3, TOK // 2), (4, None), (5, None), (6, None))

    def __init__(self, part, out, into, send, recv):
        self.part, self.out, self.into, self.send, self.recv = part, out, into, send, recv
        self.rep, self.me, self.left, self.right, self.far, self.across = place_of()
        self.to = (
            self.across, self.left, self.right, self.left, self.right, self.right, self.left, self.across,
        )

    def copy(self, channel):
        slot, rows = self.SLOTS[channel]
        at = (slot,) if rows is None else (slot, pl.ds(rows, TOK // 2))
        return pltpu.make_async_remote_copy(
            src_ref=self.out.at[at],
            dst_ref=self.into.at[at],
            send_sem=self.send.at[channel],
            recv_sem=self.recv.at[channel],
            device_id=(self.rep, self.to[channel]),
            device_id_type=MESH,
        )

    def arrived(self, *channels):
        for channel in channels:
            self.copy(channel).wait_recv()

    def fill(self, slot, block, *arrived):
        for at in range(0, MODEL, WIDE):
            lanes = slice(at, at + WIDE)
            value = self.part(block, lanes)
            for other in arrived:
                value = value + self.into[other, :, lanes].astype(F32)
            self.out[slot, :, lanes] = value.astype(BF)

    def leaf(self, slot):
        self.fill(slot, other_side((self.far, self.left, self.right)[slot]))
        self.copy(slot).start()

    def middle(self):
        self.arrived(0)
        self.fill(3, self.far, 0)
        self.copy(3).start()
        self.copy(4).start()
        self.arrived(1, 2)
        self.fill(6, self.across, 1, 2)
        self.copy(7).start()

    def last(self):
        half = TOK // 2
        self.fill(4, self.right)
        self.fill(5, self.left)
        self.arrived(3, 4)
        for slot, rows in ((4, slice(half, TOK)), (5, slice(0, half))):
            value = self.out[slot, rows].astype(F32) + self.into[3, rows].astype(F32)
            self.out[slot, rows] = value.astype(BF)
            self.copy(1 + slot).start()

    def total(self, lanes):
        value = self.part(self.me, lanes)
        for slot in (4, 5, 6):
            value = value + self.into[slot, :, lanes].astype(F32)
        return value

    def sent(self):
        for channel in range(8):
            self.copy(channel).wait_send()


def own_heads(vector, me):
    pick = (iota2((HEADS, 128), 0) == iota2((HEADS, 128), 1) + me * OWN) & (
        iota2((HEADS, 128), 1) < OWN
    )
    wide = jnp.broadcast_to(vector, (8, HEADS))
    return mm_right(wide, pick.astype(BF), 3)[0:1]


def own_channels(vector, me):
    pick = iota2((HEADS, CH), 0) == iota2((HEADS, CH), 1) // HEAD_DIM + me * OWN
    wide = jnp.broadcast_to(vector, (8, HEADS))
    return mm_right(wide, pick.astype(BF), 3)[0:1]


def own_slices(me, conv_weight, conv_bias):
    own = pl.ds(pl.multiple_of(me * CH, 128), CH)
    taps = jnp.concatenate([conv_weight[:, INNER:], conv_weight[:, own]], axis=1)
    shift = jnp.concatenate([conv_bias[:, INNER:], conv_bias[:, own]], axis=1)
    return taps, shift


def layer_kernel(
    first_ref, resid, cotangent, w_in, narrow, w_out, norm_gain, conv_weight, conv_bias, dt_bias,
    a_log, skip, gate_gain,
    mixed_out, grad_out, gates_out, tail_out, outs_out, small_out, norm_out,
    x_all, low_all, w_all, proj, y, states, d_normed, sums, carry, stage, taps, shift,
    totals, normed_out, gain_sum, norm_sum, small, heads, late, scatter_out, scatter_in,
    near_y, core_out, core_gate, near_out, near_gate, part_out, part_gate, side_out, side_gate,
    quarter, gates, outs,
    tail_swap, tail_pieces, tail,
    packed, packed_in, packed_y, packed_all, norm_parts, norm_all,
    x_send, x_recv, low_send, low_recv, piece_send, piece_recv, y_send, y_recv, core_send, core_recv,
    sum_send, sum_recv, here, mix_send, mix_recv, grad_send, grad_recv, g_send, g_recv, norm_send, norm_recv, owner_send, owner_recv, free, core_free,
):
    rep, me, left, right, far, across = place_of()
    core = lax.rem(rep, 2)
    along_y = rep // 4
    first_len = first_ref[0]
    load_resid = pltpu.make_async_copy(resid, stage.at[0], here.at[0])
    load_cot = pltpu.make_async_copy(cotangent, stage.at[1], here.at[1])
    load_resid.start()
    load_cot.start()
    all_entered = enter(rep, me)

    load_resid.wait()

    def norm_rows(at, unused):
        rows = stage[0, pl.ds(pl.multiple_of(at * CHUNK, CHUNK), CHUNK), :]
        scale = lax.rsqrt(jnp.mean(rows * rows, axis=1, keepdims=True) + epsilon)
        own = pl.ds(pl.multiple_of(me * TOK + at * CHUNK, CHUNK), CHUNK)
        x_all[own, :] = (rows * scale * norm_gain[...]).astype(BF)
        return unused

    lax.fori_loop(0, TOK // CHUNK, norm_rows, 0)
    all_entered()
    gather_x = Gather(x_all, x_send, x_recv)
    gather_x.start(0, 1, 2)

    own_rows = pl.ds(pl.multiple_of(along_y * PIECE, 16), PIECE)

    def landing(block):
        return pl.ds(pl.multiple_of(block * 192 + along_y * PIECE, 16), PIECE)

    def weight_pieces(to, make):
        wide = pl.ds(pl.multiple_of(core * INNER + to * CH, 128), CH)
        half = pl.ds(pl.multiple_of(core * BC, 128), BC)
        make(w_in.at[own_rows, wide], w_all.at[core, landing(me), pl.ds(0, CH)])
        make(narrow.at[own_rows, half], w_all.at[core, landing(me), pl.ds(CH, BC)])

    for o in range(1, SHARDS):
        to = lax.rem(me + o, SHARDS)
        weight_pieces(
            to,
            lambda src, dst: pltpu.make_async_remote_copy(
                src_ref=src, dst_ref=dst, send_sem=piece_send.at[o], recv_sem=piece_recv.at[o],
                device_id=(rep, to), device_id_type=MESH,
            ).start(),
        )
    weight_pieces(me, lambda src, dst: pltpu.make_async_copy(src, dst, here.at[2]).start())

    load_cot.wait()
    low_all[block_rows(me), :] = stage[1].astype(BF)
    gather_low = Gather(low_all, low_send, low_recv)

    taps_now, shift_now = own_slices(me, conv_weight, conv_bias)
    taps[...] = taps_now
    shift[...] = shift_now
    proj[pl.ds(0, HALO), :] = jnp.zeros((HALO, COLS), BF)
    carry[...] = jnp.zeros_like(carry)

    pltpu.make_async_copy(
        w_all.at[core, landing(me)], w_all.at[core, landing(me)], here.at[2]
    ).wait()
    for o in range(1, SHARDS):
        source = lax.rem(me + SHARDS - o, SHARDS)
        piece = w_all.at[core, landing(source)]
        pltpu.make_async_remote_copy(
            src_ref=piece, dst_ref=piece, send_sem=piece_send.at[o], recv_sem=piece_recv.at[o],
            device_id=(rep, source), device_id_type=MESH,
        ).wait()
    for o in range(1, 4):
        for block in range(SHARDS):
            piece = w_all.at[core, landing(block)]
            pltpu.make_async_remote_copy(
                src_ref=piece, dst_ref=piece, send_sem=y_send.at[o], recv_sem=y_recv.at[o],
                device_id=(lax.rem(rep + 4 * o, 16), me), device_id_type=MESH,
            ).start()
    gather_x.arrived(0)
    gather_x.start(3)
    gather_x.arrived(1)
    gather_x.start(4)
    gather_x.arrived(2)
    gather_x.start(5, 6)
    gather_x.arrived(3)
    gather_x.start(7)
    gather_x.arrived(4)
    gather_x.start(8)
    gather_low.start(0, 1, 2)
    for o in range(1, 4):
        landed = w_all.at[core, pl.ds(0, QUARTER)]
        pltpu.make_async_remote_copy(
            src_ref=landed, dst_ref=landed, send_sem=y_send.at[o], recv_sem=y_recv.at[o],
            device_id=(lax.rem(rep + 4 * o, 16), me), device_id_type=MESH,
        ).wait()

    def halves(which):
        return pltpu.make_async_remote_copy(
            src_ref=w_all.at[which], dst_ref=w_all.at[which], send_sem=core_send.at[0],
            recv_sem=core_recv.at[0], device_id=(rep + 1 - 2 * core, me), device_id_type=MESH,
        )

    halves(core).start()
    halves(1 - core).wait_recv()
    halves(core).wait_send()
    pick = (iota2((128, 128), 0) == iota2((128, 128), 1) + me * OWN) & (iota2((128, 128), 1) < OWN)
    w_all[1, :, CH : CH + 128] = mm(w_all[1, :, CH : CH + 128], pick.astype(BF)).astype(BF)

    side = (me // 4) * 4

    def project(at, unused):
        rows = x_all[block_rows(at), :]
        begin = pl.multiple_of(HALO + at * TOK, 16)
        proj[pl.ds(begin, TOK), :HALF] = mm(rows, w_all[0]).astype(BF)
        proj[pl.ds(begin, TOK), HALF:] = mm(rows, w_all[1, :, : CH + 128]).astype(BF)
        return unused

    lax.fori_loop(side, side + 4, project, 0)
    gather_low.arrived(0)
    gather_low.start(3)
    gather_low.arrived(1)
    gather_low.start(4)
    gather_x.arrived(5, 6, 7, 8)
    lax.fori_loop(4 - side, 8 - side, project, 0)

    step_bias = own_heads(dt_bias[...], me)
    rate_log = own_heads(a_log[...], me)
    skip_wide = own_channels(skip[...], me)

    def scan(b, unused):
        @pl.when(b == 6)
        def relay():
            gather_low.arrived(3, 4, 2)
            gather_low.start(7, 8, 5, 6)

        forward_block(
            b, first_len, proj, taps[...], shift[...], step_bias, rate_log, skip_wide, y, states,
            sums.at[me, 0], carry,
        )
        return unused

    lax.fori_loop(0, NB, scan, 0)
    states[NB] = carry[...]

    gain = gate_gain[:, pl.ds(pl.multiple_of(me * CH, 128), CH)]

    def normed(at, unused):
        begin = pl.multiple_of(at * TOK, TOK)
        dn = mm(low_all[block_rows(at), :], w_out[...], ((1,), (1,)))
        d_normed[pl.ds(begin, TOK), :] = dn.astype(BF)
        gate = proj[pl.ds(HALO + begin, TOK), :CH].astype(F32)
        gated = y[pl.ds(begin, TOK), :] * (gate * sigmoid(gate))
        both = jnp.sum(gated * gain * dn, axis=1, keepdims=True)
        sums[me, 1, pl.ds(2 * at, 1), :] = to_row(both[:L])
        sums[me, 1, pl.ds(2 * at + 1, 1), :] = to_row(both[L:])
        return unused

    lax.fori_loop(side, side + 4, normed, 0)
    gather_low.arrived(5, 6)

    def normed_near(at, unused):
        return normed(other_side(side + lax.rem(me + at, 4)), unused)

    lax.fori_loop(3, 6, normed_near, 0)
    gather_low.arrived(7, 8)
    lax.fori_loop(6, 7, normed_near, 0)

    def sum_copy(o, slot, to):
        return pltpu.make_async_remote_copy(
            src_ref=sums.at[slot], dst_ref=sums.at[slot], send_sem=sum_send.at[o],
            recv_sem=sum_recv.at[o], device_id=(rep, to), device_id_type=MESH,
        )

    for o in range(1, SHARDS):
        sum_copy(o, me, lax.rem(me + o, SHARDS)).start()
    for o in range(1, SHARDS):
        source = lax.rem(me + SHARDS - o, SHARDS)
        sum_copy(o, source, source).wait_recv()
    for o in range(1, SHARDS):
        sum_copy(o, me, lax.rem(me + o, SHARDS)).wait_send()
    total = sums[0]
    for slot in range(1, SHARDS):
        total = total + sums[slot]
    totals[...] = total

    def send(index, src, dst, to):
        return pltpu.make_async_remote_copy(
            src_ref=src, dst_ref=dst, send_sem=g_send.at[index], recv_sem=g_recv.at[index],
            device_id=to, device_id_type=MESH,
        )

    def y_peer(o):
        return lax.rem(rep + 4 * o, 16), me

    def y_of(o):
        return lax.rem(along_y + o, 4)

    gain_sum[...] = jnp.zeros_like(gain_sum)
    small[...] = jnp.zeros_like(small)
    heads[...] = jnp.zeros_like(heads)
    late[...] = jnp.zeros_like(late)
    carry[...] = jnp.zeros_like(carry)

    def prepare(b, unused):
        prepare_block(b, proj, y, d_normed, totals, gain, normed_out, gain_sum)
        return unused

    def mixed_part(block, lanes):
        return mm(normed_out[block_rows(block), :], w_out[:, lanes])

    mix = Scatter(mixed_part, scatter_out, scatter_in, mix_send, mix_recv)
    def prepare_two(block):
        lax.fori_loop(2 * block, 2 * block + 2, prepare, 0)

    for slot, block in enumerate((far, left, right)):
        prepare_two(other_side(block))
        mix.leaf(slot)
    prepare_two(across)
    lax.fori_loop(2 * side, 2 * side + 8, prepare, 0)

    gather_low.sent()
    def out_tile(at, unused):
        lanes = pl.ds(pl.multiple_of(at * 256, 256), 256)
        low = low_all[:, lanes]
        low_all[OUT_PART, lanes] = mm(normed_out[...], low, ((0,), (0,))).astype(BF)
        return unused

    def gate_tile(at, unused):
        lanes = pl.ds(pl.multiple_of(at * 256, 256), 256)
        rows = x_all[:, lanes]
        low_all[lanes, :CH] = mm(rows, proj[HALO:, :CH], ((0,), (0,))).astype(BF)
        return unused

    def y_rows(block, y_at):
        return pl.ds(pl.multiple_of(block * ROWS + y_at * PIECE, 16), PIECE)

    def out_rows(y_at, base=0):
        return pl.ds(pl.multiple_of(base + y_at * 96, 16), 96)

    def part_columns(which):
        return pl.ds(pl.multiple_of(which * CH, 128), CH)

    def out_half(which):
        return pl.ds(pl.multiple_of(which * HALF_OUT, 128), HALF_OUT)

    def gate_half(which):
        return pl.ds(pl.multiple_of(which * HALF_OUT, 128), HALF_OUT)

    core_copies = (
        send(1, low_all.at[OUT_PART, out_half(1 - core)], core_out, sibling(rep, me)),
        send(2, low_all.at[gate_half(1 - core), pl.ds(0, CH)], core_gate, sibling(rep, me)),
    )
    lax.fori_loop(0, MODEL // 256, out_tile, 0)
    core_copies[0].start()
    lax.fori_loop(0, MODEL // 256, gate_tile, 0)
    core_copies[1].start()

    def gate_piece(block, y_at):
        return pl.ds(pl.multiple_of(core * HALF_OUT + block * ROWS + y_at * PIECE, 16), PIECE)

    def out_to_y(o):
        src = low_all.at[out_rows(y_of(o), MODEL), out_half(core)]
        return send(2 + o, src, near_out.at[o - 1], y_peer(o))

    def gate_to_y(o, block):
        dst = near_gate.at[o - 1, pl.ds(block * PIECE, PIECE)]
        return send(5 + o, low_all.at[gate_piece(block, y_of(o)), pl.ds(0, CH)], dst, y_peer(o))

    def core_sum():
        for copy in core_copies:
            copy.wait()
        mine = out_half(core)
        both = low_all[OUT_PART, mine].astype(F32) + core_out[...].astype(F32)
        low_all[OUT_PART, mine] = both.astype(BF)
        both = low_all[gate_half(core), :CH].astype(F32) + core_gate[...].astype(F32)
        low_all[gate_half(core), :CH] = both.astype(BF)
        for o in range(1, 4):
            out_to_y(o).start()
            for block in range(SHARDS // 2):
                gate_to_y(o, block).start()

    side_copies = (
        send(9, part_gate, side_gate, beside(rep, me)),
        send(10, part_out, side_out, beside(rep, me)),
    )

    def y_sum():
        for o in range(1, 4):
            out_to_y(o).wait()
            landed = low_all.at[pl.ds(0, HALF_OUT // 4), pl.ds(0, CH)]
            send(5 + o, landed, near_gate.at[o - 1], y_peer(o)).wait()
        total = low_all[out_rows(along_y, MODEL), out_half(core)].astype(F32)
        for o in range(3):
            total = total + near_out[o].astype(F32)
        part_out[...] = total.astype(BF)
        for block in range(SHARDS // 2):
            rows = slice(block * PIECE, (block + 1) * PIECE)
            total = low_all[gate_piece(block, along_y), :CH].astype(F32)
            for o in range(3):
                total = total + near_gate[o, rows].astype(F32)
            part_gate[rows] = total.astype(BF)
        for copy in side_copies:
            copy.start()
        pl.semaphore_signal(
            core_free, inc=1, device_id=sibling(rep, me), device_id_type=MESH
        )

    own_piece = pl.ds(pl.multiple_of(along_y * PIECE, 16), PIECE)

    def gate_columns(block):
        return pl.ds(pl.multiple_of(block * CH, 128), CH)

    def own_quarter(block):
        return pl.ds(pl.multiple_of(block * PIECE, 16), PIECE)

    owner_here = core == me // 4

    def from_shard(o):
        source = lax.rem(me + SHARDS - o, SHARDS)
        dst = gates.at[own_piece, gate_columns(source)]
        return pltpu.make_async_remote_copy(
            src_ref=dst, dst_ref=dst, send_sem=owner_send.at[me], recv_sem=owner_recv.at[source],
            device_id=(rep, source), device_id_type=MESH,
        )

    def owner_copy(block):
        to = core * (SHARDS // 2) + block
        return pltpu.make_async_remote_copy(
            src_ref=part_gate.at[pl.ds(block * PIECE, PIECE)], dst_ref=gates.at[own_piece, gate_columns(me)],
            send_sem=owner_send.at[block], recv_sem=owner_recv.at[me], device_id=(rep, to),
            device_id_type=MESH,
        )

    def each_owner(act):
        for block in range(SHARDS // 2):

            @pl.when(core * (SHARDS // 2) + block != me)
            def other():
                act(owner_copy(block))

    def own_outs(y_at):
        return outs.at[out_rows(y_at), out_half(core)]

    def side_sum():
        for copy in side_copies:
            copy.wait()
        part_gate[...] = (part_gate[...].astype(F32) + side_gate[...].astype(F32)).astype(BF)
        total = part_out[...].astype(F32) + side_out[...].astype(F32)
        outs[out_rows(along_y), out_half(core)] = total.astype(BF)
        each_owner(lambda copy: copy.start())

        @pl.when(owner_here)
        def keep():
            own = pl.ds(pl.multiple_of(lax.rem(me, 4) * PIECE, 16), PIECE)
            gates[own_piece, gate_columns(me)] = part_gate[own, :]

        for o in range(1, 4):
            send(14 + o, own_outs(along_y), own_outs(along_y), y_peer(o)).start()

    def share_gates():
        each_owner(lambda copy: copy.wait_send())

        @pl.when(owner_here)
        def collect():
            for o in range(1, SHARDS):
                from_shard(o).wait_recv()
            for o in range(1, 4):
                src = gates.at[own_piece]
                send(18 + o, src, src, y_peer(o)).start()

    def to_sibling():
        for o in range(1, 4):
            src = own_outs(y_of(4 - o))
            send(14 + o, src, src, y_peer(o)).wait()
        send(22, outs.at[:, out_half(core)], outs.at[:, out_half(core)], sibling(rep, me)).start()

        @pl.when(owner_here)
        def share():
            for o in range(1, 4):
                src = gates.at[pl.ds(pl.multiple_of(y_of(4 - o) * PIECE, 16), PIECE)]
                send(18 + o, src, src, y_peer(o)).wait()
            send(23, gates, gates, sibling(rep, me)).start()

    def early_done():
        send(22, outs.at[:, out_half(core)], outs.at[:, out_half(core)], sibling(rep, me)).wait_send()
        theirs = outs.at[:, out_half(1 - core)]
        send(22, theirs, theirs, sibling(rep, me)).wait_recv()

        @pl.when(owner_here)
        def sent():
            send(23, gates, gates, sibling(rep, me)).wait_send()

        @pl.when(jnp.logical_not(owner_here))
        def got():
            send(23, gates, gates, sibling(rep, me)).wait_recv()

        pltpu.make_async_copy(gates, gates_out, here.at[3]).start()
        pltpu.make_async_copy(outs, outs_out, here.at[10]).start()

    def backward(at, unused):
        @pl.when(at == 1)
        def hook_a():
            core_sum()

        @pl.when(at == 4)
        def hook_b():
            mix.middle()

        @pl.when(at == 10)
        def hook_c():
            y_sum()

        @pl.when(at == 9)
        def hook_d():
            mix.last()

        @pl.when(at == 13)
        def hook_e():
            side_sum()

        backward_block(
            NB - 1 - at, first_len, proj, d_normed, taps[...], shift[...], step_bias, rate_log, skip_wide,
            y, states, small, heads, carry, late,
        )
        return unused

    lax.fori_loop(0, NB, backward, 0)

    def d_in_part(block, lanes):
        begin = pl.multiple_of(HALO + block * TOK, 16)
        return mm(proj[pl.ds(begin, TOK), :HALF], w_all[0, lanes, :], ((1,), (1,))) + mm(
            proj[pl.ds(begin, TOK), HALF:], w_all[1, lanes, : CH + 128], ((1,), (1,))
        )

    mix.arrived(5, 6, 7)
    for at in range(0, MODEL, WIDE):
        lanes = slice(at, at + WIDE)
        stage[1, :, lanes] = stage[0, :, lanes] + mix.total(lanes)
    store_mixed = pltpu.make_async_copy(stage.at[1], mixed_out, here.at[5])
    store_mixed.start()
    mix.sent()
    for peer in (left, right, across):
        pl.semaphore_signal(free, inc=1, device_id=(rep, peer), device_id_type=MESH)
    pl.semaphore_wait(free, 3)
    d_in = Scatter(d_in_part, scatter_out, scatter_in, grad_send, grad_recv)
    for slot in range(3):
        d_in.leaf(slot)
    store_mixed.wait()
    load_again = pltpu.make_async_copy(cotangent, stage.at[1], here.at[6])
    load_again.start()

    def small_copy(which):
        peer = (sibling, beside)[which](rep, me)
        return send(44 + which, packed.at[which], packed_in.at[which], peer)

    def small_first():
        small_copy(0).wait()
        packed[1] = packed[0] + packed_in[0]
        small_copy(1).start()

    def small_second():
        small_copy(1).wait()
        packed_y[along_y] = packed[1] + packed_in[1]
        for o in range(1, 4):
            send(46 + o, packed_y.at[along_y], packed_y.at[along_y], y_peer(o)).start()

    def small_third():
        for o in range(1, 4):
            src = packed_y.at[y_of(4 - o)]
            send(46 + o, src, src, y_peer(o)).wait()
        packed_all[me] = packed_y[0] + packed_y[1] + packed_y[2] + packed_y[3]
        for o in range(1, SHARDS):
            to = rep, lax.rem(me + o, SHARDS)
            send(50 + o, packed_all.at[me], packed_all.at[me], to).start()

    def small_last():
        for o in range(1, SHARDS):
            source = lax.rem(me + SHARDS - o, SHARDS)
            send(50 + o, packed_all.at[source], packed_all.at[source], (rep, source)).wait()
        pltpu.make_async_copy(packed_all, small_out, here.at[9]).start()

    def norm_copy(index, ref, to):
        return pltpu.make_async_remote_copy(
            src_ref=ref, dst_ref=ref, send_sem=norm_send.at[index], recv_sem=norm_recv.at[index],
            device_id=to, device_id_type=MESH,
        )

    packed[0] = jnp.zeros_like(packed[0])
    packed[0, :5, :XBC] = small[:5]
    packed[0, 5:6, :CH] = small[5:6, :CH]
    packed[0, 5:6, CH : 2 * CH] = gain_sum[...]
    packed[0, 5:6, 2 * CH : 2 * CH + 128] = heads[0:1]
    packed[0, 5:6, 2 * CH + 128 : 2 * CH + 256] = heads[1:2]
    small_copy(0).start()

    def tail_tiles(which):
        def tile(at, unused):
            lanes = pl.ds(pl.multiple_of(at * 256, 256), 256)
            part = mm(x_all[:, lanes], proj[HALO:, part_columns(1 + which)], ((0,), (0,)))
            low_all[lanes, part_columns(1 + which)] = part.astype(BF)
            return unused

        lax.fori_loop(0, MODEL // 256, tile, 0)

    mine = part_columns(1 + core)
    share_gates()
    tail_tiles(1 - core)
    received = low_all.at[pl.ds(0, MODEL), part_columns(0)]
    core_copy = send(28, low_all.at[pl.ds(0, MODEL), part_columns(2 - core)], received, sibling(rep, me))
    pl.semaphore_wait(core_free, 1)
    core_copy.start()
    tail_tiles(core)
    core_copy.wait()

    def add_core(at, unused):
        rows = block_rows(at)
        both = low_all[rows, mine].astype(F32) + low_all[rows, :CH].astype(F32)
        low_all[rows, mine] = both.astype(BF)
        return unused

    lax.fori_loop(0, MODEL // TOK, add_core, 0)
    for o in range(1, 4):
        for block in range(SHARDS):
            src = low_all.at[y_rows(block, y_of(o)), mine]
            send(28 + o, src, near_y.at[o - 1, pl.ds(block * PIECE, PIECE)], y_peer(o)).start()
    small_first()
    d_in.middle()
    to_sibling()
    for o in range(1, 4):
        send(28 + o, low_all.at[pl.ds(0, QUARTER), mine], near_y.at[o - 1], y_peer(o)).wait()
    for block in range(SHARDS):
        rows = slice(block * PIECE, (block + 1) * PIECE)
        total = low_all[y_rows(block, along_y), mine].astype(F32)
        for o in range(3):
            total = total + near_y[o, rows].astype(F32)
        quarter[rows] = total.astype(BF)
    side_copy = send(32, quarter, tail_swap, beside(rep, me))
    side_copy.start()
    small_second()
    d_in.last()
    side_copy.wait()
    quarter[...] = (quarter[...].astype(F32) + tail_swap[...].astype(F32)).astype(BF)
    for o in range(1, SHARDS):
        to = lax.rem(me + o, SHARDS)
        send(32 + o, quarter.at[own_quarter(to)], tail_pieces.at[me], (rep, to)).start()
    tail_pieces[me] = quarter[own_quarter(me), :]
    small_third()
    early_done()
    for o in range(1, SHARDS):
        source = lax.rem(me + SHARDS - o, SHARDS)
        send(32 + o, quarter.at[own_quarter(source)], tail_pieces.at[source], (rep, source)).wait()

    @pl.when(core == 0)
    def assemble_first():
        total = tail_pieces[0, :, :BC].astype(F32)
        for block in range(1, SHARDS):
            total = total + tail_pieces[block, :, :BC].astype(F32)
        tail[0, own_piece, :BC] = total.astype(BF)
        for block in range(SHARDS):
            tail[0, own_piece, BC + 128 * block : BC + 128 * block + 128] = tail_pieces[block, :, BC:]
        tail[0, own_piece, BC + 1024 :] = jnp.zeros((PIECE, TAIL - BC - 1024), BF)

    @pl.when(core == 1)
    def assemble_second():
        total = jnp.zeros((PIECE, 128), F32)
        for block in range(SHARDS):
            tail[1, own_piece, 256 * block : 256 * block + 256] = tail_pieces[block, :, :256]
            put = (iota2((128, 128), 1) == iota2((128, 128), 0) + block * OWN) & (
                iota2((128, 128), 0) < OWN
            )
            total = total + mm(tail_pieces[block, :, 256:], put.astype(BF))
        tail[1, own_piece, 2048:] = total.astype(BF)

    for o in range(1, 4):
        src = tail.at[core, own_piece]
        send(40 + o, src, src, y_peer(o)).start()

    small_last()
    d_in.arrived(5, 6, 7)
    for at in range(MODEL // CH):
        y[at * TOK : (at + 1) * TOK, :] = d_in.total(slice(at * CH, (at + 1) * CH))
    load_again.wait()
    norm_sum[...] = jnp.zeros_like(norm_sum)

    def norm_back(at, unused):
        chunk = pl.ds(pl.multiple_of(at * CHUNK, CHUNK), CHUNK)
        rows = stage[0, chunk, :]
        pieces = [
            y[pl.ds(pl.multiple_of(k * TOK + at * CHUNK, CHUNK), CHUNK), :] for k in range(MODEL // CH)
        ]
        d_rows = jnp.concatenate(pieces, axis=1)
        scale = lax.rsqrt(jnp.mean(rows * rows, axis=1, keepdims=True) + epsilon)
        unit = rows * scale
        d_unit = d_rows * norm_gain[...]
        norm_sum[...] += jnp.sum((d_rows * unit).reshape(CHUNK // 8, 8, MODEL), axis=0)
        stage[1, chunk, :] += scale * (d_unit - unit * jnp.mean(d_unit * unit, axis=1, keepdims=True))
        return unused

    lax.fori_loop(0, TOK // CHUNK, norm_back, 0)
    store_grad = pltpu.make_async_copy(stage.at[1], grad_out, here.at[7])
    store_grad.start()

    for at in range(MODEL // 128):
        norm_parts[rep, at : at + 1, :] = jnp.sum(
            norm_sum[:, 128 * at : 128 * at + 128], axis=0, keepdims=True
        )
    norm_parts[rep, MODEL // 128 :, :] = jnp.zeros((16 - MODEL // 128, 128), F32)
    for o in range(1, 16):
        to = lax.rem(rep + o, 16), me
        norm_copy(o, norm_parts.at[rep], to).start()
    for o in range(1, 16):
        source = lax.rem(rep + 16 - o, 16)
        norm_copy(o, norm_parts.at[source], (source, me)).wait()
    total = norm_parts[0]
    for at in range(1, 16):
        total = total + norm_parts[at]
    norm_all[me] = total
    for o in range(1, SHARDS):
        norm_copy(15 + o, norm_all.at[me], (rep, lax.rem(me + o, SHARDS))).start()

    for o in range(1, 4):
        src = tail.at[core, pl.ds(pl.multiple_of(y_of(4 - o) * PIECE, 16), PIECE)]
        send(40 + o, src, src, y_peer(o)).wait()
    last_copy = send(58, tail.at[core], tail.at[core], sibling(rep, me))
    last_copy.start()
    send(58, tail.at[1 - core], tail.at[1 - core], sibling(rep, me)).wait_recv()
    last_copy.wait_send()
    store_tail = pltpu.make_async_copy(tail, tail_out, here.at[8])
    store_tail.start()
    for o in range(1, SHARDS):
        source = lax.rem(me + SHARDS - o, SHARDS)
        norm_copy(15 + o, norm_all.at[source], (rep, source)).wait()
    store_norm = pltpu.make_async_copy(norm_all, norm_out, here.at[4])
    store_norm.start()
    d_in.sent()
    gather_x.sent()
    pltpu.make_async_copy(gates, gates_out, here.at[3]).wait()
    pltpu.make_async_copy(outs, outs_out, here.at[10]).wait()
    store_grad.wait()
    store_tail.wait()
    pltpu.make_async_copy(packed_all, small_out, here.at[9]).wait()
    store_norm.wait()


def prepare_block(b, proj, y, d_normed, totals, gain, normed_out, gain_sum):
    r0 = pl.multiple_of(b * L, L)
    here = pl.ds(pl.multiple_of(HALO + b * L, 16), L)
    gate = proj[here, :CH].astype(F32)
    mixer = y[pl.ds(r0, L), :]
    sig = sigmoid(gate)
    silu = gate * sig
    gated = mixer * silu
    inv = lax.rsqrt(totals[0, pl.ds(b, 1), :] * (1.0 / INNER) + epsilon)
    back = inv * inv * inv * totals[1, pl.ds(b, 1), :] * (1.0 / INNER)
    inv = jnp.concatenate([to_column(inv)] * (CH // 128), axis=1)
    back = jnp.concatenate([to_column(back)] * (CH // 128), axis=1)
    dn = d_normed[pl.ds(r0, L), :].astype(F32)
    scaled = gated * inv
    normed_out[pl.ds(r0, L), :] = (scaled * gain).astype(BF)
    gain_sum[...] += jnp.sum(dn * scaled, axis=0, keepdims=True)
    d_gated = inv * gain * dn - gated * back
    d_normed[pl.ds(r0, L), :] = (d_gated * silu).astype(BF)
    proj[here, :CH] = (d_gated * mixer * (sig + silu * (1.0 - sig))).astype(BF)


def backward_block(
    b, first_len, proj, d_out, taps, shift, step_bias, rate_log, skip, y_in, states, small, heads,
    carry, late,
):
    upper = (iota2((L, L), 1) >= iota2((L, L), 0)).astype(BF)
    columns = head_columns()
    r0 = pl.multiple_of(b * L, L)
    rows = proj[pl.ds(r0, HALO + L), :]
    gate, xbc, conv, raw, step, log_decay, cum = block_front(
        rows, r0, first_len, taps, shift, step_bias, rate_log
    )
    sig = sigmoid(conv)
    act = conv * sig
    x = act[:, BC:]
    b_low = act[:, :STATE].astype(BF)
    c_low = act[:, STATE:BC].astype(BF)
    cum_rows = jnp.transpose(cum)
    scores = mm(c_low, b_low, ((1,), (1,)))
    step_wide = spread(step)
    scaled = x * step_wide
    scaled_low = scaled.astype(BF)
    decays = decay_weights(cum, cum_rows)

    y = y_in[pl.ds(r0, L), :]
    dy_low = d_out[pl.ds(r0, L), :]
    dy = dy_low.astype(F32)

    state = states[b]
    end_state = states[b + 1]
    d_state = carry[...]
    state_low = state.astype(BF)
    d_state_low = d_state.astype(BF)
    enter = jnp.exp(spread(cum))
    tail = jnp.exp(spread(cum[L - 1 : L] - cum))
    lane = iota2((L, 128), 1)
    d_scores = jnp.zeros((L, L), F32)
    weights = []
    for h in range(OWN):
        part = slice(128 * (h // 2), 128 * (h // 2) + 128)
        mine = (lane < HEAD_DIM) if h % 2 == 0 else (lane >= HEAD_DIM)
        d_weight = mm(
            dy_low[:, part],
            jnp.where(mine, scaled[:, part], 0.0).astype(BF),
            ((1,), (1,)),
        )
        d_scores = d_scores + d_weight * decays[h]
        weights.append((decays[h] * scores).astype(BF))
    d_scores_low = d_scores.astype(BF)
    d_scaled = pair_mix(weights, dy_low, ((0,), (0,)))
    d_scaled = d_scaled + tail * mm(b_low, d_state_low, ((1,), (1,)))
    enter_dy = (enter * dy).astype(BF)
    d_c = mm(d_scores_low, b_low) + mm(enter_dy, state_low)
    d_b = mm(d_scores_low, c_low, ((0,), (0,))) + mm((tail * scaled).astype(BF), d_state_low)

    ssm = y - skip * x
    d_cum = mm_right(
        dy_low.astype(F32) * ssm - scaled_low.astype(F32) * d_scaled, columns, 3
    )
    through = jnp.zeros((1, 128), F32)
    for piece in split(end_state * d_state, 3):
        through = through + jnp.sum(
            mm(piece, columns, ((0,), (0,))), axis=0, keepdims=True
        )
    d_cum = d_cum + jnp.where(iota2((L, 1), 0) == L - 1, through, 0.0)
    d_log = mm_left(upper, d_cum, 3)
    rate = jnp.exp(rate_log)
    d_step = mm_right(d_scaled * x, columns, 3) - rate * d_log
    d_raw = d_step * sigmoid(raw)
    d_x = d_scaled * step_wide + skip * dy

    carry[...] = head_rows(cum_rows, L - 1) * d_state + mm(enter_dy, c_low, ((0,), (0,)))

    d_act = jnp.concatenate([d_b, d_c, d_x], axis=1)
    d_conv = d_act * (sig + act * (1.0 - sig))
    row = r0 + iota2((L + 8, 1), 0)
    longer = jnp.concatenate([d_conv, late[...]], axis=0)
    late[...] = d_conv[:8]
    d_xbc = jnp.zeros((L, XBC), F32)
    for k in range(CONV):
        ahead = CONV - 1 - k
        masked = longer
        if ahead:
            masked = longer * tap_mask(row, first_len, ahead)
        d_xbc = d_xbc + taps[k : k + 1] * masked[ahead : ahead + L]
        small[k : k + 1, :] += jnp.sum(
            masked[:L] * xbc[HALO - ahead : HALO - ahead + L], axis=0, keepdims=True
        )
    small[4:5, :] += jnp.sum(d_conv, axis=0, keepdims=True)
    small[5:6, :CH] += jnp.sum(dy * x, axis=0, keepdims=True)
    heads[0:1, :] += jnp.sum(d_raw, axis=0, keepdims=True)
    heads[1:2, :] += jnp.sum(d_log * log_decay, axis=0, keepdims=True)
    proj[pl.ds(pl.multiple_of(HALO + b * L, 16), L), CH:] = jnp.concatenate(
        [d_xbc, d_raw], axis=1
    ).astype(BF)


def finish_kernel(
    mixed_in, grad_in, gates, tail, outs, packed, norm, mixed, grad, norm_grad, in_grad, conv_grad, bias_grad,
    dt_grad, rate_grad, skip_grad, gain_grad, out_grad, moved,
):
    copies = (
        pltpu.make_async_copy(mixed_in, mixed, moved.at[0]),
        pltpu.make_async_copy(grad_in, grad, moved.at[1]),
    )
    for copy in copies:
        copy.start()
    out_grad[0] = outs[...].astype(F32)
    in_grad[0, :, :INNER] = gates[...].astype(F32)
    for s in range(SHARDS):
        begin = INNER + CH * s
        in_grad[0, :, begin : begin + 128] = tail[0, :, BC + 128 * s : BC + 128 * s + 128].astype(F32)
        in_grad[0, :, begin + 128 : begin + CH] = tail[1, :, 256 * s : 256 * s + 256].astype(F32)
    in_grad[0, :, 2 * INNER : 2 * INNER + BC] = tail[0, :, :BC].astype(F32)
    in_grad[0, :, 2 * INNER + BC :] = tail[1, :, 2048 : 2048 + HEADS].astype(F32)
    parts = [packed[s] for s in range(SHARDS)]
    both = parts[0][:, :BC]
    for s in range(1, SHARDS):
        both = both + parts[s][:, :BC]
    conv_grad[0, :, INNER:] = both[:CONV]
    bias_grad[:, INNER:] = both[CONV : CONV + 1]
    heads = [jnp.zeros((8, 128), F32)] * 3
    for s in range(SHARDS):
        own = slice(CH * s, CH * s + CH)
        conv_grad[0, :, own] = parts[s][:CONV, BC:XBC]
        bias_grad[:, own] = parts[s][CONV : CONV + 1, BC:XBC]
        gain_grad[:, own] = parts[s][5:6, CH : 2 * CH]
        put = (iota2((128, 128), 1) == iota2((128, 128), 0) + s * OWN) & (iota2((128, 128), 0) < OWN)
        put_wide = iota2((CH, 128), 1) == iota2((CH, 128), 0) // HEAD_DIM + s * OWN
        rows = (
            (parts[s][5:6, 2 * CH : 2 * CH + 128], put),
            (parts[s][5:6, 2 * CH + 128 : 2 * CH + 256], put),
            (parts[s][5:6, :CH], put_wide),
        )
        for at, (row, to) in enumerate(rows):
            wide = jnp.broadcast_to(row, (8, row.shape[1]))
            heads[at] = heads[at] + mm_right(wide, to.astype(BF), 3)
    for at, ref in enumerate((dt_grad, rate_grad, skip_grad)):
        ref[...] = heads[at][0:1, :HEADS]
    total = norm[0]
    for s in range(1, SHARDS):
        total = total + norm[s]
    for at in range(MODEL // 128):
        norm_grad[:, 128 * at : 128 * at + 128] = total[at : at + 1]
    for copy in copies:
        copy.wait()


VM = pl.BlockSpec(memory_space=pltpu.VMEM)
SM = pl.BlockSpec(memory_space=pltpu.SMEM)
ANY = pl.BlockSpec(memory_space=pl.ANY)
LIMIT = 61 << 20


def local(
    resid,
    cotangent,
    first_length,
    norm_gain,
    in_weight,
    conv_weight,
    conv_bias,
    dt_bias,
    a_log,
    skip,
    gate_gain,
    out_weight,
):
    w = in_weight[0]
    narrow = jnp.pad(w[:, 2 * INNER :], ((0, 0), (0, 4 * 128 - BC - HEADS)))
    dma = pltpu.SemaphoreType.DMA
    outs = (
        ((TOK, MODEL), F32), ((TOK, MODEL), F32), ((ROWS, INNER), BF), ((2, ROWS, TAIL), BF),
        ((CH, MODEL), BF), ((SHARDS, 8, MODEL), F32), ((SHARDS, 16, 128), F32),
    )
    scratch = (
        ((GROUP, MODEL), BF), ((GROUP, MODEL), BF), ((2, MODEL, HALF), BF),
        ((HALO + GROUP, COLS), BF), ((GROUP, CH), F32), ((NB + 1, CH, STATE), F32), ((GROUP, CH), BF),
        ((SHARDS, 2, NB, L), F32), ((CH, STATE), F32), ((2, TOK, MODEL), F32), ((CONV, XBC), F32),
        ((1, XBC), F32),
        ((2, NB, L), F32), ((GROUP, CH), BF), ((1, CH), F32), ((8, MODEL), F32), ((8, XBC), F32),
        ((8, 128), F32),
        ((8, XBC), F32), ((7, TOK, MODEL), BF), ((7, TOK, MODEL), BF),
        ((3, QUARTER, CH), BF), ((CH, HALF_OUT), BF), ((HALF_OUT, CH), BF), ((3, 96, HALF_OUT), BF),
        ((3, QUARTER // 2, CH), BF), ((96, HALF_OUT), BF), ((QUARTER // 2, CH), BF),
        ((96, HALF_OUT), BF), ((QUARTER // 2, CH), BF),
        ((QUARTER, CH), BF),
        ((ROWS, INNER), BF), ((CH, MODEL), BF),
        ((QUARTER, CH), BF),
        ((SHARDS, PIECE, CH), BF), ((2, ROWS, TAIL), BF),
        ((2, 8, MODEL), F32), ((2, 8, MODEL), F32), ((4, 8, MODEL), F32), ((SHARDS, 8, MODEL), F32),
        ((16, 16, 128), F32), ((SHARDS, 16, 128), F32),
    )
    mixed, grad, gates, tail, out_grad, packed, norm = pl.pallas_call(
        layer_kernel,
        out_shape=tuple(jax.ShapeDtypeStruct(*shape) for shape in outs),
        in_specs=[SM, ANY, ANY, ANY, ANY] + [VM] * 8,
        out_specs=(ANY,) * 7,
        scratch_shapes=[pltpu.VMEM(*shape) for shape in scratch]
        + [dma((9,))] * 4 + [dma((SHARDS,))] * 2 + [dma((4,))] * 2 + [dma((1,))] * 2
        + [dma((SHARDS,))] * 2 + [dma((11,))] + [dma((8,))] * 4 + [dma((60,))] * 2 + [dma((23,))] * 2 + [dma((SHARDS,))] * 2
        + [pltpu.SemaphoreType.REGULAR] * 2,
        compiler_params=pltpu.CompilerParams(
            vmem_limit_bytes=LIMIT, collective_id=0, has_side_effects=True
        ),
    )(
        first_length, resid, cotangent, w, narrow, out_weight[0], norm_gain, conv_weight[0], conv_bias,
        dt_bias, a_log, skip, gate_gain,
    )
    wide = CONVCH
    shapes = (
        (TOK, MODEL), (TOK, MODEL), (1, MODEL), (1, ROWS, 2 * INNER + BC + HEADS), (1, CONV, wide), (1, wide),
        (1, HEADS), (1, HEADS), (1, HEADS), (1, INNER), (1, CH, MODEL),
    )
    return pl.pallas_call(
        finish_kernel,
        out_shape=tuple(jax.ShapeDtypeStruct(shape, F32) for shape in shapes),
        in_specs=[VM] * 7,
        out_specs=(ANY, ANY) + (VM,) * 9,
        scratch_shapes=[dma((2,))],
        compiler_params=pltpu.CompilerParams(vmem_limit_bytes=LIMIT),
    )(mixed, grad, gates, tail, out_grad, packed, norm)


def solution(mesh):
    rows = P(("rep", "shard"), None)
    weight = P(None, "shard", None)
    return jax.shard_map(
        local,
        mesh=mesh,
        in_specs=(rows, rows, P("rep"), P(), weight, P(), P(), P(), P(), P(), P(), weight),
        out_specs=(rows, rows, P(), weight, P(), P(), P(), P(), P(), P(), weight),
        check_vma=False,
    )
```

```python
import jax
import jax.numpy as jnp
from jax import lax
from jax.experimental import pallas as pl
from jax.experimental.pallas import tpu as pltpu
from jax.sharding import PartitionSpec as P

HEADS = 48
HEAD_DIM = 64
STATE = 128
CONV = 4
INNER = 3072
CONVCH = 3328
MODEL = 1536
SHARDS = 8
OWN = HEADS // SHARDS
CH = OWN * HEAD_DIM
XBC = CH + 2 * STATE
HALF = 640
COLS = 2 * CH + 2 * STATE + 128
BC = 2 * STATE
TOK = 256
GROUP = TOK * SHARDS
L = 128
NB = GROUP // L
HALO = 16
PIECE = 48
MESH = pl.DeviceIdType.MESH
ROWS = MODEL // SHARDS
QUARTER = SHARDS * PIECE
TAIL = 8 * 256 + 128
FRONT = 64
CHUNK = 32
HALF_OUT = MODEL // 2
WIDE = 512
OUT_PART = pl.ds(MODEL, CH)
RESET = -200.0

epsilon = 1e-05
F32 = jnp.float32
BF = jnp.bfloat16


def mm(a, b, dims=((1,), (0,))):
    return lax.dot_general(a, b, (dims, ((), ())), preferred_element_type=F32)


def split(v, parts):
    out = []
    for _ in range(parts):
        piece = v.astype(BF)
        out.append(piece)
        v = v - piece.astype(F32)
    return out


def mm_left(ones, v, parts):
    return sum(mm(ones, piece) for piece in split(v, parts))


def mm_right(v, ones, parts):
    return sum(mm(piece, ones) for piece in split(v, parts))


def iota2(shape, dim):
    return lax.broadcasted_iota(jnp.int32, shape, dim)


def head_columns():
    return (iota2((CH, 128), 0) // HEAD_DIM == iota2((CH, 128), 1)).astype(BF)


def spread(per_head):
    lane = iota2((per_head.shape[0], 128), 1)
    tiles = []
    for pair in range(OWN // 2):
        left = per_head[:, 2 * pair : 2 * pair + 1]
        right = per_head[:, 2 * pair + 1 : 2 * pair + 2]
        tiles.append(jnp.where(lane < HEAD_DIM, left, right))
    return jnp.concatenate(tiles, axis=1)


def head_rows(cum_rows, at):
    pieces = [
        jnp.broadcast_to(cum_rows[h : h + 1, at : at + 1], (HEAD_DIM, 1)) for h in range(OWN)
    ]
    return jnp.exp(jnp.concatenate(pieces, axis=0))


def tap_mask(row, first_len, back):
    past = row - first_len
    return jnp.where((past >= 0) & (past < back), 0.0, 1.0)


def block_front(rows, r0, first_len, taps, shift, step_bias, rate_log):
    xbc = rows[:, CH : CH + XBC].astype(F32)
    row = r0 + iota2((L, 1), 0)
    conv = jnp.broadcast_to(shift, (L, XBC))
    for k in range(CONV):
        back = CONV - 1 - k
        term = taps[k : k + 1] * xbc[HALO - back : HALO - back + L]
        if back:
            term = term * tap_mask(row, first_len, back)
        conv = conv + term
    gate = rows[HALO:, :CH].astype(F32)
    raw = rows[HALO:, CH + XBC :].astype(F32) + step_bias
    step = jnp.maximum(raw, 0.0) + jnp.log1p(jnp.exp(-jnp.abs(raw)))
    log_decay = -step * jnp.exp(rate_log)
    with_reset = log_decay + jnp.where(row == first_len, RESET, 0.0)
    lower = (iota2((L, L), 0) >= iota2((L, L), 1)).astype(BF)
    cum = mm_left(lower, with_reset, 3)
    return gate, xbc, conv, raw, step, log_decay, cum


def sigmoid(v):
    return 1.0 / (1.0 + jnp.exp(-v))


def pair_mix(weights, value, dims=((1,), (0,))):
    lane = iota2((L, 128), 1)
    tiles = []
    for pair in range(OWN // 2):
        part = value[:, 128 * pair : 128 * pair + 128]
        tiles.append(
            jnp.where(
                lane < HEAD_DIM,
                mm(weights[2 * pair], part, dims),
                mm(weights[2 * pair + 1], part, dims),
            )
        )
    return jnp.concatenate(tiles, axis=1)


def decay_weights(cum, cum_rows):
    causal = iota2((L, L), 0) >= iota2((L, L), 1)
    out = []
    for h in range(OWN):
        gap = cum[:, h : h + 1] - cum_rows[h : h + 1, :]
        out.append(jnp.exp(jnp.where(causal, gap, -1e30)))
    return out


def to_row(column):
    return jnp.transpose(jnp.broadcast_to(column, (L, L)))[0:1]


def to_column(row):
    return jnp.transpose(jnp.broadcast_to(row, (L, L)))


def forward_block(b, first_len, proj, taps, shift, step_bias, rate_log, skip, y_out, states, sums, carry):
    r0 = pl.multiple_of(b * L, L)
    rows = proj[pl.ds(r0, HALO + L), :]
    gate, xbc, conv, raw, step, log_decay, cum = block_front(
        rows, r0, first_len, taps, shift, step_bias, rate_log
    )
    act = conv * sigmoid(conv)
    x = act[:, BC:]
    b_low = act[:, :STATE].astype(BF)
    c_low = act[:, STATE:BC].astype(BF)
    cum_rows = jnp.transpose(cum)
    scores = mm(c_low, b_low, ((1,), (1,)))
    scaled = x * spread(step)
    scaled_low = scaled.astype(BF)
    weights = [(w * scores).astype(BF) for w in decay_weights(cum, cum_rows)]
    state = carry[...]
    states[b] = state
    y = pair_mix(weights, scaled_low)
    y = y + jnp.exp(spread(cum)) * mm(c_low, state.astype(BF), ((1,), (1,)))
    tail = jnp.exp(spread(cum[L - 1 : L] - cum))
    carry[...] = head_rows(cum_rows, L - 1) * state + mm(
        (tail * scaled).astype(BF), b_low, ((0,), (0,))
    )
    y = y + skip * x
    y_out[pl.ds(r0, L), :] = y
    gated = y * (gate * sigmoid(gate))
    sums[pl.ds(b, 1), :] = to_row(jnp.sum(gated * gated, axis=1, keepdims=True))


def place_of():
    rep, me = lax.axis_index("rep"), lax.axis_index("shard")
    hi, z = me // 4, lax.rem(me, 4)
    left = hi * 4 + lax.rem(z + 3, 4)
    right = hi * 4 + lax.rem(z + 1, 4)
    far = hi * 4 + lax.rem(z + 2, 4)
    across = lax.rem(me + 4, 8)
    return rep, me, left, right, far, across


def sibling(rep, me):
    return rep + 1 - 2 * lax.rem(rep, 2), me


def beside(rep, me):
    return rep + 2 - 4 * lax.rem(rep // 2, 2), me


def other_side(block):
    return lax.rem(block + 4, 8)


def enter(rep, me):
    barrier = pltpu.get_barrier_semaphore()
    peers = [(rep, lax.rem(me + o, SHARDS)) for o in range(1, SHARDS)]
    peers += [(lax.rem(rep + 4 * o, 16), me) for o in range(1, 4)]
    peers += [sibling(rep, me), beside(rep, me)]
    for peer in peers:
        pl.semaphore_signal(barrier, inc=1, device_id=peer, device_id_type=MESH)
    return lambda: pl.semaphore_wait(barrier, len(peers))


def block_rows(block, part=(0, TOK)):
    begin, end = part
    return pl.ds(pl.multiple_of(block * TOK + begin, 16), end - begin)


FIRST, SECOND = (0, TOK // 2), (TOK // 2, TOK)
EDGE = 48
TOP, REST = (0, EDGE), (EDGE, TOK)


class Gather:
    def __init__(self, blocks, send, recv):
        self.blocks, self.send, self.recv = blocks, send, recv
        self.rep, self.me, self.left, self.right, self.far, self.across = place_of()

    def move(self, channel, block, to, rows=(0, TOK)):
        ref = self.blocks.at[block_rows(block, rows)]
        return pltpu.make_async_remote_copy(
            src_ref=ref,
            dst_ref=ref,
            send_sem=self.send.at[channel],
            recv_sem=self.recv.at[channel],
            device_id=(self.rep, to),
            device_id_type=MESH,
        )

    def outgoing(self, channel):
        me, left, right, across = self.me, self.left, self.right, self.across
        return (
            lambda: self.move(0, me, right),
            lambda: self.move(1, me, left),
            lambda: self.move(2, me, across),
            lambda: self.move(3, left, right, FIRST),
            lambda: self.move(4, right, left, SECOND),
            lambda: self.move(5, across, right, REST),
            lambda: self.move(6, across, left, REST),
            lambda: self.move(7, self.far, across, FIRST),
            lambda: self.move(8, self.far, across, SECOND),
            lambda: self.move(9, left, across, TOP),
            lambda: self.move(10, right, across, TOP),
        )[channel]()

    def incoming(self, channel):
        left, right, far, across = self.left, self.right, self.far, self.across
        return (
            lambda: self.move(0, left, left),
            lambda: self.move(1, right, right),
            lambda: self.move(2, across, across),
            lambda: self.move(3, far, left, FIRST),
            lambda: self.move(4, far, right, SECOND),
            lambda: self.move(5, other_side(left), left, REST),
            lambda: self.move(6, other_side(right), right, REST),
            lambda: self.move(7, other_side(far), across, FIRST),
            lambda: self.move(8, other_side(far), across, SECOND),
            lambda: self.move(9, other_side(left), across, TOP),
            lambda: self.move(10, other_side(right), across, TOP),
        )[channel]()

    def start(self, *channels):
        for channel in channels:
            self.outgoing(channel).start()

    def arrived(self, *channels):
        for channel in channels:
            self.incoming(channel).wait_recv()

    def sent(self):
        for channel in range(11):
            self.outgoing(channel).wait_send()


class Scatter:
    SLOTS = (
        (0, (0, TOK)), (1, REST), (2, REST), (3, FIRST), (3, SECOND), (4, (0, TOK)), (5, (0, TOK)),
        (6, (0, TOK)), (1, TOP), (2, TOP),
    )

    def __init__(self, part, out, into, send, recv):
        self.part, self.out, self.into, self.send, self.recv = part, out, into, send, recv
        self.rep, self.me, self.left, self.right, self.far, self.across = place_of()
        self.to = (
            self.across, self.left, self.right, self.left, self.right, self.right, self.left, self.across,
            self.across, self.across,
        )

    def copy(self, channel):
        slot, rows = self.SLOTS[channel]
        at = (slot, pl.ds(rows[0], rows[1] - rows[0]))
        return pltpu.make_async_remote_copy(
            src_ref=self.out.at[at],
            dst_ref=self.into.at[at],
            send_sem=self.send.at[channel],
            recv_sem=self.recv.at[channel],
            device_id=(self.rep, self.to[channel]),
            device_id_type=MESH,
        )

    def arrived(self, *channels):
        for channel in channels:
            self.copy(channel).wait_recv()

    def fill(self, slot, block, *arrived):
        for at in range(0, MODEL, WIDE):
            lanes = slice(at, at + WIDE)
            value = self.part(block, lanes)
            for other in arrived:
                value = value + self.into[other, :, lanes].astype(F32)
            self.out[slot, :, lanes] = value.astype(BF)

    def add(self, slot, into, rows):
        rows = slice(*rows)
        value = self.out[slot, rows].astype(F32)
        for other in into:
            value = value + self.into[other, rows].astype(F32)
        self.out[slot, rows] = value.astype(BF)

    def leaf(self, slot):
        self.fill(slot, other_side((self.far, self.left, self.right)[slot]))
        self.copy(slot).start()
        if slot:
            self.copy(7 + slot).start()

    def middle(self):
        self.arrived(0)
        self.fill(3, self.far, 0)
        self.copy(3).start()
        self.copy(4).start()
        self.fill(6, self.across)
        self.arrived(1, 2)
        self.add(6, (1, 2), REST)

    def cross(self):
        self.copy(7).start()

    def near(self):
        self.fill(4, self.right)
        self.fill(5, self.left)

    def last(self):
        self.arrived(8, 9)
        self.add(4, (2,), TOP)
        self.add(5, (1,), TOP)
        self.arrived(3, 4)
        self.add(4, (3,), SECOND)
        self.copy(5).start()
        self.add(5, (3,), FIRST)
        self.copy(6).start()

    def total(self, lanes):
        value = self.part(self.me, lanes)
        for slot in (4, 5, 6):
            value = value + self.into[slot, :, lanes].astype(F32)
        return value

    def sent(self):
        for channel in range(10):
            self.copy(channel).wait_send()


def own_heads(vector, me):
    pick = (iota2((HEADS, 128), 0) == iota2((HEADS, 128), 1) + me * OWN) & (
        iota2((HEADS, 128), 1) < OWN
    )
    wide = jnp.broadcast_to(vector, (8, HEADS))
    return mm_right(wide, pick.astype(BF), 3)[0:1]


def own_channels(vector, me):
    pick = iota2((HEADS, CH), 0) == iota2((HEADS, CH), 1) // HEAD_DIM + me * OWN
    wide = jnp.broadcast_to(vector, (8, HEADS))
    return mm_right(wide, pick.astype(BF), 3)[0:1]


def own_slices(me, conv_weight, conv_bias):
    own = pl.ds(pl.multiple_of(me * CH, 128), CH)
    taps = jnp.concatenate([conv_weight[:, INNER:], conv_weight[:, own]], axis=1)
    shift = jnp.concatenate([conv_bias[:, INNER:], conv_bias[:, own]], axis=1)
    return taps, shift


def layer_kernel(
    first_ref, resid, cotangent, w_in, narrow, w_out, norm_gain, conv_weight, conv_bias, dt_bias,
    a_log, skip, gate_gain,
    mixed_out, grad_out, gates_out, tail_out, outs_out, small_out,
    x_all, low_all, w_all, proj, y, states, d_normed, sums, carry, stage, taps, shift,
    totals, normed_out, gain_sum, norm_sum, small, heads, late, scatter_out, scatter_in,
    near_y, core_out, core_gate, near_out, near_gate, part_out, part_gate, side_out, side_gate,
    quarter, gates, outs,
    tail_swap, tail_pieces, tail,
    packed, packed_in, packed_y, packed_all,
    x_send, x_recv, low_send, low_recv, piece_send, piece_recv, y_send, y_recv, core_send, core_recv,
    sum_send, sum_recv, here, mix_send, mix_recv, grad_send, grad_recv, g_send, g_recv, owner_send, owner_recv, free, core_free,
):
    rep, me, left, right, far, across = place_of()
    core = lax.rem(rep, 2)
    along_y = rep // 4
    first_len = first_ref[0]
    load_resid = pltpu.make_async_copy(resid, stage.at[0], here.at[0])
    load_cot = pltpu.make_async_copy(cotangent, stage.at[1], here.at[1])
    load_resid.start()
    load_cot.start()
    all_entered = enter(rep, me)

    load_resid.wait()

    def norm_rows(at, unused):
        rows = stage[0, pl.ds(pl.multiple_of(at * FRONT, FRONT), FRONT), :]
        scale = lax.rsqrt(jnp.mean(rows * rows, axis=1, keepdims=True) + epsilon)
        own = pl.ds(pl.multiple_of(me * TOK + at * FRONT, FRONT), FRONT)
        x_all[own, :] = (rows * scale * norm_gain[...]).astype(BF)
        return unused

    lax.fori_loop(0, TOK // FRONT, norm_rows, 0)
    all_entered()
    gather_x = Gather(x_all, x_send, x_recv)
    gather_x.start(0, 1, 2)

    own_rows = pl.ds(pl.multiple_of(along_y * PIECE, 16), PIECE)

    def landing(block):
        return pl.ds(pl.multiple_of(block * 192 + along_y * PIECE, 16), PIECE)

    def weight_pieces(to, make):
        wide = pl.ds(pl.multiple_of(core * INNER + to * CH, 128), CH)
        half = pl.ds(pl.multiple_of(core * BC, 128), BC)
        make(w_in.at[own_rows, wide], w_all.at[core, landing(me), pl.ds(0, CH)])
        make(narrow.at[own_rows, half], w_all.at[core, landing(me), pl.ds(CH, BC)])

    for o in range(1, SHARDS):
        to = lax.rem(me + o, SHARDS)
        weight_pieces(
            to,
            lambda src, dst: pltpu.make_async_remote_copy(
                src_ref=src, dst_ref=dst, send_sem=piece_send.at[o], recv_sem=piece_recv.at[o],
                device_id=(rep, to), device_id_type=MESH,
            ).start(),
        )
    weight_pieces(me, lambda src, dst: pltpu.make_async_copy(src, dst, here.at[2]).start())

    load_cot.wait()
    low_all[block_rows(me), :] = stage[1].astype(BF)
    gather_low = Gather(low_all, low_send, low_recv)

    taps_now, shift_now = own_slices(me, conv_weight, conv_bias)
    taps[...] = taps_now
    shift[...] = shift_now
    proj[pl.ds(0, HALO), :] = jnp.zeros((HALO, COLS), BF)
    carry[...] = jnp.zeros_like(carry)

    pltpu.make_async_copy(
        w_all.at[core, landing(me)], w_all.at[core, landing(me)], here.at[2]
    ).wait()
    for o in range(1, SHARDS):
        source = lax.rem(me + SHARDS - o, SHARDS)
        piece = w_all.at[core, landing(source)]
        pltpu.make_async_remote_copy(
            src_ref=piece, dst_ref=piece, send_sem=piece_send.at[o], recv_sem=piece_recv.at[o],
            device_id=(rep, source), device_id_type=MESH,
        ).wait()
    for o in range(1, 4):
        for block in range(SHARDS):
            piece = w_all.at[core, landing(block)]
            pltpu.make_async_remote_copy(
                src_ref=piece, dst_ref=piece, send_sem=y_send.at[o], recv_sem=y_recv.at[o],
                device_id=(lax.rem(rep + 4 * o, 16), me), device_id_type=MESH,
            ).start()
    gather_x.arrived(0)
    gather_x.start(3, 9)
    gather_x.arrived(1)
    gather_x.start(4, 10)
    gather_x.arrived(2)
    gather_x.start(5, 6)
    gather_x.arrived(3)
    gather_x.start(7)
    gather_x.arrived(4)
    gather_x.start(8)
    gather_low.start(0, 1, 2)
    for o in range(1, 4):
        landed = w_all.at[core, pl.ds(0, QUARTER)]
        pltpu.make_async_remote_copy(
            src_ref=landed, dst_ref=landed, send_sem=y_send.at[o], recv_sem=y_recv.at[o],
            device_id=(lax.rem(rep + 4 * o, 16), me), device_id_type=MESH,
        ).wait()

    def halves(which):
        return pltpu.make_async_remote_copy(
            src_ref=w_all.at[which], dst_ref=w_all.at[which], send_sem=core_send.at[0],
            recv_sem=core_recv.at[0], device_id=(rep + 1 - 2 * core, me), device_id_type=MESH,
        )

    halves(core).start()
    halves(1 - core).wait_recv()
    halves(core).wait_send()
    pick = (iota2((128, 128), 0) == iota2((128, 128), 1) + me * OWN) & (iota2((128, 128), 1) < OWN)
    w_all[1, :, CH : CH + 128] = mm(w_all[1, :, CH : CH + 128], pick.astype(BF)).astype(BF)

    side = (me // 4) * 4

    def project(at, unused):
        rows = x_all[block_rows(at), :]
        begin = pl.multiple_of(HALO + at * TOK, 16)
        proj[pl.ds(begin, TOK), :HALF] = mm(rows, w_all[0]).astype(BF)
        proj[pl.ds(begin, TOK), HALF:] = mm(rows, w_all[1, :, : CH + 128]).astype(BF)
        return unused

    lax.fori_loop(side, side + 4, project, 0)
    gather_low.arrived(0)
    gather_low.start(3, 9)
    gather_low.arrived(1)
    gather_low.start(4, 10)
    gather_x.arrived(5, 6, 7, 8, 9, 10)
    lax.fori_loop(4 - side, 8 - side, project, 0)

    step_bias = own_heads(dt_bias[...], me)
    rate_log = own_heads(a_log[...], me)
    skip_wide = own_channels(skip[...], me)

    def scan(b, unused):
        @pl.when(b == 6)
        def relay():
            gather_low.arrived(3, 4, 2)
            gather_low.start(7, 8, 5, 6)

        forward_block(
            b, first_len, proj, taps[...], shift[...], step_bias, rate_log, skip_wide, y, states,
            sums.at[me, 0], carry,
        )
        return unused

    lax.fori_loop(0, NB, scan, 0)
    states[NB] = carry[...]

    gain = gate_gain[:, pl.ds(pl.multiple_of(me * CH, 128), CH)]

    def normed(at, unused):
        begin = pl.multiple_of(at * TOK, TOK)
        dn = mm(low_all[block_rows(at), :], w_out[...], ((1,), (1,)))
        d_normed[pl.ds(begin, TOK), :] = dn.astype(BF)
        gate = proj[pl.ds(HALO + begin, TOK), :CH].astype(F32)
        gated = y[pl.ds(begin, TOK), :] * (gate * sigmoid(gate))
        both = jnp.sum(gated * gain * dn, axis=1, keepdims=True)
        sums[me, 1, pl.ds(2 * at, 1), :] = to_row(both[:L])
        sums[me, 1, pl.ds(2 * at + 1, 1), :] = to_row(both[L:])
        return unused

    def sum_copy(kind, o, slot, to):
        ref = sums.at[slot, kind]
        return pltpu.make_async_remote_copy(
            src_ref=ref, dst_ref=ref, send_sem=sum_send.at[SHARDS * kind + o],
            recv_sem=sum_recv.at[SHARDS * kind + o], device_id=(rep, to), device_id_type=MESH,
        )

    def start_sum(kind):
        for o in range(1, SHARDS):
            sum_copy(kind, o, me, lax.rem(me + o, SHARDS)).start()

    def end_sum(kind):
        for o in range(1, SHARDS):
            source = lax.rem(me + SHARDS - o, SHARDS)
            sum_copy(kind, o, source, source).wait_recv()
        total = sums[0, kind]
        for slot in range(1, SHARDS):
            total = total + sums[slot, kind]
        totals[kind] = total
        for o in range(1, SHARDS):
            sum_copy(kind, o, me, lax.rem(me + o, SHARDS)).wait_send()

    def scale_out(b, unused):
        scale_block(b, proj, y, totals, gain, normed_out)
        return unused

    def mixed_part(block, lanes):
        return mm(normed_out[block_rows(block), :], w_out[:, lanes])

    mix = Scatter(mixed_part, scatter_out, scatter_in, mix_send, mix_recv)
    start_sum(0)
    lax.fori_loop(side, side + 4, normed, 0)
    end_sum(0)
    lax.fori_loop(0, NB, scale_out, 0)
    gather_low.arrived(5, 6, 9, 10)

    def normed_near(at, unused):
        return normed(other_side(side + lax.rem(me + at, 4)), unused)

    lax.fori_loop(3, 6, normed_near, 0)
    gather_low.arrived(7, 8)
    lax.fori_loop(6, 7, normed_near, 0)
    start_sum(1)

    def send(index, src, dst, to):
        return pltpu.make_async_remote_copy(
            src_ref=src, dst_ref=dst, send_sem=g_send.at[index], recv_sem=g_recv.at[index],
            device_id=to, device_id_type=MESH,
        )

    def y_peer(o):
        return lax.rem(rep + 4 * o, 16), me

    def y_of(o):
        return lax.rem(along_y + o, 4)

    gain_sum[...] = jnp.zeros_like(gain_sum)
    small[...] = jnp.zeros_like(small)
    heads[...] = jnp.zeros_like(heads)
    late[...] = jnp.zeros_like(late)
    carry[...] = jnp.zeros_like(carry)

    def prepare(b, unused):
        prepare_block(b, proj, y, d_normed, totals, gain, gain_sum)
        return unused

    for slot in range(3):
        mix.leaf(slot)
    gather_low.sent()
    def row_dots(at, part, weight):
        dots = jnp.sum(part * weight.astype(F32), axis=1, keepdims=True)
        for half in range(2):
            lanes = pl.ds(pl.multiple_of(at * 256 + half * L, L), L)
            norm_sum[0:1, lanes] += to_row(dots[half * L : half * L + L])

    norm_sum[...] = jnp.zeros_like(norm_sum)

    def out_tile(at, unused):
        lanes = pl.ds(pl.multiple_of(at * 256, 256), 256)
        low = low_all[:, lanes]
        low_all[OUT_PART, lanes] = mm(normed_out[...], low, ((0,), (0,))).astype(BF)
        return unused

    def gate_tile(at, unused):
        lanes = pl.ds(pl.multiple_of(at * 256, 256), 256)
        rows = x_all[:, lanes]
        part = mm(rows, proj[HALO:, :CH], ((0,), (0,)))
        low_all[lanes, :CH] = part.astype(BF)
        row_dots(at, part, w_all[0, lanes, :CH])
        return unused

    def y_rows(block, y_at):
        return pl.ds(pl.multiple_of(block * ROWS + y_at * PIECE, 16), PIECE)

    def out_rows(y_at, base=0):
        return pl.ds(pl.multiple_of(base + y_at * 96, 16), 96)

    def part_columns(which):
        return pl.ds(pl.multiple_of(which * CH, 128), CH)

    def out_half(which):
        return pl.ds(pl.multiple_of(which * HALF_OUT, 128), HALF_OUT)

    def gate_half(which):
        return pl.ds(pl.multiple_of(which * HALF_OUT, 128), HALF_OUT)

    core_copies = (
        send(1, low_all.at[OUT_PART, out_half(1 - core)], core_out, sibling(rep, me)),
        send(2, low_all.at[gate_half(1 - core), pl.ds(0, CH)], core_gate, sibling(rep, me)),
    )
    lax.fori_loop(0, MODEL // 256, out_tile, 0)
    core_copies[0].start()
    end_sum(1)
    lax.fori_loop(0, NB, prepare, 0)
    lax.fori_loop(0, MODEL // 256, gate_tile, 0)
    core_copies[1].start()

    def gate_piece(block, y_at):
        return pl.ds(pl.multiple_of(core * HALF_OUT + block * ROWS + y_at * PIECE, 16), PIECE)

    def out_to_y(o):
        src = low_all.at[out_rows(y_of(o), MODEL), out_half(core)]
        return send(2 + o, src, near_out.at[o - 1], y_peer(o))

    def gate_to_y(o, block):
        dst = near_gate.at[o - 1, pl.ds(block * PIECE, PIECE)]
        return send(5 + o, low_all.at[gate_piece(block, y_of(o)), pl.ds(0, CH)], dst, y_peer(o))

    def core_sum():
        for copy in core_copies:
            copy.wait()
        mine = out_half(core)
        both = low_all[OUT_PART, mine].astype(F32) + core_out[...].astype(F32)
        low_all[OUT_PART, mine] = both.astype(BF)
        both = low_all[gate_half(core), :CH].astype(F32) + core_gate[...].astype(F32)
        low_all[gate_half(core), :CH] = both.astype(BF)
        for o in range(1, 4):
            out_to_y(o).start()
            for block in range(SHARDS // 2):
                gate_to_y(o, block).start()

    side_copies = (
        send(9, part_gate, side_gate, beside(rep, me)),
        send(10, part_out, side_out, beside(rep, me)),
    )

    def y_sum():
        for o in range(1, 4):
            out_to_y(o).wait()
            landed = low_all.at[pl.ds(0, HALF_OUT // 4), pl.ds(0, CH)]
            send(5 + o, landed, near_gate.at[o - 1], y_peer(o)).wait()
        total = low_all[out_rows(along_y, MODEL), out_half(core)].astype(F32)
        for o in range(3):
            total = total + near_out[o].astype(F32)
        part_out[...] = total.astype(BF)
        for block in range(SHARDS // 2):
            rows = slice(block * PIECE, (block + 1) * PIECE)
            total = low_all[gate_piece(block, along_y), :CH].astype(F32)
            for o in range(3):
                total = total + near_gate[o, rows].astype(F32)
            part_gate[rows] = total.astype(BF)
        for copy in side_copies:
            copy.start()
        pl.semaphore_signal(
            core_free, inc=1, device_id=sibling(rep, me), device_id_type=MESH
        )

    own_piece = pl.ds(pl.multiple_of(along_y * PIECE, 16), PIECE)

    def gate_columns(block):
        return pl.ds(pl.multiple_of(block * CH, 128), CH)

    def own_quarter(block):
        return pl.ds(pl.multiple_of(block * PIECE, 16), PIECE)

    owner_here = core == me // 4

    def from_shard(o):
        source = lax.rem(me + SHARDS - o, SHARDS)
        dst = gates.at[own_piece, gate_columns(source)]
        return pltpu.make_async_remote_copy(
            src_ref=dst, dst_ref=dst, send_sem=owner_send.at[me], recv_sem=owner_recv.at[source],
            device_id=(rep, source), device_id_type=MESH,
        )

    def owner_copy(block):
        to = core * (SHARDS // 2) + block
        return pltpu.make_async_remote_copy(
            src_ref=part_gate.at[pl.ds(block * PIECE, PIECE)], dst_ref=gates.at[own_piece, gate_columns(me)],
            send_sem=owner_send.at[block], recv_sem=owner_recv.at[me], device_id=(rep, to),
            device_id_type=MESH,
        )

    def each_owner(act):
        for block in range(SHARDS // 2):

            @pl.when(core * (SHARDS // 2) + block != me)
            def other():
                act(owner_copy(block))

    def own_outs(y_at):
        return outs.at[out_rows(y_at), out_half(core)]

    def side_sum():
        for copy in side_copies:
            copy.wait()
        part_gate[...] = (part_gate[...].astype(F32) + side_gate[...].astype(F32)).astype(BF)
        total = part_out[...].astype(F32) + side_out[...].astype(F32)
        outs[out_rows(along_y), out_half(core)] = total.astype(BF)
        each_owner(lambda copy: copy.start())

        @pl.when(owner_here)
        def keep():
            own = pl.ds(pl.multiple_of(lax.rem(me, 4) * PIECE, 16), PIECE)
            gates[own_piece, gate_columns(me)] = part_gate[own, :]

        for o in range(1, 4):
            send(14 + o, own_outs(along_y), own_outs(along_y), y_peer(o)).start()

    def share_gates():
        each_owner(lambda copy: copy.wait_send())

        @pl.when(owner_here)
        def collect():
            for o in range(1, SHARDS):
                from_shard(o).wait_recv()
            for o in range(1, 4):
                src = gates.at[own_piece]
                send(18 + o, src, src, y_peer(o)).start()

    def to_sibling():
        for o in range(1, 4):
            src = own_outs(y_of(4 - o))
            send(14 + o, src, src, y_peer(o)).wait()
        send(22, outs.at[:, out_half(core)], outs.at[:, out_half(core)], sibling(rep, me)).start()

        @pl.when(owner_here)
        def share():
            for o in range(1, 4):
                src = gates.at[pl.ds(pl.multiple_of(y_of(4 - o) * PIECE, 16), PIECE)]
                send(18 + o, src, src, y_peer(o)).wait()
            send(23, gates, gates, sibling(rep, me)).start()

    def early_done():
        send(22, outs.at[:, out_half(core)], outs.at[:, out_half(core)], sibling(rep, me)).wait_send()
        theirs = outs.at[:, out_half(1 - core)]
        send(22, theirs, theirs, sibling(rep, me)).wait_recv()

        @pl.when(owner_here)
        def sent():
            send(23, gates, gates, sibling(rep, me)).wait_send()

        @pl.when(jnp.logical_not(owner_here))
        def got():
            send(23, gates, gates, sibling(rep, me)).wait_recv()

        pltpu.make_async_copy(gates, gates_out, here.at[3]).start()
        pltpu.make_async_copy(outs, outs_out, here.at[10]).start()

    def backward(at, unused):
        @pl.when(at == 1)
        def hook_a():
            core_sum()

        @pl.when(at == 4)
        def hook_b():
            mix.middle()
            mix.cross()

        @pl.when(at == 10)
        def hook_c():
            y_sum()

        @pl.when(at == 9)
        def hook_d():
            mix.near()
            mix.last()

        @pl.when(at == 13)
        def hook_e():
            side_sum()

        backward_block(
            NB - 1 - at, first_len, proj, d_normed, taps[...], shift[...], step_bias, rate_log, skip_wide,
            y, states, small, heads, carry, late,
        )
        return unused

    lax.fori_loop(0, NB, backward, 0)

    def d_in_part(block, lanes):
        begin = pl.multiple_of(HALO + block * TOK, 16)
        return mm(proj[pl.ds(begin, TOK), :HALF], w_all[0, lanes, :], ((1,), (1,))) + mm(
            proj[pl.ds(begin, TOK), HALF:], w_all[1, lanes, : CH + 128], ((1,), (1,))
        )

    mix.arrived(5, 6, 7)
    for at in range(0, MODEL, WIDE):
        lanes = slice(at, at + WIDE)
        stage[1, :, lanes] = stage[0, :, lanes] + mix.total(lanes)
    store_mixed = pltpu.make_async_copy(stage.at[1], mixed_out, here.at[5])
    store_mixed.start()
    mix.sent()
    for peer in (left, right, across):
        pl.semaphore_signal(free, inc=1, device_id=(rep, peer), device_id_type=MESH)
    pl.semaphore_wait(free, 3)
    d_in = Scatter(d_in_part, scatter_out, scatter_in, grad_send, grad_recv)
    for slot in range(3):
        d_in.leaf(slot)
    store_mixed.wait()
    load_again = pltpu.make_async_copy(cotangent, stage.at[1], here.at[6])
    load_again.start()

    def small_copy(which):
        peer = (sibling, beside)[which](rep, me)
        return send(44 + which, packed.at[which], packed_in.at[which], peer)

    def small_first():
        small_copy(0).wait()
        packed[1] = packed[0] + packed_in[0]
        small_copy(1).start()

    def small_second():
        small_copy(1).wait()
        packed_y[along_y] = packed[1] + packed_in[1]
        for o in range(1, 4):
            send(46 + o, packed_y.at[along_y], packed_y.at[along_y], y_peer(o)).start()

    def small_third():
        for o in range(1, 4):
            src = packed_y.at[y_of(4 - o)]
            send(46 + o, src, src, y_peer(o)).wait()
        packed_all[me] = packed_y[0] + packed_y[1] + packed_y[2] + packed_y[3]
        for o in range(1, SHARDS):
            to = rep, lax.rem(me + o, SHARDS)
            send(50 + o, packed_all.at[me], packed_all.at[me], to).start()

    def small_last():
        for o in range(1, SHARDS):
            source = lax.rem(me + SHARDS - o, SHARDS)
            send(50 + o, packed_all.at[source], packed_all.at[source], (rep, source)).wait()
        pltpu.make_async_copy(packed_all, small_out, here.at[9]).start()

    def tail_tiles(which):
        def tile(at, unused):
            lanes = pl.ds(pl.multiple_of(at * 256, 256), 256)
            part = mm(x_all[:, lanes], proj[HALO:, part_columns(1 + which)], ((0,), (0,)))
            low_all[lanes, part_columns(1 + which)] = part.astype(BF)
            first = jnp.concatenate([w_all[0, lanes, CH:], w_all[1, lanes, :128]], axis=1).astype(F32)
            second = w_all[1, lanes, 128 : CH + 128].astype(F32)
            row_dots(at, part, jnp.where(which == 0, first, second))
            return unused

        lax.fori_loop(0, MODEL // 256, tile, 0)

    mine = part_columns(1 + core)
    share_gates()
    tail_tiles(1 - core)
    received = low_all.at[pl.ds(0, MODEL), part_columns(0)]
    core_copy = send(28, low_all.at[pl.ds(0, MODEL), part_columns(2 - core)], received, sibling(rep, me))
    pl.semaphore_wait(core_free, 1)
    core_copy.start()
    tail_tiles(core)
    packed[0] = jnp.zeros_like(packed[0])
    packed[0, :5, :XBC] = small[:5]
    packed[0, 5:6, :CH] = small[5:6, :CH]
    packed[0, 5:6, CH : 2 * CH] = gain_sum[...]
    packed[0, 5:6, 2 * CH : 2 * CH + 128] = heads[0:1]
    packed[0, 5:6, 2 * CH + 128 : 2 * CH + 256] = heads[1:2]
    packed[0, 6:7, :] = norm_sum[0:1, :] / norm_gain[...]
    small_copy(0).start()
    core_copy.wait()

    def add_core(at, unused):
        rows = block_rows(at)
        both = low_all[rows, mine].astype(F32) + low_all[rows, :CH].astype(F32)
        low_all[rows, mine] = both.astype(BF)
        return unused

    lax.fori_loop(0, MODEL // TOK, add_core, 0)
    for o in range(1, 4):
        for block in range(SHARDS):
            src = low_all.at[y_rows(block, y_of(o)), mine]
            send(28 + o, src, near_y.at[o - 1, pl.ds(block * PIECE, PIECE)], y_peer(o)).start()
    small_first()
    d_in.middle()
    for o in range(1, 4):
        send(28 + o, low_all.at[pl.ds(0, QUARTER), mine], near_y.at[o - 1], y_peer(o)).wait()
    for block in range(SHARDS):
        rows = slice(block * PIECE, (block + 1) * PIECE)
        total = low_all[y_rows(block, along_y), mine].astype(F32)
        for o in range(3):
            total = total + near_y[o, rows].astype(F32)
        quarter[rows] = total.astype(BF)
    side_copy = send(32, quarter, tail_swap, beside(rep, me))
    side_copy.start()
    small_second()
    to_sibling()
    d_in.near()
    side_copy.wait()
    quarter[...] = (quarter[...].astype(F32) + tail_swap[...].astype(F32)).astype(BF)
    for o in range(1, SHARDS):
        to = lax.rem(me + o, SHARDS)
        send(32 + o, quarter.at[own_quarter(to)], tail_pieces.at[me], (rep, to)).start()
    tail_pieces[me] = quarter[own_quarter(me), :]
    d_in.cross()
    d_in.last()
    small_third()
    early_done()
    for o in range(1, SHARDS):
        source = lax.rem(me + SHARDS - o, SHARDS)
        send(32 + o, quarter.at[own_quarter(source)], tail_pieces.at[source], (rep, source)).wait()

    @pl.when(core == 0)
    def assemble_first():
        total = tail_pieces[0, :, :BC].astype(F32)
        for block in range(1, SHARDS):
            total = total + tail_pieces[block, :, :BC].astype(F32)
        tail[0, own_piece, :BC] = total.astype(BF)
        for block in range(SHARDS):
            tail[0, own_piece, BC + 128 * block : BC + 128 * block + 128] = tail_pieces[block, :, BC:]
        tail[0, own_piece, BC + 1024 :] = jnp.zeros((PIECE, TAIL - BC - 1024), BF)

    @pl.when(core == 1)
    def assemble_second():
        total = jnp.zeros((PIECE, 128), F32)
        for block in range(SHARDS):
            tail[1, own_piece, 256 * block : 256 * block + 256] = tail_pieces[block, :, :256]
            put = (iota2((128, 128), 1) == iota2((128, 128), 0) + block * OWN) & (
                iota2((128, 128), 0) < OWN
            )
            total = total + mm(tail_pieces[block, :, 256:], put.astype(BF))
        tail[1, own_piece, 2048:] = total.astype(BF)

    for o in range(1, 4):
        src = tail.at[core, own_piece]
        send(40 + o, src, src, y_peer(o)).start()

    for o in range(1, 4):
        src = tail.at[core, pl.ds(pl.multiple_of(y_of(4 - o) * PIECE, 16), PIECE)]
        send(40 + o, src, src, y_peer(o)).wait()
    last_copy = send(58, tail.at[core], tail.at[core], sibling(rep, me))
    last_copy.start()
    small_last()
    d_in.arrived(5, 6, 7)
    for at in range(MODEL // CH):
        y[at * TOK : (at + 1) * TOK, :] = d_in.total(slice(at * CH, (at + 1) * CH))
    load_again.wait()
    def norm_back(at, unused):
        chunk = pl.ds(pl.multiple_of(at * CHUNK, CHUNK), CHUNK)
        rows = stage[0, chunk, :]
        pieces = [
            y[pl.ds(pl.multiple_of(k * TOK + at * CHUNK, CHUNK), CHUNK), :] for k in range(MODEL // CH)
        ]
        d_rows = jnp.concatenate(pieces, axis=1)
        scale = lax.rsqrt(jnp.mean(rows * rows, axis=1, keepdims=True) + epsilon)
        unit = rows * scale
        d_unit = d_rows * norm_gain[...]
        stage[1, chunk, :] += scale * (d_unit - unit * jnp.mean(d_unit * unit, axis=1, keepdims=True))
        return unused

    lax.fori_loop(0, TOK // CHUNK, norm_back, 0)
    store_grad = pltpu.make_async_copy(stage.at[1], grad_out, here.at[7])
    store_grad.start()

    send(58, tail.at[1 - core], tail.at[1 - core], sibling(rep, me)).wait_recv()
    last_copy.wait_send()
    store_tail = pltpu.make_async_copy(tail, tail_out, here.at[8])
    store_tail.start()
    d_in.sent()
    gather_x.sent()
    pltpu.make_async_copy(gates, gates_out, here.at[3]).wait()
    pltpu.make_async_copy(outs, outs_out, here.at[10]).wait()
    store_grad.wait()
    store_tail.wait()
    pltpu.make_async_copy(packed_all, small_out, here.at[9]).wait()


def scale_block(b, proj, y, totals, gain, normed_out):
    r0 = pl.multiple_of(b * L, L)
    gate = proj[pl.ds(pl.multiple_of(HALO + b * L, 16), L), :CH].astype(F32)
    inv = to_column(lax.rsqrt(totals[0, pl.ds(b, 1), :] * (1.0 / INNER) + epsilon))
    inv = jnp.concatenate([inv] * (CH // 128), axis=1)
    gated = y[pl.ds(r0, L), :] * (gate * sigmoid(gate))
    normed_out[pl.ds(r0, L), :] = (gated * inv * gain).astype(BF)


def prepare_block(b, proj, y, d_normed, totals, gain, gain_sum):
    r0 = pl.multiple_of(b * L, L)
    here = pl.ds(pl.multiple_of(HALO + b * L, 16), L)
    gate = proj[here, :CH].astype(F32)
    mixer = y[pl.ds(r0, L), :]
    sig = sigmoid(gate)
    silu = gate * sig
    gated = mixer * silu
    inv = lax.rsqrt(totals[0, pl.ds(b, 1), :] * (1.0 / INNER) + epsilon)
    back = inv * inv * inv * totals[1, pl.ds(b, 1), :] * (1.0 / INNER)
    inv = jnp.concatenate([to_column(inv)] * (CH // 128), axis=1)
    back = jnp.concatenate([to_column(back)] * (CH // 128), axis=1)
    dn = d_normed[pl.ds(r0, L), :].astype(F32)
    scaled = gated * inv
    gain_sum[...] += jnp.sum(dn * scaled, axis=0, keepdims=True)
    d_gated = inv * gain * dn - gated * back
    d_normed[pl.ds(r0, L), :] = (d_gated * silu).astype(BF)
    proj[here, :CH] = (d_gated * mixer * (sig + silu * (1.0 - sig))).astype(BF)


def backward_block(
    b, first_len, proj, d_out, taps, shift, step_bias, rate_log, skip, y_in, states, small, heads,
    carry, late,
):
    upper = (iota2((L, L), 1) >= iota2((L, L), 0)).astype(BF)
    columns = head_columns()
    r0 = pl.multiple_of(b * L, L)
    rows = proj[pl.ds(r0, HALO + L), :]
    gate, xbc, conv, raw, step, log_decay, cum = block_front(
        rows, r0, first_len, taps, shift, step_bias, rate_log
    )
    sig = sigmoid(conv)
    act = conv * sig
    x = act[:, BC:]
    b_low = act[:, :STATE].astype(BF)
    c_low = act[:, STATE:BC].astype(BF)
    cum_rows = jnp.transpose(cum)
    scores = mm(c_low, b_low, ((1,), (1,)))
    step_wide = spread(step)
    scaled = x * step_wide
    scaled_low = scaled.astype(BF)
    decays = decay_weights(cum, cum_rows)

    y = y_in[pl.ds(r0, L), :]
    dy_low = d_out[pl.ds(r0, L), :]
    dy = dy_low.astype(F32)

    state = states[b]
    end_state = states[b + 1]
    d_state = carry[...]
    state_low = state.astype(BF)
    d_state_low = d_state.astype(BF)
    enter = jnp.exp(spread(cum))
    tail = jnp.exp(spread(cum[L - 1 : L] - cum))
    lane = iota2((L, 128), 1)
    d_scores = jnp.zeros((L, L), F32)
    weights = []
    for h in range(OWN):
        part = slice(128 * (h // 2), 128 * (h // 2) + 128)
        mine = (lane < HEAD_DIM) if h % 2 == 0 else (lane >= HEAD_DIM)
        d_weight = mm(
            dy_low[:, part],
            jnp.where(mine, scaled[:, part], 0.0).astype(BF),
            ((1,), (1,)),
        )
        d_scores = d_scores + d_weight * decays[h]
        weights.append((decays[h] * scores).astype(BF))
    d_scores_low = d_scores.astype(BF)
    d_scaled = pair_mix(weights, dy_low, ((0,), (0,)))
    d_scaled = d_scaled + tail * mm(b_low, d_state_low, ((1,), (1,)))
    enter_dy = (enter * dy).astype(BF)
    d_c = mm(d_scores_low, b_low) + mm(enter_dy, state_low)
    d_b = mm(d_scores_low, c_low, ((0,), (0,))) + mm((tail * scaled).astype(BF), d_state_low)

    ssm = y - skip * x
    d_cum = mm_right(
        dy_low.astype(F32) * ssm - scaled_low.astype(F32) * d_scaled, columns, 3
    )
    through = jnp.zeros((1, 128), F32)
    for piece in split(end_state * d_state, 3):
        through = through + jnp.sum(
            mm(piece, columns, ((0,), (0,))), axis=0, keepdims=True
        )
    d_cum = d_cum + jnp.where(iota2((L, 1), 0) == L - 1, through, 0.0)
    d_log = mm_left(upper, d_cum, 3)
    rate = jnp.exp(rate_log)
    d_step = mm_right(d_scaled * x, columns, 3) - rate * d_log
    d_raw = d_step * sigmoid(raw)
    d_x = d_scaled * step_wide + skip * dy

    carry[...] = head_rows(cum_rows, L - 1) * d_state + mm(enter_dy, c_low, ((0,), (0,)))

    d_act = jnp.concatenate([d_b, d_c, d_x], axis=1)
    d_conv = d_act * (sig + act * (1.0 - sig))
    row = r0 + iota2((L + 8, 1), 0)
    longer = jnp.concatenate([d_conv, late[...]], axis=0)
    late[...] = d_conv[:8]
    d_xbc = jnp.zeros((L, XBC), F32)
    for k in range(CONV):
        ahead = CONV - 1 - k
        masked = longer
        if ahead:
            masked = longer * tap_mask(row, first_len, ahead)
        d_xbc = d_xbc + taps[k : k + 1] * masked[ahead : ahead + L]
        small[k : k + 1, :] += jnp.sum(
            masked[:L] * xbc[HALO - ahead : HALO - ahead + L], axis=0, keepdims=True
        )
    small[4:5, :] += jnp.sum(d_conv, axis=0, keepdims=True)
    small[5:6, :CH] += jnp.sum(dy * x, axis=0, keepdims=True)
    heads[0:1, :] += jnp.sum(d_raw, axis=0, keepdims=True)
    heads[1:2, :] += jnp.sum(d_log * log_decay, axis=0, keepdims=True)
    proj[pl.ds(pl.multiple_of(HALO + b * L, 16), L), CH:] = jnp.concatenate(
        [d_xbc, d_raw], axis=1
    ).astype(BF)


def finish_kernel(
    mixed_in, grad_in, gates, tail, outs, packed, mixed, grad, norm_grad, in_grad, conv_grad, bias_grad,
    dt_grad, rate_grad, skip_grad, gain_grad, out_grad, moved,
):
    copies = (
        pltpu.make_async_copy(mixed_in, mixed, moved.at[0]),
        pltpu.make_async_copy(grad_in, grad, moved.at[1]),
    )
    for copy in copies:
        copy.start()
    out_grad[0] = outs[...].astype(F32)
    in_grad[0, :, :INNER] = gates[...].astype(F32)
    for s in range(SHARDS):
        begin = INNER + CH * s
        in_grad[0, :, begin : begin + 128] = tail[0, :, BC + 128 * s : BC + 128 * s + 128].astype(F32)
        in_grad[0, :, begin + 128 : begin + CH] = tail[1, :, 256 * s : 256 * s + 256].astype(F32)
    in_grad[0, :, 2 * INNER : 2 * INNER + BC] = tail[0, :, :BC].astype(F32)
    in_grad[0, :, 2 * INNER + BC :] = tail[1, :, 2048 : 2048 + HEADS].astype(F32)
    parts = [packed[s] for s in range(SHARDS)]
    both = parts[0][:, :BC]
    for s in range(1, SHARDS):
        both = both + parts[s][:, :BC]
    conv_grad[0, :, INNER:] = both[:CONV]
    bias_grad[:, INNER:] = both[CONV : CONV + 1]
    heads = [jnp.zeros((8, 128), F32)] * 3
    for s in range(SHARDS):
        own = slice(CH * s, CH * s + CH)
        conv_grad[0, :, own] = parts[s][:CONV, BC:XBC]
        bias_grad[:, own] = parts[s][CONV : CONV + 1, BC:XBC]
        gain_grad[:, own] = parts[s][5:6, CH : 2 * CH]
        put = (iota2((128, 128), 1) == iota2((128, 128), 0) + s * OWN) & (iota2((128, 128), 0) < OWN)
        put_wide = iota2((CH, 128), 1) == iota2((CH, 128), 0) // HEAD_DIM + s * OWN
        rows = (
            (parts[s][5:6, 2 * CH : 2 * CH + 128], put),
            (parts[s][5:6, 2 * CH + 128 : 2 * CH + 256], put),
            (parts[s][5:6, :CH], put_wide),
        )
        for at, (row, to) in enumerate(rows):
            wide = jnp.broadcast_to(row, (8, row.shape[1]))
            heads[at] = heads[at] + mm_right(wide, to.astype(BF), 3)
    for at, ref in enumerate((dt_grad, rate_grad, skip_grad)):
        ref[...] = heads[at][0:1, :HEADS]
    total = parts[0][6:7]
    for s in range(1, SHARDS):
        total = total + parts[s][6:7]
    norm_grad[...] = total
    for copy in copies:
        copy.wait()


VM = pl.BlockSpec(memory_space=pltpu.VMEM)
SM = pl.BlockSpec(memory_space=pltpu.SMEM)
ANY = pl.BlockSpec(memory_space=pl.ANY)
LIMIT = 61 << 20


def local(
    resid,
    cotangent,
    first_length,
    norm_gain,
    in_weight,
    conv_weight,
    conv_bias,
    dt_bias,
    a_log,
    skip,
    gate_gain,
    out_weight,
):
    w = in_weight[0]
    narrow = jnp.pad(w[:, 2 * INNER :], ((0, 0), (0, 4 * 128 - BC - HEADS)))
    dma = pltpu.SemaphoreType.DMA
    outs = (
        ((TOK, MODEL), F32), ((TOK, MODEL), F32), ((ROWS, INNER), BF), ((2, ROWS, TAIL), BF),
        ((CH, MODEL), BF), ((SHARDS, 8, MODEL), F32),
    )
    scratch = (
        ((GROUP, MODEL), BF), ((GROUP, MODEL), BF), ((2, MODEL, HALF), BF),
        ((HALO + GROUP, COLS), BF), ((GROUP, CH), F32), ((NB + 1, CH, STATE), F32), ((GROUP, CH), BF),
        ((SHARDS, 2, NB, L), F32), ((CH, STATE), F32), ((2, TOK, MODEL), F32), ((CONV, XBC), F32),
        ((1, XBC), F32),
        ((2, NB, L), F32), ((GROUP, CH), BF), ((1, CH), F32), ((8, MODEL), F32), ((8, XBC), F32),
        ((8, 128), F32),
        ((8, XBC), F32), ((7, TOK, MODEL), BF), ((7, TOK, MODEL), BF),
        ((3, QUARTER, CH), BF), ((CH, HALF_OUT), BF), ((HALF_OUT, CH), BF), ((3, 96, HALF_OUT), BF),
        ((3, QUARTER // 2, CH), BF), ((96, HALF_OUT), BF), ((QUARTER // 2, CH), BF),
        ((96, HALF_OUT), BF), ((QUARTER // 2, CH), BF),
        ((QUARTER, CH), BF),
        ((ROWS, INNER), BF), ((CH, MODEL), BF),
        ((QUARTER, CH), BF),
        ((SHARDS, PIECE, CH), BF), ((2, ROWS, TAIL), BF),
        ((2, 8, MODEL), F32), ((2, 8, MODEL), F32), ((4, 8, MODEL), F32), ((SHARDS, 8, MODEL), F32),
    )
    mixed, grad, gates, tail, out_grad, packed = pl.pallas_call(
        layer_kernel,
        out_shape=tuple(jax.ShapeDtypeStruct(*shape) for shape in outs),
        in_specs=[SM, ANY, ANY, ANY, ANY] + [VM] * 8,
        out_specs=(ANY,) * 6,
        scratch_shapes=[pltpu.VMEM(*shape) for shape in scratch]
        + [dma((11,))] * 4 + [dma((SHARDS,))] * 2 + [dma((4,))] * 2 + [dma((1,))] * 2
        + [dma((2 * SHARDS,))] * 2 + [dma((11,))] + [dma((10,))] * 4 + [dma((60,))] * 2 + [dma((SHARDS,))] * 2
        + [pltpu.SemaphoreType.REGULAR] * 2,
        compiler_params=pltpu.CompilerParams(
            vmem_limit_bytes=LIMIT, collective_id=0, has_side_effects=True
        ),
    )(
        first_length, resid, cotangent, w, narrow, out_weight[0], norm_gain, conv_weight[0], conv_bias,
        dt_bias, a_log, skip, gate_gain,
    )
    wide = CONVCH
    shapes = (
        (TOK, MODEL), (TOK, MODEL), (1, MODEL), (1, ROWS, 2 * INNER + BC + HEADS), (1, CONV, wide), (1, wide),
        (1, HEADS), (1, HEADS), (1, HEADS), (1, INNER), (1, CH, MODEL),
    )
    return pl.pallas_call(
        finish_kernel,
        out_shape=tuple(jax.ShapeDtypeStruct(shape, F32) for shape in shapes),
        in_specs=[VM] * 6,
        out_specs=(ANY, ANY) + (VM,) * 9,
        scratch_shapes=[dma((2,))],
        compiler_params=pltpu.CompilerParams(vmem_limit_bytes=LIMIT),
    )(mixed, grad, gates, tail, out_grad, packed)


def solution(mesh):
    rows = P(("rep", "shard"), None)
    weight = P(None, "shard", None)
    return jax.shard_map(
        local,
        mesh=mesh,
        in_specs=(rows, rows, P("rep"), P(), weight, P(), P(), P(), P(), P(), P(), weight),
        out_specs=(rows, rows, P(), weight, P(), P(), P(), P(), P(), P(), weight),
        check_vma=False,
    )
```

```python
import jax
import jax.numpy as jnp
from jax import lax
from jax.experimental import pallas as pl
from jax.experimental.pallas import tpu as pltpu
from jax.sharding import PartitionSpec as P

HEADS = 48
HEAD_DIM = 64
STATE = 128
CONV = 4
INNER = 3072
CONVCH = 3328
MODEL = 1536
SHARDS = 8
OWN = HEADS // SHARDS
CH = OWN * HEAD_DIM
XBC = CH + 2 * STATE
HALF = 640
COLS = 2 * CH + 2 * STATE + 128
BC = 2 * STATE
TOK = 256
GROUP = TOK * SHARDS
L = 128
NB = GROUP // L
HALO = 16
PIECE = 48
MESH = pl.DeviceIdType.MESH
ROWS = MODEL // SHARDS
QUARTER = SHARDS * PIECE
TAIL_WIDTH = (2 * 128 + 8 * 128, 8 * 256 + 128)
TAIL = max(TAIL_WIDTH)
FRONT = 64
CHUNK = 32
HALF_OUT = MODEL // 2
WIDE = 512
OUT_PART = pl.ds(MODEL, CH)
RESET = -200.0

epsilon = 1e-05
F32 = jnp.float32
BF = jnp.bfloat16


def mm(a, b, dims=((1,), (0,))):
    return lax.dot_general(a, b, (dims, ((), ())), preferred_element_type=F32)


def split(v, parts):
    out = []
    for _ in range(parts):
        piece = v.astype(BF)
        out.append(piece)
        v = v - piece.astype(F32)
    return out


def mm_left(ones, v, parts):
    return sum(mm(ones, piece) for piece in split(v, parts))


def mm_right(v, ones, parts):
    return sum(mm(piece, ones) for piece in split(v, parts))


def iota2(shape, dim):
    return lax.broadcasted_iota(jnp.int32, shape, dim)


def head_columns():
    return (iota2((CH, 128), 0) // HEAD_DIM == iota2((CH, 128), 1)).astype(BF)


def spread(per_head):
    lane = iota2((per_head.shape[0], 128), 1)
    tiles = []
    for pair in range(OWN // 2):
        left = per_head[:, 2 * pair : 2 * pair + 1]
        right = per_head[:, 2 * pair + 1 : 2 * pair + 2]
        tiles.append(jnp.where(lane < HEAD_DIM, left, right))
    return jnp.concatenate(tiles, axis=1)


def head_rows(cum_rows, at):
    pieces = [
        jnp.broadcast_to(cum_rows[h : h + 1, at : at + 1], (HEAD_DIM, 1)) for h in range(OWN)
    ]
    return jnp.exp(jnp.concatenate(pieces, axis=0))


def tap_mask(row, first_len, back):
    past = row - first_len
    return jnp.where((past >= 0) & (past < back), 0.0, 1.0)


def block_front(rows, r0, first_len, taps, shift, step_bias, rate_log):
    xbc = rows[:, CH : CH + XBC].astype(F32)
    row = r0 + iota2((L, 1), 0)
    conv = jnp.broadcast_to(shift, (L, XBC))
    for k in range(CONV):
        back = CONV - 1 - k
        term = taps[k : k + 1] * xbc[HALO - back : HALO - back + L]
        if back:
            term = term * tap_mask(row, first_len, back)
        conv = conv + term
    gate = rows[HALO:, :CH].astype(F32)
    raw = rows[HALO:, CH + XBC :].astype(F32) + step_bias
    step = jnp.maximum(raw, 0.0) + jnp.log1p(jnp.exp(-jnp.abs(raw)))
    log_decay = -step * jnp.exp(rate_log)
    with_reset = log_decay + jnp.where(row == first_len, RESET, 0.0)
    lower = (iota2((L, L), 0) >= iota2((L, L), 1)).astype(BF)
    cum = mm_left(lower, with_reset, 3)
    return gate, xbc, conv, raw, step, log_decay, cum


def sigmoid(v):
    return 0.5 * jnp.tanh(0.5 * v) + 0.5


def pair_mix(weights, value, dims=((1,), (0,))):
    lane = iota2((L, 128), 1)
    tiles = []
    for pair in range(OWN // 2):
        part = value[:, 128 * pair : 128 * pair + 128]
        tiles.append(
            jnp.where(
                lane < HEAD_DIM,
                mm(weights[2 * pair], part, dims),
                mm(weights[2 * pair + 1], part, dims),
            )
        )
    return jnp.concatenate(tiles, axis=1)


def decay_weights(cum, cum_rows):
    causal = iota2((L, L), 0) >= iota2((L, L), 1)
    out = []
    for h in range(OWN):
        gap = cum[:, h : h + 1] - cum_rows[h : h + 1, :]
        out.append(jnp.exp(jnp.where(causal, gap, -1e30)))
    return out


def to_row(column):
    return jnp.transpose(jnp.broadcast_to(column, (L, L)))[0:1]


def to_column(row):
    return jnp.transpose(jnp.broadcast_to(row, (L, L)))


def forward_block(b, first_len, proj, taps, shift, step_bias, rate_log, skip, y_out, states, sums, carry):
    r0 = pl.multiple_of(b * L, L)
    rows = proj[pl.ds(r0, HALO + L), :]
    gate, xbc, conv, raw, step, log_decay, cum = block_front(
        rows, r0, first_len, taps, shift, step_bias, rate_log
    )
    act = conv * sigmoid(conv)
    x = act[:, BC:]
    b_low = act[:, :STATE].astype(BF)
    c_low = act[:, STATE:BC].astype(BF)
    cum_rows = jnp.transpose(cum)
    scores = mm(c_low, b_low, ((1,), (1,)))
    scaled = x * spread(step)
    scaled_low = scaled.astype(BF)
    weights = [(w * scores).astype(BF) for w in decay_weights(cum, cum_rows)]
    state = carry[...]
    states[b] = state
    y = pair_mix(weights, scaled_low)
    y = y + spread(jnp.exp(cum)) * mm(c_low, state.astype(BF), ((1,), (1,)))
    tail = spread(jnp.exp(cum[L - 1 : L] - cum))
    carry[...] = head_rows(cum_rows, L - 1) * state + mm(
        (tail * scaled).astype(BF), b_low, ((0,), (0,))
    )
    y = y + skip * x
    y_out[pl.ds(r0, L), :] = y
    gated = y * (gate * sigmoid(gate))
    sums[pl.ds(b, 1), :] = to_row(jnp.sum(gated * gated, axis=1, keepdims=True))


def place_of():
    rep, me = lax.axis_index("rep"), lax.axis_index("shard")
    hi, z = me // 4, lax.rem(me, 4)
    left = hi * 4 + lax.rem(z + 3, 4)
    right = hi * 4 + lax.rem(z + 1, 4)
    far = hi * 4 + lax.rem(z + 2, 4)
    across = lax.rem(me + 4, 8)
    return rep, me, left, right, far, across


def sibling(rep, me):
    return rep + 1 - 2 * lax.rem(rep, 2), me


def beside(rep, me):
    return rep + 2 - 4 * lax.rem(rep // 2, 2), me


def other_side(block):
    return lax.rem(block + 4, 8)


def enter(rep, me):
    barrier = pltpu.get_barrier_semaphore()
    peers = [(rep, lax.rem(me + o, SHARDS)) for o in range(1, SHARDS)]
    peers += [(lax.rem(rep + 4 * o, 16), me) for o in range(1, 4)]
    peers += [sibling(rep, me), beside(rep, me)]
    for peer in peers:
        pl.semaphore_signal(barrier, inc=1, device_id=peer, device_id_type=MESH)
    return lambda: pl.semaphore_wait(barrier, len(peers))


def block_rows(block, part=(0, TOK)):
    begin, end = part
    return pl.ds(pl.multiple_of(block * TOK + begin, 16), end - begin)


FIRST, SECOND = (0, TOK // 2), (TOK // 2, TOK)
EDGE = 48
TOP, REST = (0, EDGE), (EDGE, TOK)


class Gather:
    def __init__(self, blocks, send, recv):
        self.blocks, self.send, self.recv = blocks, send, recv
        self.rep, self.me, self.left, self.right, self.far, self.across = place_of()

    def move(self, channel, block, to, rows=(0, TOK)):
        ref = self.blocks.at[block_rows(block, rows)]
        return pltpu.make_async_remote_copy(
            src_ref=ref,
            dst_ref=ref,
            send_sem=self.send.at[channel],
            recv_sem=self.recv.at[channel],
            device_id=(self.rep, to),
            device_id_type=MESH,
        )

    def outgoing(self, channel):
        me, left, right, across = self.me, self.left, self.right, self.across
        return (
            lambda: self.move(0, me, right),
            lambda: self.move(1, me, left),
            lambda: self.move(2, me, across),
            lambda: self.move(3, left, right, FIRST),
            lambda: self.move(4, right, left, SECOND),
            lambda: self.move(5, across, right, REST),
            lambda: self.move(6, across, left, REST),
            lambda: self.move(7, self.far, across, FIRST),
            lambda: self.move(8, self.far, across, SECOND),
            lambda: self.move(9, left, across, TOP),
            lambda: self.move(10, right, across, TOP),
        )[channel]()

    def incoming(self, channel):
        left, right, far, across = self.left, self.right, self.far, self.across
        return (
            lambda: self.move(0, left, left),
            lambda: self.move(1, right, right),
            lambda: self.move(2, across, across),
            lambda: self.move(3, far, left, FIRST),
            lambda: self.move(4, far, right, SECOND),
            lambda: self.move(5, other_side(left), left, REST),
            lambda: self.move(6, other_side(right), right, REST),
            lambda: self.move(7, other_side(far), across, FIRST),
            lambda: self.move(8, other_side(far), across, SECOND),
            lambda: self.move(9, other_side(left), across, TOP),
            lambda: self.move(10, other_side(right), across, TOP),
        )[channel]()

    def start(self, *channels):
        for channel in channels:
            self.outgoing(channel).start()

    def arrived(self, *channels):
        for channel in channels:
            self.incoming(channel).wait_recv()

    def sent(self):
        for channel in range(11):
            self.outgoing(channel).wait_send()


class Scatter:
    SLOTS = (
        (0, (0, TOK)), (1, REST), (2, REST), (3, FIRST), (3, SECOND), (4, (0, TOK)), (5, (0, TOK)),
        (6, (0, TOK)), (1, TOP), (2, TOP),
    )

    def __init__(self, part, out, into, send, recv):
        self.part, self.out, self.into, self.send, self.recv = part, out, into, send, recv
        self.rep, self.me, self.left, self.right, self.far, self.across = place_of()
        self.to = (
            self.across, self.left, self.right, self.left, self.right, self.right, self.left, self.across,
            self.across, self.across,
        )

    def copy(self, channel):
        slot, rows = self.SLOTS[channel]
        at = (slot, pl.ds(rows[0], rows[1] - rows[0]))
        return pltpu.make_async_remote_copy(
            src_ref=self.out.at[at],
            dst_ref=self.into.at[at],
            send_sem=self.send.at[channel],
            recv_sem=self.recv.at[channel],
            device_id=(self.rep, self.to[channel]),
            device_id_type=MESH,
        )

    def arrived(self, *channels):
        for channel in channels:
            self.copy(channel).wait_recv()

    def fill(self, slot, block, *arrived):
        for at in range(0, MODEL, WIDE):
            lanes = slice(at, at + WIDE)
            value = self.part(block, lanes)
            for other in arrived:
                value = value + self.into[other, :, lanes].astype(F32)
            self.out[slot, :, lanes] = value.astype(BF)

    def add(self, slot, into, rows):
        rows = slice(*rows)
        value = self.out[slot, rows].astype(F32)
        for other in into:
            value = value + self.into[other, rows].astype(F32)
        self.out[slot, rows] = value.astype(BF)

    def leaf(self, slot):
        self.fill(slot, other_side((self.far, self.left, self.right)[slot]))
        self.copy(slot).start()
        if slot:
            self.copy(7 + slot).start()

    def middle(self):
        self.arrived(0)
        self.fill(3, self.far, 0)
        self.copy(3).start()
        self.copy(4).start()
        self.fill(6, self.across)
        self.arrived(1, 2)
        self.add(6, (1, 2), REST)

    def cross(self):
        self.copy(7).start()

    def near(self):
        self.fill(4, self.right)
        self.fill(5, self.left)

    def last(self):
        self.arrived(8, 9)
        self.add(4, (2,), TOP)
        self.add(5, (1,), TOP)
        self.arrived(3, 4)
        self.add(4, (3,), SECOND)
        self.copy(5).start()
        self.add(5, (3,), FIRST)
        self.copy(6).start()

    def total(self, lanes):
        value = self.part(self.me, lanes)
        for slot in (4, 5, 6):
            value = value + self.into[slot, :, lanes].astype(F32)
        return value

    def sent(self):
        for channel in range(10):
            self.copy(channel).wait_send()


def own_heads(vector, me):
    pick = (iota2((HEADS, 128), 0) == iota2((HEADS, 128), 1) + me * OWN) & (
        iota2((HEADS, 128), 1) < OWN
    )
    wide = jnp.broadcast_to(vector, (8, HEADS))
    return mm_right(wide, pick.astype(BF), 3)[0:1]


def own_channels(vector, me):
    pick = iota2((HEADS, CH), 0) == iota2((HEADS, CH), 1) // HEAD_DIM + me * OWN
    wide = jnp.broadcast_to(vector, (8, HEADS))
    return mm_right(wide, pick.astype(BF), 3)[0:1]


def own_slices(me, conv_weight, conv_bias):
    own = pl.ds(pl.multiple_of(me * CH, 128), CH)
    taps = jnp.concatenate([conv_weight[:, INNER:], conv_weight[:, own]], axis=1)
    shift = jnp.concatenate([conv_bias[:, INNER:], conv_bias[:, own]], axis=1)
    return taps, shift


def layer_kernel(
    first_ref, resid, cotangent, w_in, narrow, w_out, norm_gain, conv_weight, conv_bias, dt_bias,
    a_log, skip, gate_gain,
    mixed_out, grad_out, gates_out, tail_out, outs_out, small_out,
    x_all, low_all, w_all, proj, y, states, d_normed, sums, carry, stage, taps, shift,
    totals, normed_out, gain_sum, norm_sum, small, heads, late, scatter_out, scatter_in,
    near_y, core_out, core_gate, near_out, near_gate, part_out, part_gate, side_out, side_gate,
    quarter, gates, outs,
    tail_swap, tail_pieces, tail,
    packed, packed_in, packed_y, packed_all,
    x_send, x_recv, low_send, low_recv, piece_send, piece_recv, y_send, y_recv, core_send, core_recv,
    sum_send, sum_recv, here, mix_send, mix_recv, grad_send, grad_recv, g_send, g_recv, owner_send, owner_recv, free, core_free,
):
    rep, me, left, right, far, across = place_of()
    core = lax.rem(rep, 2)
    along_y = rep // 4
    first_len = first_ref[0]
    load_resid = pltpu.make_async_copy(resid, stage.at[0], here.at[0])
    load_cot = pltpu.make_async_copy(cotangent, stage.at[1], here.at[1])
    load_resid.start()
    load_cot.start()
    all_entered = enter(rep, me)

    load_resid.wait()

    def norm_rows(at, unused):
        rows = stage[0, pl.ds(pl.multiple_of(at * FRONT, FRONT), FRONT), :]
        scale = lax.rsqrt(jnp.mean(rows * rows, axis=1, keepdims=True) + epsilon)
        own = pl.ds(pl.multiple_of(me * TOK + at * FRONT, FRONT), FRONT)
        x_all[own, :] = (rows * scale * norm_gain[...]).astype(BF)
        return unused

    lax.fori_loop(0, TOK // FRONT, norm_rows, 0)
    all_entered()
    gather_x = Gather(x_all, x_send, x_recv)
    gather_x.start(0, 1, 2)

    own_rows = pl.ds(pl.multiple_of(along_y * PIECE, 16), PIECE)

    def landing(block):
        return pl.ds(pl.multiple_of(block * 192 + along_y * PIECE, 16), PIECE)

    def weight_pieces(to, make):
        wide = pl.ds(pl.multiple_of(core * INNER + to * CH, 128), CH)
        half = pl.ds(pl.multiple_of(core * BC, 128), BC)
        make(w_in.at[own_rows, wide], w_all.at[core, landing(me), pl.ds(0, CH)])
        make(narrow.at[own_rows, half], w_all.at[core, landing(me), pl.ds(CH, BC)])

    for o in range(1, SHARDS):
        to = lax.rem(me + o, SHARDS)
        weight_pieces(
            to,
            lambda src, dst: pltpu.make_async_remote_copy(
                src_ref=src, dst_ref=dst, send_sem=piece_send.at[o], recv_sem=piece_recv.at[o],
                device_id=(rep, to), device_id_type=MESH,
            ).start(),
        )
    weight_pieces(me, lambda src, dst: pltpu.make_async_copy(src, dst, here.at[2]).start())

    load_cot.wait()
    low_all[block_rows(me), :] = stage[1].astype(BF)
    gather_low = Gather(low_all, low_send, low_recv)

    taps_now, shift_now = own_slices(me, conv_weight, conv_bias)
    taps[...] = taps_now
    shift[...] = shift_now
    proj[pl.ds(0, HALO), :] = jnp.zeros((HALO, COLS), BF)
    carry[...] = jnp.zeros_like(carry)

    pltpu.make_async_copy(
        w_all.at[core, landing(me)], w_all.at[core, landing(me)], here.at[2]
    ).wait()
    for o in range(1, SHARDS):
        source = lax.rem(me + SHARDS - o, SHARDS)
        piece = w_all.at[core, landing(source)]
        pltpu.make_async_remote_copy(
            src_ref=piece, dst_ref=piece, send_sem=piece_send.at[o], recv_sem=piece_recv.at[o],
            device_id=(rep, source), device_id_type=MESH,
        ).wait()
    for o in range(1, 4):
        for block in range(SHARDS):
            piece = w_all.at[core, landing(block)]
            pltpu.make_async_remote_copy(
                src_ref=piece, dst_ref=piece, send_sem=y_send.at[o], recv_sem=y_recv.at[o],
                device_id=(lax.rem(rep + 4 * o, 16), me), device_id_type=MESH,
            ).start()
    gather_x.arrived(0)
    gather_x.start(3, 9)
    gather_x.arrived(1)
    gather_x.start(4, 10)
    gather_x.arrived(2)
    gather_x.start(5, 6)
    gather_x.arrived(3)
    gather_x.start(7)
    gather_x.arrived(4)
    gather_x.start(8)
    gather_low.start(0, 1, 2)
    for o in range(1, 4):
        landed = w_all.at[core, pl.ds(0, QUARTER)]
        pltpu.make_async_remote_copy(
            src_ref=landed, dst_ref=landed, send_sem=y_send.at[o], recv_sem=y_recv.at[o],
            device_id=(lax.rem(rep + 4 * o, 16), me), device_id_type=MESH,
        ).wait()

    def halves(which):
        return pltpu.make_async_remote_copy(
            src_ref=w_all.at[which], dst_ref=w_all.at[which], send_sem=core_send.at[0],
            recv_sem=core_recv.at[0], device_id=(rep + 1 - 2 * core, me), device_id_type=MESH,
        )

    halves(core).start()
    halves(1 - core).wait_recv()
    halves(core).wait_send()
    pick = (iota2((128, 128), 0) == iota2((128, 128), 1) + me * OWN) & (iota2((128, 128), 1) < OWN)
    w_all[1, :, CH : CH + 128] = mm(w_all[1, :, CH : CH + 128], pick.astype(BF)).astype(BF)

    side = (me // 4) * 4

    def project(at, unused):
        rows = x_all[block_rows(at), :]
        begin = pl.multiple_of(HALO + at * TOK, 16)
        proj[pl.ds(begin, TOK), :HALF] = mm(rows, w_all[0]).astype(BF)
        proj[pl.ds(begin, TOK), HALF:] = mm(rows, w_all[1, :, : CH + 128]).astype(BF)
        return unused

    lax.fori_loop(side, side + 4, project, 0)
    gather_low.arrived(0)
    gather_low.start(3, 9)
    gather_low.arrived(1)
    gather_low.start(4, 10)
    gather_x.arrived(5, 6, 7, 8, 9, 10)
    lax.fori_loop(4 - side, 8 - side, project, 0)

    step_bias = own_heads(dt_bias[...], me)
    rate_log = own_heads(a_log[...], me)
    skip_wide = own_channels(skip[...], me)

    def scan(b, unused):
        @pl.when(b == 6)
        def relay():
            gather_low.arrived(3, 4, 2)
            gather_low.start(7, 8, 5, 6)

        forward_block(
            b, first_len, proj, taps[...], shift[...], step_bias, rate_log, skip_wide, y, states,
            sums.at[me, 0], carry,
        )
        return unused

    lax.fori_loop(0, NB, scan, 0)
    states[NB] = carry[...]

    gain = gate_gain[:, pl.ds(pl.multiple_of(me * CH, 128), CH)]

    def normed(at, unused):
        begin = pl.multiple_of(at * TOK, TOK)
        dn = mm(low_all[block_rows(at), :], w_out[...], ((1,), (1,)))
        d_normed[pl.ds(begin, TOK), :] = dn.astype(BF)
        gate = proj[pl.ds(HALO + begin, TOK), :CH].astype(F32)
        gated = y[pl.ds(begin, TOK), :] * (gate * sigmoid(gate))
        both = jnp.sum(gated * gain * dn, axis=1, keepdims=True)
        sums[me, 1, pl.ds(2 * at, 1), :] = to_row(both[:L])
        sums[me, 1, pl.ds(2 * at + 1, 1), :] = to_row(both[L:])
        return unused

    def sum_copy(kind, o, slot, to):
        ref = sums.at[slot, kind]
        return pltpu.make_async_remote_copy(
            src_ref=ref, dst_ref=ref, send_sem=sum_send.at[SHARDS * kind + o],
            recv_sem=sum_recv.at[SHARDS * kind + o], device_id=(rep, to), device_id_type=MESH,
        )

    def start_sum(kind):
        for o in range(1, SHARDS):
            sum_copy(kind, o, me, lax.rem(me + o, SHARDS)).start()

    def end_sum(kind):
        for o in range(1, SHARDS):
            source = lax.rem(me + SHARDS - o, SHARDS)
            sum_copy(kind, o, source, source).wait_recv()
        total = sums[0, kind]
        for slot in range(1, SHARDS):
            total = total + sums[slot, kind]
        totals[kind] = total
        for o in range(1, SHARDS):
            sum_copy(kind, o, me, lax.rem(me + o, SHARDS)).wait_send()

    def scale_out(b, unused):
        scale_block(b, proj, y, totals, gain, normed_out)
        return unused

    def mixed_part(block, lanes):
        return mm(normed_out[block_rows(block), :], w_out[:, lanes])

    mix = Scatter(mixed_part, scatter_out, scatter_in, mix_send, mix_recv)
    start_sum(0)
    lax.fori_loop(side, side + 4, normed, 0)
    end_sum(0)
    lax.fori_loop(0, NB, scale_out, 0)
    gather_low.arrived(5, 6, 9, 10)

    def normed_near(at, unused):
        return normed(other_side(side + lax.rem(me + at, 4)), unused)

    lax.fori_loop(3, 6, normed_near, 0)
    gather_low.arrived(7, 8)
    lax.fori_loop(6, 7, normed_near, 0)
    start_sum(1)

    def send(index, src, dst, to):
        return pltpu.make_async_remote_copy(
            src_ref=src, dst_ref=dst, send_sem=g_send.at[index], recv_sem=g_recv.at[index],
            device_id=to, device_id_type=MESH,
        )

    def y_peer(o):
        return lax.rem(rep + 4 * o, 16), me

    def y_of(o):
        return lax.rem(along_y + o, 4)

    gain_sum[...] = jnp.zeros_like(gain_sum)
    small[...] = jnp.zeros_like(small)
    heads[...] = jnp.zeros_like(heads)
    late[...] = jnp.zeros_like(late)
    carry[...] = jnp.zeros_like(carry)

    def prepare(b, unused):
        prepare_block(b, proj, y, d_normed, totals, gain, gain_sum)
        return unused

    for slot in range(3):
        mix.leaf(slot)
    gather_low.sent()
    def row_dots(at, part, weight):
        dots = jnp.sum(part * weight.astype(F32), axis=1, keepdims=True)
        for half in range(2):
            lanes = pl.ds(pl.multiple_of(at * 256 + half * L, L), L)
            norm_sum[0:1, lanes] += to_row(dots[half * L : half * L + L])

    norm_sum[...] = jnp.zeros_like(norm_sum)

    def out_tile(at, unused):
        lanes = pl.ds(pl.multiple_of(at * 256, 256), 256)
        low = low_all[:, lanes]
        low_all[OUT_PART, lanes] = mm(normed_out[...], low, ((0,), (0,))).astype(BF)
        return unused

    def gate_tile(at, unused):
        lanes = pl.ds(pl.multiple_of(at * 256, 256), 256)
        rows = x_all[:, lanes]
        part = mm(rows, proj[HALO:, :CH], ((0,), (0,)))
        low_all[lanes, :CH] = part.astype(BF)
        row_dots(at, part, w_all[0, lanes, :CH])
        return unused

    def y_rows(block, y_at):
        return pl.ds(pl.multiple_of(block * ROWS + y_at * PIECE, 16), PIECE)

    def out_rows(y_at, base=0):
        return pl.ds(pl.multiple_of(base + y_at * 96, 16), 96)

    def part_columns(which):
        return pl.ds(pl.multiple_of(which * CH, 128), CH)

    def out_half(which):
        return pl.ds(pl.multiple_of(which * HALF_OUT, 128), HALF_OUT)

    def gate_half(which):
        return pl.ds(pl.multiple_of(which * HALF_OUT, 128), HALF_OUT)

    core_copies = (
        send(1, low_all.at[OUT_PART, out_half(1 - core)], core_out, sibling(rep, me)),
        send(2, low_all.at[gate_half(1 - core), pl.ds(0, CH)], core_gate, sibling(rep, me)),
    )
    lax.fori_loop(0, MODEL // 256, out_tile, 0)
    core_copies[0].start()
    end_sum(1)
    lax.fori_loop(0, NB, prepare, 0)
    lax.fori_loop(0, MODEL // 256, gate_tile, 0)
    core_copies[1].start()

    def gate_piece(block, y_at):
        return pl.ds(pl.multiple_of(core * HALF_OUT + block * ROWS + y_at * PIECE, 16), PIECE)

    def out_to_y(o):
        src = low_all.at[out_rows(y_of(o), MODEL), out_half(core)]
        return send(2 + o, src, near_out.at[o - 1], y_peer(o))

    def gate_to_y(o, block):
        dst = near_gate.at[o - 1, pl.ds(block * PIECE, PIECE)]
        return send(5 + o, low_all.at[gate_piece(block, y_of(o)), pl.ds(0, CH)], dst, y_peer(o))

    def core_sum():
        for copy in core_copies:
            copy.wait()
        mine = out_half(core)
        both = low_all[OUT_PART, mine].astype(F32) + core_out[...].astype(F32)
        low_all[OUT_PART, mine] = both.astype(BF)
        both = low_all[gate_half(core), :CH].astype(F32) + core_gate[...].astype(F32)
        low_all[gate_half(core), :CH] = both.astype(BF)
        for o in range(1, 4):
            out_to_y(o).start()
            for block in range(SHARDS // 2):
                gate_to_y(o, block).start()

    side_copies = (
        send(9, part_gate, side_gate, beside(rep, me)),
        send(10, part_out, side_out, beside(rep, me)),
    )

    def y_sum():
        for o in range(1, 4):
            out_to_y(o).wait()
            landed = low_all.at[pl.ds(0, HALF_OUT // 4), pl.ds(0, CH)]
            send(5 + o, landed, near_gate.at[o - 1], y_peer(o)).wait()
        total = low_all[out_rows(along_y, MODEL), out_half(core)].astype(F32)
        for o in range(3):
            total = total + near_out[o].astype(F32)
        part_out[...] = total.astype(BF)
        for block in range(SHARDS // 2):
            rows = slice(block * PIECE, (block + 1) * PIECE)
            total = low_all[gate_piece(block, along_y), :CH].astype(F32)
            for o in range(3):
                total = total + near_gate[o, rows].astype(F32)
            part_gate[rows] = total.astype(BF)
        for copy in side_copies:
            copy.start()
        pl.semaphore_signal(
            core_free, inc=1, device_id=sibling(rep, me), device_id_type=MESH
        )

    own_piece = pl.ds(pl.multiple_of(along_y * PIECE, 16), PIECE)

    def gate_columns(block):
        return pl.ds(pl.multiple_of(block * CH, 128), CH)

    def own_quarter(block):
        return pl.ds(pl.multiple_of(block * PIECE, 16), PIECE)

    owner_here = core == me // 4

    def from_shard(o):
        source = lax.rem(me + SHARDS - o, SHARDS)
        dst = gates.at[own_piece, gate_columns(source)]
        return pltpu.make_async_remote_copy(
            src_ref=dst, dst_ref=dst, send_sem=owner_send.at[me], recv_sem=owner_recv.at[source],
            device_id=(rep, source), device_id_type=MESH,
        )

    def owner_copy(block):
        to = core * (SHARDS // 2) + block
        return pltpu.make_async_remote_copy(
            src_ref=part_gate.at[pl.ds(block * PIECE, PIECE)], dst_ref=gates.at[own_piece, gate_columns(me)],
            send_sem=owner_send.at[block], recv_sem=owner_recv.at[me], device_id=(rep, to),
            device_id_type=MESH,
        )

    def each_owner(act):
        for block in range(SHARDS // 2):

            @pl.when(core * (SHARDS // 2) + block != me)
            def other():
                act(owner_copy(block))

    def own_outs(y_at):
        return outs.at[out_rows(y_at), out_half(core)]

    def side_sum():
        for copy in side_copies:
            copy.wait()
        part_gate[...] = (part_gate[...].astype(F32) + side_gate[...].astype(F32)).astype(BF)
        total = part_out[...].astype(F32) + side_out[...].astype(F32)
        outs[out_rows(along_y), out_half(core)] = total.astype(BF)
        each_owner(lambda copy: copy.start())

        @pl.when(owner_here)
        def keep():
            own = pl.ds(pl.multiple_of(lax.rem(me, 4) * PIECE, 16), PIECE)
            gates[own_piece, gate_columns(me)] = part_gate[own, :]

        for o in range(1, 4):
            send(14 + o, own_outs(along_y), own_outs(along_y), y_peer(o)).start()

    def share_gates():
        each_owner(lambda copy: copy.wait_send())

        @pl.when(owner_here)
        def collect():
            for o in range(1, SHARDS):
                from_shard(o).wait_recv()
            for o in range(1, 4):
                src = gates.at[own_piece]
                send(18 + o, src, src, y_peer(o)).start()

    def to_sibling():
        for o in range(1, 4):
            src = own_outs(y_of(4 - o))
            send(14 + o, src, src, y_peer(o)).wait()
        send(22, outs.at[:, out_half(core)], outs.at[:, out_half(core)], sibling(rep, me)).start()

        @pl.when(owner_here)
        def share():
            for o in range(1, 4):
                src = gates.at[pl.ds(pl.multiple_of(y_of(4 - o) * PIECE, 16), PIECE)]
                send(18 + o, src, src, y_peer(o)).wait()
            send(23, gates, gates, sibling(rep, me)).start()

    def early_done():
        send(22, outs.at[:, out_half(core)], outs.at[:, out_half(core)], sibling(rep, me)).wait_send()
        theirs = outs.at[:, out_half(1 - core)]
        send(22, theirs, theirs, sibling(rep, me)).wait_recv()

        @pl.when(owner_here)
        def sent():
            send(23, gates, gates, sibling(rep, me)).wait_send()

        @pl.when(jnp.logical_not(owner_here))
        def got():
            send(23, gates, gates, sibling(rep, me)).wait_recv()

        pltpu.make_async_copy(gates, gates_out, here.at[3]).start()
        pltpu.make_async_copy(outs, outs_out, here.at[10]).start()

    def backward(at, unused):
        @pl.when(at == 1)
        def hook_a():
            core_sum()

        @pl.when(at == 3)
        def hook_b():
            mix.middle()
            mix.cross()

        @pl.when(at == 10)
        def hook_c():
            y_sum()

        @pl.when(at == 8)
        def hook_d():
            mix.near()
            mix.last()

        @pl.when(at == 13)
        def hook_e():
            side_sum()

        backward_block(
            NB - 1 - at, first_len, proj, d_normed, taps[...], shift[...], step_bias, rate_log, skip_wide,
            y, states, small, heads, carry, late,
        )
        return unused

    lax.fori_loop(0, NB, backward, 0)

    def d_in_part(block, lanes):
        begin = pl.multiple_of(HALO + block * TOK, 16)
        return mm(proj[pl.ds(begin, TOK), :HALF], w_all[0, lanes, :], ((1,), (1,))) + mm(
            proj[pl.ds(begin, TOK), HALF:], w_all[1, lanes, : CH + 128], ((1,), (1,))
        )

    mix.arrived(5, 6, 7)
    for at in range(0, MODEL, WIDE):
        lanes = slice(at, at + WIDE)
        stage[1, :, lanes] = stage[0, :, lanes] + mix.total(lanes)
    store_mixed = pltpu.make_async_copy(stage.at[1], mixed_out, here.at[5])
    store_mixed.start()
    mix.sent()
    for peer in (left, right, across):
        pl.semaphore_signal(free, inc=1, device_id=(rep, peer), device_id_type=MESH)
    pl.semaphore_wait(free, 3)
    d_in = Scatter(d_in_part, scatter_out, scatter_in, grad_send, grad_recv)
    d_in.leaf(0)
    store_mixed.wait()
    load_again = pltpu.make_async_copy(cotangent, stage.at[1], here.at[6])
    load_again.start()

    def small_copy(which):
        peer = (sibling, beside)[which](rep, me)
        return send(44 + which, packed.at[which], packed_in.at[which], peer)

    def small_first():
        small_copy(0).wait()
        packed[1] = packed[0] + packed_in[0]
        small_copy(1).start()

    def small_second():
        small_copy(1).wait()
        packed_y[along_y] = packed[1] + packed_in[1]
        for o in range(1, 4):
            send(46 + o, packed_y.at[along_y], packed_y.at[along_y], y_peer(o)).start()

    def small_third():
        for o in range(1, 4):
            src = packed_y.at[y_of(4 - o)]
            send(46 + o, src, src, y_peer(o)).wait()
        packed_all[me] = packed_y[0] + packed_y[1] + packed_y[2] + packed_y[3]
        for o in range(1, SHARDS):
            to = rep, lax.rem(me + o, SHARDS)
            send(50 + o, packed_all.at[me], packed_all.at[me], to).start()

    def small_last():
        for o in range(1, SHARDS):
            source = lax.rem(me + SHARDS - o, SHARDS)
            send(50 + o, packed_all.at[source], packed_all.at[source], (rep, source)).wait()
        pltpu.make_async_copy(packed_all, small_out, here.at[9]).start()

    def tail_tiles(which):
        def tile(at, unused):
            lanes = pl.ds(pl.multiple_of(at * 256, 256), 256)
            part = mm(x_all[:, lanes], proj[HALO:, part_columns(1 + which)], ((0,), (0,)))
            low_all[lanes, part_columns(1 + which)] = part.astype(BF)
            first = jnp.concatenate([w_all[0, lanes, CH:], w_all[1, lanes, :128]], axis=1).astype(F32)
            second = w_all[1, lanes, 128 : CH + 128].astype(F32)
            row_dots(at, part, jnp.where(which == 0, first, second))
            return unused

        lax.fori_loop(0, MODEL // 256, tile, 0)

    mine = part_columns(1 + core)
    share_gates()
    tail_tiles(1 - core)
    received = low_all.at[pl.ds(0, MODEL), part_columns(0)]
    core_copy = send(28, low_all.at[pl.ds(0, MODEL), part_columns(2 - core)], received, sibling(rep, me))
    pl.semaphore_wait(core_free, 1)
    core_copy.start()
    d_in.leaf(1)
    d_in.leaf(2)
    tail_tiles(core)
    packed[0] = jnp.zeros_like(packed[0])
    packed[0, :5, :XBC] = small[:5]
    packed[0, 5:6, :CH] = small[5:6, :CH]
    packed[0, 5:6, CH : 2 * CH] = gain_sum[...]
    packed[0, 5:6, 2 * CH : 2 * CH + 128] = heads[0:1]
    packed[0, 5:6, 2 * CH + 128 : 2 * CH + 256] = heads[1:2]
    packed[0, 6:7, :] = norm_sum[0:1, :] / norm_gain[...]
    small_copy(0).start()
    core_copy.wait()

    def add_core(at, unused):
        rows = block_rows(at)
        both = low_all[rows, mine].astype(F32) + low_all[rows, :CH].astype(F32)
        low_all[rows, mine] = both.astype(BF)
        return unused

    lax.fori_loop(0, MODEL // TOK, add_core, 0)
    for o in range(1, 4):
        for block in range(SHARDS):
            src = low_all.at[y_rows(block, y_of(o)), mine]
            send(28 + o, src, near_y.at[o - 1, pl.ds(block * PIECE, PIECE)], y_peer(o)).start()
    small_first()
    d_in.middle()
    d_in.near()
    for o in range(1, 4):
        send(28 + o, low_all.at[pl.ds(0, QUARTER), mine], near_y.at[o - 1], y_peer(o)).wait()
    for block in range(SHARDS):
        rows = slice(block * PIECE, (block + 1) * PIECE)
        total = low_all[y_rows(block, along_y), mine].astype(F32)
        for o in range(3):
            total = total + near_y[o, rows].astype(F32)
        quarter[rows] = total.astype(BF)
    side_copy = send(32, quarter, tail_swap, beside(rep, me))
    side_copy.start()
    small_second()
    to_sibling()
    side_copy.wait()
    quarter[...] = (quarter[...].astype(F32) + tail_swap[...].astype(F32)).astype(BF)
    for o in range(1, SHARDS):
        to = lax.rem(me + o, SHARDS)
        send(32 + o, quarter.at[own_quarter(to)], tail_pieces.at[me], (rep, to)).start()
    tail_pieces[me] = quarter[own_quarter(me), :]
    d_in.cross()
    d_in.last()
    small_third()
    early_done()
    for o in range(1, SHARDS):
        source = lax.rem(me + SHARDS - o, SHARDS)
        send(32 + o, quarter.at[own_quarter(source)], tail_pieces.at[source], (rep, source)).wait()

    @pl.when(core == 0)
    def assemble_first():
        total = tail_pieces[0, :, :BC].astype(F32)
        for block in range(1, SHARDS):
            total = total + tail_pieces[block, :, :BC].astype(F32)
        tail[0, own_piece, :BC] = total.astype(BF)
        for block in range(SHARDS):
            tail[0, own_piece, BC + 128 * block : BC + 128 * block + 128] = tail_pieces[block, :, BC:]

    @pl.when(core == 1)
    def assemble_second():
        total = jnp.zeros((PIECE, 128), F32)
        for block in range(SHARDS):
            tail[1, own_piece, 256 * block : 256 * block + 256] = tail_pieces[block, :, :256]
            put = (iota2((128, 128), 1) == iota2((128, 128), 0) + block * OWN) & (
                iota2((128, 128), 0) < OWN
            )
            total = total + mm(tail_pieces[block, :, 256:], put.astype(BF))
        tail[1, own_piece, 2048:] = total.astype(BF)

    def tail_piece(which, y_at):
        rows = pl.ds(pl.multiple_of(y_at * PIECE, 16), PIECE)
        return tail.at[which, rows, pl.ds(0, TAIL_WIDTH[which])]

    def tail_half(which):
        return tail.at[which, :, pl.ds(0, TAIL_WIDTH[which])]

    def each_core(act):
        for which in range(2):

            @pl.when(core == which)
            def mine_only():
                act(which)

    def spread_tail(which):
        for o in range(1, 4):
            src = tail_piece(which, along_y)
            send(40 + o, src, src, y_peer(o)).start()

    def swap_tail(which):
        for o in range(1, 4):
            src = tail_piece(which, y_of(4 - o))
            send(40 + o, src, tail_piece(which, along_y), y_peer(o)).wait()
        send(58, tail_half(which), tail_half(which), sibling(rep, me)).start()

    def end_tail(which):
        other = tail_half(1 - which)
        send(58, other, other, sibling(rep, me)).wait_recv()
        send(58, tail_half(which), tail_half(which), sibling(rep, me)).wait_send()

    each_core(spread_tail)
    for at in range(MODEL // CH):
        y[at * TOK : (at + 1) * TOK, :] = d_in.part(me, slice(at * CH, (at + 1) * CH))

    each_core(swap_tail)
    small_last()
    d_in.arrived(5, 6, 7)
    load_again.wait()
    def norm_back(at, unused):
        chunk = pl.ds(pl.multiple_of(at * CHUNK, CHUNK), CHUNK)
        rows = stage[0, chunk, :]
        pieces = [
            y[pl.ds(pl.multiple_of(k * TOK + at * CHUNK, CHUNK), CHUNK), :] for k in range(MODEL // CH)
        ]
        d_rows = jnp.concatenate(pieces, axis=1)
        for slot in (4, 5, 6):
            d_rows = d_rows + scatter_in[slot, chunk, :].astype(F32)
        scale = lax.rsqrt(jnp.mean(rows * rows, axis=1, keepdims=True) + epsilon)
        unit = rows * scale
        d_unit = d_rows * norm_gain[...]
        stage[1, chunk, :] += scale * (d_unit - unit * jnp.mean(d_unit * unit, axis=1, keepdims=True))
        return unused

    lax.fori_loop(0, TOK // CHUNK, norm_back, 0)
    store_grad = pltpu.make_async_copy(stage.at[1], grad_out, here.at[7])
    store_grad.start()

    each_core(end_tail)
    store_tail = pltpu.make_async_copy(tail, tail_out, here.at[8])
    store_tail.start()
    d_in.sent()
    gather_x.sent()
    pltpu.make_async_copy(gates, gates_out, here.at[3]).wait()
    pltpu.make_async_copy(outs, outs_out, here.at[10]).wait()
    store_grad.wait()
    store_tail.wait()
    pltpu.make_async_copy(packed_all, small_out, here.at[9]).wait()


def scale_block(b, proj, y, totals, gain, normed_out):
    r0 = pl.multiple_of(b * L, L)
    gate = proj[pl.ds(pl.multiple_of(HALO + b * L, 16), L), :CH].astype(F32)
    inv = to_column(lax.rsqrt(totals[0, pl.ds(b, 1), :] * (1.0 / INNER) + epsilon))
    inv = jnp.concatenate([inv] * (CH // 128), axis=1)
    gated = y[pl.ds(r0, L), :] * (gate * sigmoid(gate))
    normed_out[pl.ds(r0, L), :] = (gated * inv * gain).astype(BF)


def prepare_block(b, proj, y, d_normed, totals, gain, gain_sum):
    r0 = pl.multiple_of(b * L, L)
    here = pl.ds(pl.multiple_of(HALO + b * L, 16), L)
    gate = proj[here, :CH].astype(F32)
    mixer = y[pl.ds(r0, L), :]
    sig = sigmoid(gate)
    silu = gate * sig
    gated = mixer * silu
    inv = lax.rsqrt(totals[0, pl.ds(b, 1), :] * (1.0 / INNER) + epsilon)
    back = inv * inv * inv * totals[1, pl.ds(b, 1), :] * (1.0 / INNER)
    inv = jnp.concatenate([to_column(inv)] * (CH // 128), axis=1)
    back = jnp.concatenate([to_column(back)] * (CH // 128), axis=1)
    dn = d_normed[pl.ds(r0, L), :].astype(F32)
    scaled = gated * inv
    gain_sum[...] += jnp.sum(dn * scaled, axis=0, keepdims=True)
    d_gated = inv * gain * dn - gated * back
    d_normed[pl.ds(r0, L), :] = (d_gated * silu).astype(BF)
    proj[here, :CH] = (d_gated * mixer * (sig + silu * (1.0 - sig))).astype(BF)


def backward_block(
    b, first_len, proj, d_out, taps, shift, step_bias, rate_log, skip, y_in, states, small, heads,
    carry, late,
):
    upper = (iota2((L, L), 1) >= iota2((L, L), 0)).astype(BF)
    columns = head_columns()
    r0 = pl.multiple_of(b * L, L)
    rows = proj[pl.ds(r0, HALO + L), :]
    gate, xbc, conv, raw, step, log_decay, cum = block_front(
        rows, r0, first_len, taps, shift, step_bias, rate_log
    )
    sig = sigmoid(conv)
    act = conv * sig
    x = act[:, BC:]
    b_low = act[:, :STATE].astype(BF)
    c_low = act[:, STATE:BC].astype(BF)
    cum_rows = jnp.transpose(cum)
    scores = mm(c_low, b_low, ((1,), (1,)))
    step_wide = spread(step)
    scaled = x * step_wide
    scaled_low = scaled.astype(BF)
    decays = decay_weights(cum, cum_rows)

    y = y_in[pl.ds(r0, L), :]
    dy_low = d_out[pl.ds(r0, L), :]
    dy = dy_low.astype(F32)

    state = states[b]
    end_state = states[b + 1]
    d_state = carry[...]
    state_low = state.astype(BF)
    d_state_low = d_state.astype(BF)
    enter = spread(jnp.exp(cum))
    tail = spread(jnp.exp(cum[L - 1 : L] - cum))
    lane = iota2((L, 128), 1)
    d_scores = jnp.zeros((L, L), F32)
    weights = []
    for h in range(OWN):
        part = slice(128 * (h // 2), 128 * (h // 2) + 128)
        mine = (lane < HEAD_DIM) if h % 2 == 0 else (lane >= HEAD_DIM)
        d_weight = mm(
            dy_low[:, part],
            jnp.where(mine, scaled[:, part], 0.0).astype(BF),
            ((1,), (1,)),
        )
        d_scores = d_scores + d_weight * decays[h]
        weights.append((decays[h] * scores).astype(BF))
    d_scores_low = d_scores.astype(BF)
    d_scaled = pair_mix(weights, dy_low, ((0,), (0,)))
    d_scaled = d_scaled + tail * mm(b_low, d_state_low, ((1,), (1,)))
    enter_dy = (enter * dy).astype(BF)
    d_c = mm(d_scores_low, b_low) + mm(enter_dy, state_low)
    d_b = mm(d_scores_low, c_low, ((0,), (0,))) + mm((tail * scaled).astype(BF), d_state_low)

    ssm = y - skip * x
    pieces = split(dy_low.astype(F32) * ssm - scaled_low.astype(F32) * d_scaled, 2)
    pieces += split(d_scaled * x, 2)
    sums = mm(jnp.concatenate(pieces, axis=0), columns)
    d_cum = sums[:L] + sums[L : 2 * L]
    inner = end_state * d_state
    heads_lane = iota2((1, 128), 1)
    through = jnp.zeros((1, 128), F32)
    for h in range(OWN):
        total = jnp.sum(inner[HEAD_DIM * h : HEAD_DIM * h + HEAD_DIM], axis=0, keepdims=True)
        total = jnp.sum(total, axis=1, keepdims=True)
        through = through + jnp.where(heads_lane == h, total, 0.0)
    d_cum = d_cum + jnp.where(iota2((L, 1), 0) == L - 1, through, 0.0)
    d_log = mm_left(upper, d_cum, 2)
    d_step = sums[2 * L : 3 * L] + sums[3 * L :] - jnp.exp(rate_log) * d_log
    d_raw = d_step * sigmoid(raw)
    d_x = d_scaled * step_wide + skip * dy

    carry[...] = head_rows(cum_rows, L - 1) * d_state + mm(enter_dy, c_low, ((0,), (0,)))

    d_act = jnp.concatenate([d_b, d_c, d_x], axis=1)
    d_conv = d_act * (sig + act * (1.0 - sig))
    row = r0 + iota2((L + 8, 1), 0)
    longer = jnp.concatenate([d_conv, late[...]], axis=0)
    late[...] = d_conv[:8]
    d_xbc = jnp.zeros((L, XBC), F32)
    for k in range(CONV):
        ahead = CONV - 1 - k
        masked = longer
        if ahead:
            masked = longer * tap_mask(row, first_len, ahead)
        d_xbc = d_xbc + taps[k : k + 1] * masked[ahead : ahead + L]
        small[k : k + 1, :] += jnp.sum(
            masked[:L] * xbc[HALO - ahead : HALO - ahead + L], axis=0, keepdims=True
        )
    small[4:5, :] += jnp.sum(d_conv, axis=0, keepdims=True)
    small[5:6, :CH] += jnp.sum(dy * x, axis=0, keepdims=True)
    heads[0:1, :] += jnp.sum(d_raw, axis=0, keepdims=True)
    heads[1:2, :] += jnp.sum(d_log * log_decay, axis=0, keepdims=True)
    proj[pl.ds(pl.multiple_of(HALO + b * L, 16), L), CH:] = jnp.concatenate(
        [d_xbc, d_raw], axis=1
    ).astype(BF)


def finish_kernel(
    mixed_in, grad_in, gates_in, tail_in, outs_in, packed, mixed, grad, norm_grad, in_grad, conv_grad, bias_grad,
    dt_grad, rate_grad, skip_grad, gain_grad, out_grad,
    mixed_here, grad_here, gates, tail, outs, in_here, out_here, into, out,
):
    loads = [
        pltpu.make_async_copy(src, dst, into.at[at])
        for at, (src, dst) in enumerate(
            ((outs_in, outs), (gates_in, gates), (tail_in, tail), (mixed_in, mixed_here), (grad_in, grad_here))
        )
    ]
    for load in loads:
        load.start()
    stores = []

    def store(src, dst):
        stores.append(pltpu.make_async_copy(src, dst, out.at[len(stores)]))
        stores[-1].start()

    loads[0].wait()
    out_here[...] = outs[...].astype(F32)
    store(out_here, out_grad.at[0])
    loads[1].wait()
    loads[2].wait()
    for chunk in range(0, ROWS, PIECE):
        rows = slice(chunk, chunk + PIECE)
        in_here[rows, :INNER] = gates[rows, :].astype(F32)
        for s in range(SHARDS):
            begin = INNER + CH * s
            in_here[rows, begin : begin + 128] = tail[0, rows, BC + 128 * s : BC + 128 * s + 128].astype(F32)
            in_here[rows, begin + 128 : begin + CH] = tail[1, rows, 256 * s : 256 * s + 256].astype(F32)
        in_here[rows, 2 * INNER : 2 * INNER + BC] = tail[0, rows, :BC].astype(F32)
        in_here[rows, 2 * INNER + BC :] = tail[1, rows, 2048 : 2048 + HEADS].astype(F32)
        store(in_here.at[pl.ds(chunk, PIECE)], in_grad.at[0, pl.ds(chunk, PIECE)])
    loads[3].wait()
    store(mixed_here, mixed)
    loads[4].wait()
    store(grad_here, grad)
    parts = [packed[s] for s in range(SHARDS)]
    both = parts[0][:, :BC]
    for s in range(1, SHARDS):
        both = both + parts[s][:, :BC]
    conv_grad[0, :, INNER:] = both[:CONV]
    bias_grad[:, INNER:] = both[CONV : CONV + 1]
    heads = [jnp.zeros((8, 128), F32)] * 3
    for s in range(SHARDS):
        own = slice(CH * s, CH * s + CH)
        conv_grad[0, :, own] = parts[s][:CONV, BC:XBC]
        bias_grad[:, own] = parts[s][CONV : CONV + 1, BC:XBC]
        gain_grad[:, own] = parts[s][5:6, CH : 2 * CH]
        put = (iota2((128, 128), 1) == iota2((128, 128), 0) + s * OWN) & (iota2((128, 128), 0) < OWN)
        put_wide = iota2((CH, 128), 1) == iota2((CH, 128), 0) // HEAD_DIM + s * OWN
        rows = (
            (parts[s][5:6, 2 * CH : 2 * CH + 128], put),
            (parts[s][5:6, 2 * CH + 128 : 2 * CH + 256], put),
            (parts[s][5:6, :CH], put_wide),
        )
        for at, (row, to) in enumerate(rows):
            wide = jnp.broadcast_to(row, (8, row.shape[1]))
            heads[at] = heads[at] + mm_right(wide, to.astype(BF), 3)
    for at, ref in enumerate((dt_grad, rate_grad, skip_grad)):
        ref[...] = heads[at][0:1, :HEADS]
    total = parts[0][6:7]
    for s in range(1, SHARDS):
        total = total + parts[s][6:7]
    norm_grad[...] = total
    for copy in stores:
        copy.wait()


VM = pl.BlockSpec(memory_space=pltpu.VMEM)
SM = pl.BlockSpec(memory_space=pltpu.SMEM)
ANY = pl.BlockSpec(memory_space=pl.ANY)
LIMIT = 61 << 20


def local(
    resid,
    cotangent,
    first_length,
    norm_gain,
    in_weight,
    conv_weight,
    conv_bias,
    dt_bias,
    a_log,
    skip,
    gate_gain,
    out_weight,
):
    w = in_weight[0]
    narrow = jnp.pad(w[:, 2 * INNER :], ((0, 0), (0, 4 * 128 - BC - HEADS)))
    dma = pltpu.SemaphoreType.DMA
    outs = (
        ((TOK, MODEL), F32), ((TOK, MODEL), F32), ((ROWS, INNER), BF), ((2, ROWS, TAIL), BF),
        ((CH, MODEL), BF), ((SHARDS, 8, MODEL), F32),
    )
    scratch = (
        ((GROUP, MODEL), BF), ((GROUP, MODEL), BF), ((2, MODEL, HALF), BF),
        ((HALO + GROUP, COLS), BF), ((GROUP, CH), F32), ((NB + 1, CH, STATE), F32), ((GROUP, CH), BF),
        ((SHARDS, 2, NB, L), F32), ((CH, STATE), F32), ((2, TOK, MODEL), F32), ((CONV, XBC), F32),
        ((1, XBC), F32),
        ((2, NB, L), F32), ((GROUP, CH), BF), ((1, CH), F32), ((8, MODEL), F32), ((8, XBC), F32),
        ((8, 128), F32),
        ((8, XBC), F32), ((7, TOK, MODEL), BF), ((7, TOK, MODEL), BF),
        ((3, QUARTER, CH), BF), ((CH, HALF_OUT), BF), ((HALF_OUT, CH), BF), ((3, 96, HALF_OUT), BF),
        ((3, QUARTER // 2, CH), BF), ((96, HALF_OUT), BF), ((QUARTER // 2, CH), BF),
        ((96, HALF_OUT), BF), ((QUARTER // 2, CH), BF),
        ((QUARTER, CH), BF),
        ((ROWS, INNER), BF), ((CH, MODEL), BF),
        ((QUARTER, CH), BF),
        ((SHARDS, PIECE, CH), BF), ((2, ROWS, TAIL), BF),
        ((2, 8, MODEL), F32), ((2, 8, MODEL), F32), ((4, 8, MODEL), F32), ((SHARDS, 8, MODEL), F32),
    )
    mixed, grad, gates, tail, out_grad, packed = pl.pallas_call(
        layer_kernel,
        out_shape=tuple(jax.ShapeDtypeStruct(*shape) for shape in outs),
        in_specs=[SM, ANY, ANY, ANY, ANY] + [VM] * 8,
        out_specs=(ANY,) * 6,
        scratch_shapes=[pltpu.VMEM(*shape) for shape in scratch]
        + [dma((11,))] * 4 + [dma((SHARDS,))] * 2 + [dma((4,))] * 2 + [dma((1,))] * 2
        + [dma((2 * SHARDS,))] * 2 + [dma((11,))] + [dma((10,))] * 4 + [dma((60,))] * 2 + [dma((SHARDS,))] * 2
        + [pltpu.SemaphoreType.REGULAR] * 2,
        compiler_params=pltpu.CompilerParams(
            vmem_limit_bytes=LIMIT, collective_id=0, has_side_effects=True
        ),
    )(
        first_length, resid, cotangent, w, narrow, out_weight[0], norm_gain, conv_weight[0], conv_bias,
        dt_bias, a_log, skip, gate_gain,
    )
    wide = CONVCH
    shapes = (
        (TOK, MODEL), (TOK, MODEL), (1, MODEL), (1, ROWS, 2 * INNER + BC + HEADS), (1, CONV, wide), (1, wide),
        (1, HEADS), (1, HEADS), (1, HEADS), (1, INNER), (1, CH, MODEL),
    )
    return pl.pallas_call(
        finish_kernel,
        out_shape=tuple(jax.ShapeDtypeStruct(shape, F32) for shape in shapes),
        in_specs=[ANY] * 5 + [VM],
        out_specs=(ANY, ANY, VM, ANY) + (VM,) * 6 + (ANY,),
        scratch_shapes=[
            pltpu.VMEM((TOK, MODEL), F32), pltpu.VMEM((TOK, MODEL), F32), pltpu.VMEM((ROWS, INNER), BF),
            pltpu.VMEM((2, ROWS, TAIL), BF), pltpu.VMEM((CH, MODEL), BF),
            pltpu.VMEM((ROWS, 2 * INNER + BC + HEADS), F32), pltpu.VMEM((CH, MODEL), F32), dma((5,)), dma((7,)),
        ],
        compiler_params=pltpu.CompilerParams(vmem_limit_bytes=LIMIT),
    )(mixed, grad, gates, tail, out_grad, packed)


def solution(mesh):
    rows = P(("rep", "shard"), None)
    weight = P(None, "shard", None)
    return jax.shard_map(
        local,
        mesh=mesh,
        in_specs=(rows, rows, P("rep"), P(), weight, P(), P(), P(), P(), P(), P(), weight),
        out_specs=(rows, rows, P(), weight, P(), P(), P(), P(), P(), P(), weight),
        check_vma=False,
    )
```

```python
import jax
import jax.numpy as jnp
from jax import lax
from jax.experimental import pallas as pl
from jax.experimental.pallas import tpu as pltpu
from jax.sharding import PartitionSpec as P

HEADS = 48
HEAD_DIM = 64
STATE = 128
CONV = 4
INNER = 3072
CONVCH = 3328
MODEL = 1536
SHARDS = 8
OWN = HEADS // SHARDS
CH = OWN * HEAD_DIM
XBC = CH + 2 * STATE
HALF = 640
COLS = 2 * CH + 2 * STATE + 128
BC = 2 * STATE
TOK = 256
GROUP = TOK * SHARDS
L = 128
NB = GROUP // L
HALO = 16
PIECE = 48
MESH = pl.DeviceIdType.MESH
ROWS = MODEL // SHARDS
QUARTER = SHARDS * PIECE
TAIL_WIDTH = (2 * 128 + 8 * 128, 8 * 256 + 128)
TAIL = max(TAIL_WIDTH)
FRONT = 64
CHUNK = 32
HALF_OUT = MODEL // 2
WIDE = 512
OUT_PART = pl.ds(MODEL, CH)
RESET = -200.0

epsilon = 1e-05
F32 = jnp.float32
BF = jnp.bfloat16


def mm(a, b, dims=((1,), (0,))):
    return lax.dot_general(a, b, (dims, ((), ())), preferred_element_type=F32)


def split(v, parts):
    out = []
    for _ in range(parts):
        piece = v.astype(BF)
        out.append(piece)
        v = v - piece.astype(F32)
    return out


def mm_left(ones, v, parts):
    return sum(mm(ones, piece) for piece in split(v, parts))


def mm_right(v, ones, parts):
    return sum(mm(piece, ones) for piece in split(v, parts))


def iota2(shape, dim):
    return lax.broadcasted_iota(jnp.int32, shape, dim)


def head_columns():
    return (iota2((CH, 128), 0) // HEAD_DIM == iota2((CH, 128), 1)).astype(BF)


def spread(per_head):
    lane = iota2((per_head.shape[0], 128), 1)
    tiles = []
    for pair in range(OWN // 2):
        left = per_head[:, 2 * pair : 2 * pair + 1]
        right = per_head[:, 2 * pair + 1 : 2 * pair + 2]
        tiles.append(jnp.where(lane < HEAD_DIM, left, right))
    return jnp.concatenate(tiles, axis=1)


def head_rows(cum_rows, at):
    pieces = [
        jnp.broadcast_to(cum_rows[h : h + 1, at : at + 1], (HEAD_DIM, 1)) for h in range(OWN)
    ]
    return jnp.exp(jnp.concatenate(pieces, axis=0))


def tap_mask(row, first_len, back):
    past = row - first_len
    return jnp.where((past >= 0) & (past < back), 0.0, 1.0)


def block_front(rows, r0, first_len, taps, shift, step_bias, rate_log):
    xbc = rows[:, CH : CH + XBC].astype(F32)
    row = r0 + iota2((L, 1), 0)
    conv = jnp.broadcast_to(shift, (L, XBC))
    for k in range(CONV):
        back = CONV - 1 - k
        term = taps[k : k + 1] * xbc[HALO - back : HALO - back + L]
        if back:
            term = term * tap_mask(row, first_len, back)
        conv = conv + term
    gate = rows[HALO:, :CH].astype(F32)
    raw = rows[HALO:, CH + XBC :].astype(F32) + step_bias
    step = jnp.maximum(raw, 0.0) + jnp.log1p(jnp.exp(-jnp.abs(raw)))
    log_decay = -step * jnp.exp(rate_log)
    with_reset = log_decay + jnp.where(row == first_len, RESET, 0.0)
    lower = (iota2((L, L), 0) >= iota2((L, L), 1)).astype(BF)
    cum = mm_left(lower, with_reset, 3)
    return gate, xbc, conv, raw, step, log_decay, cum


def sigmoid(v):
    return 0.5 * jnp.tanh(0.5 * v) + 0.5


def pair_mix(weights, value, dims=((1,), (0,))):
    lane = iota2((L, 128), 1)
    tiles = []
    for pair in range(OWN // 2):
        part = value[:, 128 * pair : 128 * pair + 128]
        tiles.append(
            jnp.where(
                lane < HEAD_DIM,
                mm(weights[2 * pair], part, dims),
                mm(weights[2 * pair + 1], part, dims),
            )
        )
    return jnp.concatenate(tiles, axis=1)


def decay_weights(cum, cum_rows):
    causal = iota2((L, L), 0) >= iota2((L, L), 1)
    out = []
    for h in range(OWN):
        gap = cum[:, h : h + 1] - cum_rows[h : h + 1, :]
        out.append(jnp.exp(jnp.where(causal, gap, -1e30)))
    return out


def to_row(column):
    return jnp.transpose(jnp.broadcast_to(column, (L, L)))[0:1]


def to_column(row):
    return jnp.transpose(jnp.broadcast_to(row, (L, L)))


def forward_block(b, first_len, proj, taps, shift, step_bias, rate_log, skip, y_out, states, sums, carry):
    r0 = pl.multiple_of(b * L, L)
    rows = proj[pl.ds(r0, HALO + L), :]
    gate, xbc, conv, raw, step, log_decay, cum = block_front(
        rows, r0, first_len, taps, shift, step_bias, rate_log
    )
    act = conv * sigmoid(conv)
    x = act[:, BC:]
    b_low = act[:, :STATE].astype(BF)
    c_low = act[:, STATE:BC].astype(BF)
    cum_rows = jnp.transpose(cum)
    scores = mm(c_low, b_low, ((1,), (1,)))
    scaled = x * spread(step)
    scaled_low = scaled.astype(BF)
    weights = [(w * scores).astype(BF) for w in decay_weights(cum, cum_rows)]
    state = carry[...]
    states[b] = state
    y = pair_mix(weights, scaled_low)
    y = y + spread(jnp.exp(cum)) * mm(c_low, state.astype(BF), ((1,), (1,)))
    tail = spread(jnp.exp(cum[L - 1 : L] - cum))
    carry[...] = head_rows(cum_rows, L - 1) * state + mm(
        (tail * scaled).astype(BF), b_low, ((0,), (0,))
    )
    y = y + skip * x
    y_out[pl.ds(r0, L), :] = y
    gated = y * (gate * sigmoid(gate))
    sums[pl.ds(b, 1), :] = to_row(jnp.sum(gated * gated, axis=1, keepdims=True))


def place_of():
    rep, me = lax.axis_index("rep"), lax.axis_index("shard")
    hi, z = me // 4, lax.rem(me, 4)
    left = hi * 4 + lax.rem(z + 3, 4)
    right = hi * 4 + lax.rem(z + 1, 4)
    far = hi * 4 + lax.rem(z + 2, 4)
    across = lax.rem(me + 4, 8)
    return rep, me, left, right, far, across


def sibling(rep, me):
    return rep + 1 - 2 * lax.rem(rep, 2), me


def beside(rep, me):
    return rep + 2 - 4 * lax.rem(rep // 2, 2), me


def other_side(block):
    return lax.rem(block + 4, 8)


def enter(rep, me):
    barrier = pltpu.get_barrier_semaphore()
    peers = [(rep, lax.rem(me + o, SHARDS)) for o in range(1, SHARDS)]
    peers += [(lax.rem(rep + 4 * o, 16), me) for o in range(1, 4)]
    peers += [sibling(rep, me), beside(rep, me)]
    for peer in peers:
        pl.semaphore_signal(barrier, inc=1, device_id=peer, device_id_type=MESH)
    return lambda: pl.semaphore_wait(barrier, len(peers))


def block_rows(block, part=(0, TOK)):
    begin, end = part
    return pl.ds(pl.multiple_of(block * TOK + begin, 16), end - begin)


FIRST, SECOND = (0, TOK // 2), (TOK // 2, TOK)
EDGE = 48
TOP, REST = (0, EDGE), (EDGE, TOK)


class Gather:
    def __init__(self, blocks, send, recv):
        self.blocks, self.send, self.recv = blocks, send, recv
        self.rep, self.me, self.left, self.right, self.far, self.across = place_of()

    def move(self, channel, block, to, rows=(0, TOK)):
        ref = self.blocks.at[block_rows(block, rows)]
        return pltpu.make_async_remote_copy(
            src_ref=ref,
            dst_ref=ref,
            send_sem=self.send.at[channel],
            recv_sem=self.recv.at[channel],
            device_id=(self.rep, to),
            device_id_type=MESH,
        )

    def outgoing(self, channel):
        me, left, right, across = self.me, self.left, self.right, self.across
        return (
            lambda: self.move(0, me, right),
            lambda: self.move(1, me, left),
            lambda: self.move(2, me, across),
            lambda: self.move(3, left, right, FIRST),
            lambda: self.move(4, right, left, SECOND),
            lambda: self.move(5, across, right, REST),
            lambda: self.move(6, across, left, REST),
            lambda: self.move(7, self.far, across, FIRST),
            lambda: self.move(8, self.far, across, SECOND),
            lambda: self.move(9, left, across, TOP),
            lambda: self.move(10, right, across, TOP),
        )[channel]()

    def incoming(self, channel):
        left, right, far, across = self.left, self.right, self.far, self.across
        return (
            lambda: self.move(0, left, left),
            lambda: self.move(1, right, right),
            lambda: self.move(2, across, across),
            lambda: self.move(3, far, left, FIRST),
            lambda: self.move(4, far, right, SECOND),
            lambda: self.move(5, other_side(left), left, REST),
            lambda: self.move(6, other_side(right), right, REST),
            lambda: self.move(7, other_side(far), across, FIRST),
            lambda: self.move(8, other_side(far), across, SECOND),
            lambda: self.move(9, other_side(left), across, TOP),
            lambda: self.move(10, other_side(right), across, TOP),
        )[channel]()

    def start(self, *channels):
        for channel in channels:
            self.outgoing(channel).start()

    def arrived(self, *channels):
        for channel in channels:
            self.incoming(channel).wait_recv()

    def sent(self):
        for channel in range(11):
            self.outgoing(channel).wait_send()


class Scatter:
    SLOTS = (
        (0, (0, TOK)), (1, REST), (2, REST), (3, FIRST), (3, SECOND), (4, (0, TOK)), (5, (0, TOK)),
        (6, (0, TOK)), (1, TOP), (2, TOP),
    )

    def __init__(self, part, out, into, send, recv):
        self.part, self.out, self.into, self.send, self.recv = part, out, into, send, recv
        self.rep, self.me, self.left, self.right, self.far, self.across = place_of()
        self.to = (
            self.across, self.left, self.right, self.left, self.right, self.right, self.left, self.across,
            self.across, self.across,
        )

    def copy(self, channel):
        slot, rows = self.SLOTS[channel]
        at = (slot, pl.ds(rows[0], rows[1] - rows[0]))
        return pltpu.make_async_remote_copy(
            src_ref=self.out.at[at],
            dst_ref=self.into.at[at],
            send_sem=self.send.at[channel],
            recv_sem=self.recv.at[channel],
            device_id=(self.rep, self.to[channel]),
            device_id_type=MESH,
        )

    def arrived(self, *channels):
        for channel in channels:
            self.copy(channel).wait_recv()

    def fill(self, slot, block, *arrived):
        for at in range(0, MODEL, WIDE):
            lanes = slice(at, at + WIDE)
            value = self.part(block, lanes)
            for other in arrived:
                value = value + self.into[other, :, lanes].astype(F32)
            self.out[slot, :, lanes] = value.astype(BF)

    def add(self, slot, into, rows):
        rows = slice(*rows)
        value = self.out[slot, rows].astype(F32)
        for other in into:
            value = value + self.into[other, rows].astype(F32)
        self.out[slot, rows] = value.astype(BF)

    def leaf(self, slot):
        self.fill(slot, other_side((self.far, self.left, self.right)[slot]))
        self.copy(slot).start()
        if slot:
            self.copy(7 + slot).start()

    def middle(self):
        self.arrived(0)
        self.fill(3, self.far, 0)
        self.copy(3).start()
        self.copy(4).start()
        self.fill(6, self.across)
        self.arrived(1, 2)
        self.add(6, (1, 2), REST)

    def cross(self):
        self.copy(7).start()

    def near(self):
        self.fill(4, self.right)
        self.fill(5, self.left)

    def last(self):
        self.arrived(8, 9)
        self.add(4, (2,), TOP)
        self.add(5, (1,), TOP)
        self.arrived(3, 4)
        self.add(4, (3,), SECOND)
        self.copy(5).start()
        self.add(5, (3,), FIRST)
        self.copy(6).start()

    def total(self, lanes):
        value = self.part(self.me, lanes)
        for slot in (4, 5, 6):
            value = value + self.into[slot, :, lanes].astype(F32)
        return value

    def sent(self):
        for channel in range(10):
            self.copy(channel).wait_send()


def own_heads(vector, me):
    pick = (iota2((HEADS, 128), 0) == iota2((HEADS, 128), 1) + me * OWN) & (
        iota2((HEADS, 128), 1) < OWN
    )
    wide = jnp.broadcast_to(vector, (8, HEADS))
    return mm_right(wide, pick.astype(BF), 3)[0:1]


def own_channels(vector, me):
    pick = iota2((HEADS, CH), 0) == iota2((HEADS, CH), 1) // HEAD_DIM + me * OWN
    wide = jnp.broadcast_to(vector, (8, HEADS))
    return mm_right(wide, pick.astype(BF), 3)[0:1]


def own_slices(me, conv_weight, conv_bias):
    own = pl.ds(pl.multiple_of(me * CH, 128), CH)
    taps = jnp.concatenate([conv_weight[:, INNER:], conv_weight[:, own]], axis=1)
    shift = jnp.concatenate([conv_bias[:, INNER:], conv_bias[:, own]], axis=1)
    return taps, shift


def layer_kernel(
    first_ref, resid, cotangent, w_in, narrow, w_out, norm_gain, conv_weight, conv_bias, dt_bias,
    a_log, skip, gate_gain,
    mixed_out, grad_out, gates_out, tail_out, outs_out, small_out,
    x_all, low_all, w_all, proj, y, states, d_normed, sums, carry, stage, taps, shift,
    totals, normed_out, gain_sum, norm_sum, small, heads, late, scatter_out, scatter_in,
    near_y, core_out, core_gate, near_out, near_gate, part_out, part_gate, side_out, side_gate,
    quarter, gates, outs,
    tail_swap, tail_pieces, tail,
    packed, packed_in, packed_y, packed_all,
    x_send, x_recv, low_send, low_recv, piece_send, piece_recv, y_send, y_recv, core_send, core_recv,
    sum_send, sum_recv, here, mix_send, mix_recv, grad_send, grad_recv, g_send, g_recv, owner_send, owner_recv, free, core_free,
):
    rep, me, left, right, far, across = place_of()
    core = lax.rem(rep, 2)
    along_y = rep // 4
    first_len = first_ref[0]
    load_resid = pltpu.make_async_copy(resid, stage.at[0], here.at[0])
    load_cot = pltpu.make_async_copy(cotangent, stage.at[1], here.at[1])
    load_resid.start()
    load_cot.start()
    all_entered = enter(rep, me)

    load_resid.wait()

    def norm_rows(at, unused):
        rows = stage[0, pl.ds(pl.multiple_of(at * FRONT, FRONT), FRONT), :]
        scale = lax.rsqrt(jnp.mean(rows * rows, axis=1, keepdims=True) + epsilon)
        own = pl.ds(pl.multiple_of(me * TOK + at * FRONT, FRONT), FRONT)
        x_all[own, :] = (rows * scale * norm_gain[...]).astype(BF)
        return unused

    lax.fori_loop(0, TOK // FRONT, norm_rows, 0)
    all_entered()
    gather_x = Gather(x_all, x_send, x_recv)
    gather_x.start(0, 1, 2)

    own_rows = pl.ds(pl.multiple_of(along_y * PIECE, 16), PIECE)

    def landing(block):
        return pl.ds(pl.multiple_of(block * 192 + along_y * PIECE, 16), PIECE)

    def weight_pieces(to, make):
        wide = pl.ds(pl.multiple_of(core * INNER + to * CH, 128), CH)
        half = pl.ds(pl.multiple_of(core * BC, 128), BC)
        make(w_in.at[own_rows, wide], w_all.at[core, landing(me), pl.ds(0, CH)])
        make(narrow.at[own_rows, half], w_all.at[core, landing(me), pl.ds(CH, BC)])

    for o in range(1, SHARDS):
        to = lax.rem(me + o, SHARDS)
        weight_pieces(
            to,
            lambda src, dst: pltpu.make_async_remote_copy(
                src_ref=src, dst_ref=dst, send_sem=piece_send.at[o], recv_sem=piece_recv.at[o],
                device_id=(rep, to), device_id_type=MESH,
            ).start(),
        )
    weight_pieces(me, lambda src, dst: pltpu.make_async_copy(src, dst, here.at[2]).start())

    load_cot.wait()
    low_all[block_rows(me), :] = stage[1].astype(BF)
    gather_low = Gather(low_all, low_send, low_recv)

    taps_now, shift_now = own_slices(me, conv_weight, conv_bias)
    taps[...] = taps_now
    shift[...] = shift_now
    proj[pl.ds(0, HALO), :] = jnp.zeros((HALO, COLS), BF)
    carry[...] = jnp.zeros_like(carry)

    pltpu.make_async_copy(
        w_all.at[core, landing(me)], w_all.at[core, landing(me)], here.at[2]
    ).wait()
    for o in range(1, SHARDS):
        source = lax.rem(me + SHARDS - o, SHARDS)
        piece = w_all.at[core, landing(source)]
        pltpu.make_async_remote_copy(
            src_ref=piece, dst_ref=piece, send_sem=piece_send.at[o], recv_sem=piece_recv.at[o],
            device_id=(rep, source), device_id_type=MESH,
        ).wait()
    for o in range(1, 4):
        for block in range(SHARDS):
            piece = w_all.at[core, landing(block)]
            pltpu.make_async_remote_copy(
                src_ref=piece, dst_ref=piece, send_sem=y_send.at[o], recv_sem=y_recv.at[o],
                device_id=(lax.rem(rep + 4 * o, 16), me), device_id_type=MESH,
            ).start()
    gather_x.arrived(0)
    gather_x.start(3, 9)
    gather_x.arrived(1)
    gather_x.start(4, 10)
    gather_x.arrived(2)
    gather_x.start(5, 6)
    gather_x.arrived(3)
    gather_x.start(7)
    gather_x.arrived(4)
    gather_x.start(8)
    gather_low.start(0, 1, 2)
    for o in range(1, 4):
        landed = w_all.at[core, pl.ds(0, QUARTER)]
        pltpu.make_async_remote_copy(
            src_ref=landed, dst_ref=landed, send_sem=y_send.at[o], recv_sem=y_recv.at[o],
            device_id=(lax.rem(rep + 4 * o, 16), me), device_id_type=MESH,
        ).wait()

    def halves(which):
        return pltpu.make_async_remote_copy(
            src_ref=w_all.at[which], dst_ref=w_all.at[which], send_sem=core_send.at[0],
            recv_sem=core_recv.at[0], device_id=(rep + 1 - 2 * core, me), device_id_type=MESH,
        )

    halves(core).start()
    halves(1 - core).wait_recv()
    halves(core).wait_send()
    pick = (iota2((128, 128), 0) == iota2((128, 128), 1) + me * OWN) & (iota2((128, 128), 1) < OWN)
    w_all[1, :, CH : CH + 128] = mm(w_all[1, :, CH : CH + 128], pick.astype(BF)).astype(BF)

    side = (me // 4) * 4

    def project(at, unused):
        rows = x_all[block_rows(at), :]
        begin = pl.multiple_of(HALO + at * TOK, 16)
        proj[pl.ds(begin, TOK), :HALF] = mm(rows, w_all[0]).astype(BF)
        proj[pl.ds(begin, TOK), HALF:] = mm(rows, w_all[1, :, : CH + 128]).astype(BF)
        return unused

    lax.fori_loop(side, side + 4, project, 0)
    gather_low.arrived(0)
    gather_low.start(3, 9)
    gather_low.arrived(1)
    gather_low.start(4, 10)
    gather_x.arrived(5, 6, 7, 8, 9, 10)
    lax.fori_loop(4 - side, 8 - side, project, 0)

    step_bias = own_heads(dt_bias[...], me)
    rate_log = own_heads(a_log[...], me)
    skip_wide = own_channels(skip[...], me)

    def scan(b, unused):
        @pl.when(b == 6)
        def relay():
            gather_low.arrived(3, 4, 2)
            gather_low.start(7, 8, 5, 6)

        forward_block(
            b, first_len, proj, taps[...], shift[...], step_bias, rate_log, skip_wide, y, states,
            sums.at[me, 0], carry,
        )
        return unused

    lax.fori_loop(0, NB, scan, 0)
    states[NB] = carry[...]

    gain = gate_gain[:, pl.ds(pl.multiple_of(me * CH, 128), CH)]

    def normed(at, unused):
        begin = pl.multiple_of(at * TOK, TOK)
        dn = mm(low_all[block_rows(at), :], w_out[...], ((1,), (1,)))
        d_normed[pl.ds(begin, TOK), :] = dn.astype(BF)
        gate = proj[pl.ds(HALO + begin, TOK), :CH].astype(F32)
        gated = y[pl.ds(begin, TOK), :] * (gate * sigmoid(gate))
        both = jnp.sum(gated * gain * dn, axis=1, keepdims=True)
        sums[me, 1, pl.ds(2 * at, 1), :] = to_row(both[:L])
        sums[me, 1, pl.ds(2 * at + 1, 1), :] = to_row(both[L:])
        return unused

    def sum_copy(kind, o, slot, to):
        ref = sums.at[slot, kind]
        return pltpu.make_async_remote_copy(
            src_ref=ref, dst_ref=ref, send_sem=sum_send.at[SHARDS * kind + o],
            recv_sem=sum_recv.at[SHARDS * kind + o], device_id=(rep, to), device_id_type=MESH,
        )

    def start_sum(kind):
        for o in range(1, SHARDS):
            sum_copy(kind, o, me, lax.rem(me + o, SHARDS)).start()

    def end_sum(kind):
        for o in range(1, SHARDS):
            source = lax.rem(me + SHARDS - o, SHARDS)
            sum_copy(kind, o, source, source).wait_recv()
        total = sums[0, kind]
        for slot in range(1, SHARDS):
            total = total + sums[slot, kind]
        totals[kind] = total
        for o in range(1, SHARDS):
            sum_copy(kind, o, me, lax.rem(me + o, SHARDS)).wait_send()

    def scale_out(b, unused):
        scale_block(b, proj, y, totals, gain, normed_out)
        return unused

    def mixed_part(block, lanes):
        return mm(normed_out[block_rows(block), :], w_out[:, lanes])

    mix = Scatter(mixed_part, scatter_out, scatter_in, mix_send, mix_recv)
    start_sum(0)
    lax.fori_loop(side, side + 4, normed, 0)
    end_sum(0)
    lax.fori_loop(0, NB, scale_out, 0)
    gather_low.arrived(5, 6, 9, 10)

    def normed_near(at, unused):
        return normed(other_side(side + lax.rem(me + at, 4)), unused)

    lax.fori_loop(3, 6, normed_near, 0)
    gather_low.arrived(7, 8)
    lax.fori_loop(6, 7, normed_near, 0)
    start_sum(1)

    def send(index, src, dst, to):
        return pltpu.make_async_remote_copy(
            src_ref=src, dst_ref=dst, send_sem=g_send.at[index], recv_sem=g_recv.at[index],
            device_id=to, device_id_type=MESH,
        )

    def y_peer(o):
        return lax.rem(rep + 4 * o, 16), me

    def y_of(o):
        return lax.rem(along_y + o, 4)

    gain_sum[...] = jnp.zeros_like(gain_sum)
    small[...] = jnp.zeros_like(small)
    heads[...] = jnp.zeros_like(heads)
    late[...] = jnp.zeros_like(late)
    carry[...] = jnp.zeros_like(carry)

    def prepare(b, unused):
        prepare_block(b, proj, y, d_normed, totals, gain, gain_sum)
        return unused

    for slot in range(3):
        mix.leaf(slot)
    gather_low.sent()
    def row_dots(at, part, weight):
        dots = jnp.sum(part * weight.astype(F32), axis=1, keepdims=True)
        for half in range(2):
            lanes = pl.ds(pl.multiple_of(at * 256 + half * L, L), L)
            norm_sum[0:1, lanes] += to_row(dots[half * L : half * L + L])

    norm_sum[...] = jnp.zeros_like(norm_sum)

    def out_tile(at, unused):
        lanes = pl.ds(pl.multiple_of(at * 256, 256), 256)
        low = low_all[:, lanes]
        low_all[OUT_PART, lanes] = mm(normed_out[...], low, ((0,), (0,))).astype(BF)
        return unused

    def gate_tile(at, unused):
        lanes = pl.ds(pl.multiple_of(at * 256, 256), 256)
        rows = x_all[:, lanes]
        part = mm(rows, proj[HALO:, :CH], ((0,), (0,)))
        low_all[lanes, :CH] = part.astype(BF)
        row_dots(at, part, w_all[0, lanes, :CH])
        return unused

    def y_rows(block, y_at):
        return pl.ds(pl.multiple_of(block * ROWS + y_at * PIECE, 16), PIECE)

    def out_rows(y_at, base=0):
        return pl.ds(pl.multiple_of(base + y_at * 96, 16), 96)

    def part_columns(which):
        return pl.ds(pl.multiple_of(which * CH, 128), CH)

    def out_half(which):
        return pl.ds(pl.multiple_of(which * HALF_OUT, 128), HALF_OUT)

    def gate_half(which):
        return pl.ds(pl.multiple_of(which * HALF_OUT, 128), HALF_OUT)

    core_copies = (
        send(1, low_all.at[OUT_PART, out_half(1 - core)], core_out, sibling(rep, me)),
        send(2, low_all.at[gate_half(1 - core), pl.ds(0, CH)], core_gate, sibling(rep, me)),
    )
    lax.fori_loop(0, MODEL // 256, out_tile, 0)
    core_copies[0].start()
    end_sum(1)
    lax.fori_loop(0, NB, prepare, 0)
    lax.fori_loop(0, MODEL // 256, gate_tile, 0)
    core_copies[1].start()

    def gate_piece(block, y_at):
        return pl.ds(pl.multiple_of(core * HALF_OUT + block * ROWS + y_at * PIECE, 16), PIECE)

    def out_to_y(o):
        src = low_all.at[out_rows(y_of(o), MODEL), out_half(core)]
        return send(2 + o, src, near_out.at[o - 1], y_peer(o))

    def gate_to_y(o, block):
        dst = near_gate.at[o - 1, pl.ds(block * PIECE, PIECE)]
        return send(5 + o, low_all.at[gate_piece(block, y_of(o)), pl.ds(0, CH)], dst, y_peer(o))

    def core_sum():
        for copy in core_copies:
            copy.wait()
        mine = out_half(core)
        both = low_all[OUT_PART, mine].astype(F32) + core_out[...].astype(F32)
        low_all[OUT_PART, mine] = both.astype(BF)
        both = low_all[gate_half(core), :CH].astype(F32) + core_gate[...].astype(F32)
        low_all[gate_half(core), :CH] = both.astype(BF)
        for o in range(1, 4):
            out_to_y(o).start()
            for block in range(SHARDS // 2):
                gate_to_y(o, block).start()

    side_copies = (
        send(9, part_gate, side_gate, beside(rep, me)),
        send(10, part_out, side_out, beside(rep, me)),
    )

    def y_sum():
        for o in range(1, 4):
            out_to_y(o).wait()
            landed = low_all.at[pl.ds(0, HALF_OUT // 4), pl.ds(0, CH)]
            send(5 + o, landed, near_gate.at[o - 1], y_peer(o)).wait()
        total = low_all[out_rows(along_y, MODEL), out_half(core)].astype(F32)
        for o in range(3):
            total = total + near_out[o].astype(F32)
        part_out[...] = total.astype(BF)
        for block in range(SHARDS // 2):
            rows = slice(block * PIECE, (block + 1) * PIECE)
            total = low_all[gate_piece(block, along_y), :CH].astype(F32)
            for o in range(3):
                total = total + near_gate[o, rows].astype(F32)
            part_gate[rows] = total.astype(BF)
        for copy in side_copies:
            copy.start()
        pl.semaphore_signal(
            core_free, inc=1, device_id=sibling(rep, me), device_id_type=MESH
        )

    own_piece = pl.ds(pl.multiple_of(along_y * PIECE, 16), PIECE)

    def gate_columns(block):
        return pl.ds(pl.multiple_of(block * CH, 128), CH)

    def own_quarter(block):
        return pl.ds(pl.multiple_of(block * PIECE, 16), PIECE)

    owner_here = core == me // 4

    def from_shard(o):
        source = lax.rem(me + SHARDS - o, SHARDS)
        dst = gates.at[own_piece, gate_columns(source)]
        return pltpu.make_async_remote_copy(
            src_ref=dst, dst_ref=dst, send_sem=owner_send.at[me], recv_sem=owner_recv.at[source],
            device_id=(rep, source), device_id_type=MESH,
        )

    def owner_copy(block):
        to = core * (SHARDS // 2) + block
        return pltpu.make_async_remote_copy(
            src_ref=part_gate.at[pl.ds(block * PIECE, PIECE)], dst_ref=gates.at[own_piece, gate_columns(me)],
            send_sem=owner_send.at[block], recv_sem=owner_recv.at[me], device_id=(rep, to),
            device_id_type=MESH,
        )

    def each_owner(act):
        for block in range(SHARDS // 2):

            @pl.when(core * (SHARDS // 2) + block != me)
            def other():
                act(owner_copy(block))

    def own_outs(y_at):
        return outs.at[out_rows(y_at), out_half(core)]

    def side_sum():
        for copy in side_copies:
            copy.wait()
        part_gate[...] = (part_gate[...].astype(F32) + side_gate[...].astype(F32)).astype(BF)
        total = part_out[...].astype(F32) + side_out[...].astype(F32)
        outs[out_rows(along_y), out_half(core)] = total.astype(BF)
        each_owner(lambda copy: copy.start())

        @pl.when(owner_here)
        def keep():
            own = pl.ds(pl.multiple_of(lax.rem(me, 4) * PIECE, 16), PIECE)
            gates[own_piece, gate_columns(me)] = part_gate[own, :]

        for o in range(1, 4):
            send(14 + o, own_outs(along_y), own_outs(along_y), y_peer(o)).start()

    def share_gates():
        each_owner(lambda copy: copy.wait_send())

        @pl.when(owner_here)
        def collect():
            for o in range(1, SHARDS):
                from_shard(o).wait_recv()
            for o in range(1, 4):
                src = gates.at[own_piece]
                send(18 + o, src, src, y_peer(o)).start()

    def to_sibling():
        for o in range(1, 4):
            src = own_outs(y_of(4 - o))
            send(14 + o, src, src, y_peer(o)).wait()
        send(22, outs.at[:, out_half(core)], outs.at[:, out_half(core)], sibling(rep, me)).start()

        @pl.when(owner_here)
        def share():
            for o in range(1, 4):
                src = gates.at[pl.ds(pl.multiple_of(y_of(4 - o) * PIECE, 16), PIECE)]
                send(18 + o, src, src, y_peer(o)).wait()
            send(23, gates, gates, sibling(rep, me)).start()

    def early_done():
        send(22, outs.at[:, out_half(core)], outs.at[:, out_half(core)], sibling(rep, me)).wait_send()
        theirs = outs.at[:, out_half(1 - core)]
        send(22, theirs, theirs, sibling(rep, me)).wait_recv()

        @pl.when(owner_here)
        def sent():
            send(23, gates, gates, sibling(rep, me)).wait_send()

        @pl.when(jnp.logical_not(owner_here))
        def got():
            send(23, gates, gates, sibling(rep, me)).wait_recv()

        pltpu.make_async_copy(gates, gates_out, here.at[3]).start()
        pltpu.make_async_copy(outs, outs_out, here.at[10]).start()

    def backward(at, unused):
        @pl.when(at == 1)
        def hook_a():
            core_sum()

        @pl.when(at == 3)
        def hook_b():
            mix.middle()
            mix.cross()

        @pl.when(at == 10)
        def hook_c():
            y_sum()

        @pl.when(at == 8)
        def hook_d():
            mix.near()
            mix.last()

        @pl.when(at == 13)
        def hook_e():
            side_sum()

        backward_block(
            NB - 1 - at, first_len, proj, d_normed, taps[...], shift[...], step_bias, rate_log, skip_wide,
            y, states, small, heads, carry, late,
        )
        return unused

    lax.fori_loop(0, NB, backward, 0)

    def d_in_part(block, lanes):
        begin = pl.multiple_of(HALO + block * TOK, 16)
        return mm(proj[pl.ds(begin, TOK), :HALF], w_all[0, lanes, :], ((1,), (1,))) + mm(
            proj[pl.ds(begin, TOK), HALF:], w_all[1, lanes, : CH + 128], ((1,), (1,))
        )

    mix.arrived(5, 6, 7)
    for at in range(0, MODEL, WIDE):
        lanes = slice(at, at + WIDE)
        stage[1, :, lanes] = stage[0, :, lanes] + mix.total(lanes)
    store_mixed = pltpu.make_async_copy(stage.at[1], mixed_out, here.at[5])
    store_mixed.start()
    mix.sent()
    for peer in (left, right, across):
        pl.semaphore_signal(free, inc=1, device_id=(rep, peer), device_id_type=MESH)
    pl.semaphore_wait(free, 3)
    d_in = Scatter(d_in_part, scatter_out, scatter_in, grad_send, grad_recv)
    for slot in range(3):
        d_in.leaf(slot)
    store_mixed.wait()
    load_again = pltpu.make_async_copy(cotangent, stage.at[1], here.at[6])
    load_again.start()

    def small_copy(which):
        peer = (sibling, beside)[which](rep, me)
        return send(44 + which, packed.at[which], packed_in.at[which], peer)

    def small_first():
        small_copy(0).wait()
        packed[1] = packed[0] + packed_in[0]
        small_copy(1).start()

    def small_second():
        small_copy(1).wait()
        packed_y[along_y] = packed[1] + packed_in[1]
        for o in range(1, 4):
            send(46 + o, packed_y.at[along_y], packed_y.at[along_y], y_peer(o)).start()

    def small_third():
        for o in range(1, 4):
            src = packed_y.at[y_of(4 - o)]
            send(46 + o, src, src, y_peer(o)).wait()
        packed_all[me] = packed_y[0] + packed_y[1] + packed_y[2] + packed_y[3]
        for o in range(1, SHARDS):
            to = rep, lax.rem(me + o, SHARDS)
            send(50 + o, packed_all.at[me], packed_all.at[me], to).start()

    def small_last():
        for o in range(1, SHARDS):
            source = lax.rem(me + SHARDS - o, SHARDS)
            send(50 + o, packed_all.at[source], packed_all.at[source], (rep, source)).wait()
        pltpu.make_async_copy(packed_all, small_out, here.at[9]).start()

    def tail_tiles(which):
        def tile(at, unused):
            lanes = pl.ds(pl.multiple_of(at * 256, 256), 256)
            part = mm(x_all[:, lanes], proj[HALO:, part_columns(1 + which)], ((0,), (0,)))
            low_all[lanes, part_columns(1 + which)] = part.astype(BF)
            first = jnp.concatenate([w_all[0, lanes, CH:], w_all[1, lanes, :128]], axis=1).astype(F32)
            second = w_all[1, lanes, 128 : CH + 128].astype(F32)
            row_dots(at, part, jnp.where(which == 0, first, second))
            return unused

        lax.fori_loop(0, MODEL // 256, tile, 0)

    mine = part_columns(1 + core)
    share_gates()
    tail_tiles(1 - core)
    received = low_all.at[pl.ds(0, MODEL), part_columns(0)]
    core_copy = send(28, low_all.at[pl.ds(0, MODEL), part_columns(2 - core)], received, sibling(rep, me))
    pl.semaphore_wait(core_free, 1)
    core_copy.start()
    tail_tiles(core)
    packed[0] = jnp.zeros_like(packed[0])
    packed[0, :5, :XBC] = small[:5]
    packed[0, 5:6, :CH] = small[5:6, :CH]
    packed[0, 5:6, CH : 2 * CH] = gain_sum[...]
    packed[0, 5:6, 2 * CH : 2 * CH + 128] = heads[0:1]
    packed[0, 5:6, 2 * CH + 128 : 2 * CH + 256] = heads[1:2]
    packed[0, 6:7, :] = norm_sum[0:1, :] / norm_gain[...]
    small_copy(0).start()
    core_copy.wait()

    def add_core(at, unused):
        rows = block_rows(at)
        both = low_all[rows, mine].astype(F32) + low_all[rows, :CH].astype(F32)
        low_all[rows, mine] = both.astype(BF)
        return unused

    lax.fori_loop(0, MODEL // TOK, add_core, 0)
    for o in range(1, 4):
        for block in range(SHARDS):
            src = low_all.at[y_rows(block, y_of(o)), mine]
            send(28 + o, src, near_y.at[o - 1, pl.ds(block * PIECE, PIECE)], y_peer(o)).start()
    small_first()
    d_in.middle()
    d_in.near()
    for o in range(1, 4):
        send(28 + o, low_all.at[pl.ds(0, QUARTER), mine], near_y.at[o - 1], y_peer(o)).wait()
    for block in range(SHARDS):
        rows = slice(block * PIECE, (block + 1) * PIECE)
        total = low_all[y_rows(block, along_y), mine].astype(F32)
        for o in range(3):
            total = total + near_y[o, rows].astype(F32)
        quarter[rows] = total.astype(BF)
    side_copy = send(32, quarter, tail_swap, beside(rep, me))
    side_copy.start()
    small_second()
    to_sibling()
    side_copy.wait()
    quarter[...] = (quarter[...].astype(F32) + tail_swap[...].astype(F32)).astype(BF)
    for o in range(1, SHARDS):
        to = lax.rem(me + o, SHARDS)
        send(32 + o, quarter.at[own_quarter(to)], tail_pieces.at[me], (rep, to)).start()
    tail_pieces[me] = quarter[own_quarter(me), :]
    d_in.cross()
    d_in.last()
    small_third()
    early_done()
    for o in range(1, SHARDS):
        source = lax.rem(me + SHARDS - o, SHARDS)
        send(32 + o, quarter.at[own_quarter(source)], tail_pieces.at[source], (rep, source)).wait()

    @pl.when(core == 0)
    def assemble_first():
        total = tail_pieces[0, :, :BC].astype(F32)
        for block in range(1, SHARDS):
            total = total + tail_pieces[block, :, :BC].astype(F32)
        tail[0, own_piece, :BC] = total.astype(BF)
        for block in range(SHARDS):
            tail[0, own_piece, BC + 128 * block : BC + 128 * block + 128] = tail_pieces[block, :, BC:]

    @pl.when(core == 1)
    def assemble_second():
        total = jnp.zeros((PIECE, 128), F32)
        for block in range(SHARDS):
            tail[1, own_piece, 256 * block : 256 * block + 256] = tail_pieces[block, :, :256]
            put = (iota2((128, 128), 1) == iota2((128, 128), 0) + block * OWN) & (
                iota2((128, 128), 0) < OWN
            )
            total = total + mm(tail_pieces[block, :, 256:], put.astype(BF))
        tail[1, own_piece, 2048:] = total.astype(BF)

    def tail_piece(which, y_at):
        rows = pl.ds(pl.multiple_of(y_at * PIECE, 16), PIECE)
        return tail.at[which, rows, pl.ds(0, TAIL_WIDTH[which])]

    def tail_half(which):
        return tail.at[which, :, pl.ds(0, TAIL_WIDTH[which])]

    def each_core(act):
        for which in range(2):

            @pl.when(core == which)
            def mine_only():
                act(which)

    def spread_tail(which):
        for o in range(1, 4):
            src = tail_piece(which, along_y)
            send(40 + o, src, src, y_peer(o)).start()

    def swap_tail(which):
        for o in range(1, 4):
            src = tail_piece(which, y_of(4 - o))
            send(40 + o, src, tail_piece(which, along_y), y_peer(o)).wait()
        send(58, tail_half(which), tail_half(which), sibling(rep, me)).start()

    def end_tail(which):
        other = tail_half(1 - which)
        send(58, other, other, sibling(rep, me)).wait_recv()
        send(58, tail_half(which), tail_half(which), sibling(rep, me)).wait_send()

    each_core(spread_tail)
    for at in range(MODEL // CH):
        y[at * TOK : (at + 1) * TOK, :] = d_in.part(me, slice(at * CH, (at + 1) * CH))

    each_core(swap_tail)
    small_last()
    d_in.arrived(5, 6, 7)
    load_again.wait()
    def norm_back(at, unused):
        chunk = pl.ds(pl.multiple_of(at * CHUNK, CHUNK), CHUNK)
        rows = stage[0, chunk, :]
        pieces = [
            y[pl.ds(pl.multiple_of(k * TOK + at * CHUNK, CHUNK), CHUNK), :] for k in range(MODEL // CH)
        ]
        d_rows = jnp.concatenate(pieces, axis=1)
        for slot in (4, 5, 6):
            d_rows = d_rows + scatter_in[slot, chunk, :].astype(F32)
        scale = lax.rsqrt(jnp.mean(rows * rows, axis=1, keepdims=True) + epsilon)
        unit = rows * scale
        d_unit = d_rows * norm_gain[...]
        stage[1, chunk, :] += scale * (d_unit - unit * jnp.mean(d_unit * unit, axis=1, keepdims=True))
        return unused

    lax.fori_loop(0, TOK // CHUNK, norm_back, 0)
    store_grad = pltpu.make_async_copy(stage.at[1], grad_out, here.at[7])
    store_grad.start()

    each_core(end_tail)
    store_tail = pltpu.make_async_copy(tail, tail_out, here.at[8])
    store_tail.start()
    d_in.sent()
    gather_x.sent()
    pltpu.make_async_copy(gates, gates_out, here.at[3]).wait()
    pltpu.make_async_copy(outs, outs_out, here.at[10]).wait()
    store_grad.wait()
    store_tail.wait()
    pltpu.make_async_copy(packed_all, small_out, here.at[9]).wait()


def scale_block(b, proj, y, totals, gain, normed_out):
    r0 = pl.multiple_of(b * L, L)
    gate = proj[pl.ds(pl.multiple_of(HALO + b * L, 16), L), :CH].astype(F32)
    inv = to_column(lax.rsqrt(totals[0, pl.ds(b, 1), :] * (1.0 / INNER) + epsilon))
    inv = jnp.concatenate([inv] * (CH // 128), axis=1)
    gated = y[pl.ds(r0, L), :] * (gate * sigmoid(gate))
    normed_out[pl.ds(r0, L), :] = (gated * inv * gain).astype(BF)


def prepare_block(b, proj, y, d_normed, totals, gain, gain_sum):
    r0 = pl.multiple_of(b * L, L)
    here = pl.ds(pl.multiple_of(HALO + b * L, 16), L)
    gate = proj[here, :CH].astype(F32)
    mixer = y[pl.ds(r0, L), :]
    sig = sigmoid(gate)
    silu = gate * sig
    gated = mixer * silu
    inv = lax.rsqrt(totals[0, pl.ds(b, 1), :] * (1.0 / INNER) + epsilon)
    back = inv * inv * inv * totals[1, pl.ds(b, 1), :] * (1.0 / INNER)
    inv = jnp.concatenate([to_column(inv)] * (CH // 128), axis=1)
    back = jnp.concatenate([to_column(back)] * (CH // 128), axis=1)
    dn = d_normed[pl.ds(r0, L), :].astype(F32)
    scaled = gated * inv
    gain_sum[...] += jnp.sum(dn * scaled, axis=0, keepdims=True)
    d_gated = inv * gain * dn - gated * back
    d_normed[pl.ds(r0, L), :] = (d_gated * silu).astype(BF)
    proj[here, :CH] = (d_gated * mixer * (sig + silu * (1.0 - sig))).astype(BF)


def backward_block(
    b, first_len, proj, d_out, taps, shift, step_bias, rate_log, skip, y_in, states, small, heads,
    carry, late,
):
    upper = (iota2((L, L), 1) >= iota2((L, L), 0)).astype(BF)
    columns = head_columns()
    r0 = pl.multiple_of(b * L, L)
    rows = proj[pl.ds(r0, HALO + L), :]
    gate, xbc, conv, raw, step, log_decay, cum = block_front(
        rows, r0, first_len, taps, shift, step_bias, rate_log
    )
    sig = sigmoid(conv)
    act = conv * sig
    x = act[:, BC:]
    b_low = act[:, :STATE].astype(BF)
    c_low = act[:, STATE:BC].astype(BF)
    cum_rows = jnp.transpose(cum)
    scores = mm(c_low, b_low, ((1,), (1,)))
    step_wide = spread(step)
    scaled = x * step_wide
    scaled_low = scaled.astype(BF)
    decays = decay_weights(cum, cum_rows)

    y = y_in[pl.ds(r0, L), :]
    dy_low = d_out[pl.ds(r0, L), :]
    dy = dy_low.astype(F32)

    state = states[b]
    end_state = states[b + 1]
    d_state = carry[...]
    state_low = state.astype(BF)
    d_state_low = d_state.astype(BF)
    enter = spread(jnp.exp(cum))
    tail = spread(jnp.exp(cum[L - 1 : L] - cum))
    lane = iota2((L, 128), 1)
    d_scores = jnp.zeros((L, L), F32)
    weights = []
    for h in range(OWN):
        part = slice(128 * (h // 2), 128 * (h // 2) + 128)
        mine = (lane < HEAD_DIM) if h % 2 == 0 else (lane >= HEAD_DIM)
        d_weight = mm(
            dy_low[:, part],
            jnp.where(mine, scaled[:, part], 0.0).astype(BF),
            ((1,), (1,)),
        )
        d_scores = d_scores + d_weight * decays[h]
        weights.append((decays[h] * scores).astype(BF))
    d_scores_low = d_scores.astype(BF)
    d_scaled = pair_mix(weights, dy_low, ((0,), (0,)))
    d_scaled = d_scaled + tail * mm(b_low, d_state_low, ((1,), (1,)))
    enter_dy = (enter * dy).astype(BF)
    d_c = mm(d_scores_low, b_low) + mm(enter_dy, state_low)
    d_b = mm(d_scores_low, c_low, ((0,), (0,))) + mm((tail * scaled).astype(BF), d_state_low)

    ssm = y - skip * x
    pieces = split(dy_low.astype(F32) * ssm - scaled_low.astype(F32) * d_scaled, 2)
    pieces += split(d_scaled * x, 2)
    sums = mm(jnp.concatenate(pieces, axis=0), columns)
    d_cum = sums[:L] + sums[L : 2 * L]
    inner = end_state * d_state
    heads_lane = iota2((1, 128), 1)
    through = jnp.zeros((1, 128), F32)
    for h in range(OWN):
        total = jnp.sum(inner[HEAD_DIM * h : HEAD_DIM * h + HEAD_DIM], axis=0, keepdims=True)
        total = jnp.sum(total, axis=1, keepdims=True)
        through = through + jnp.where(heads_lane == h, total, 0.0)
    d_cum = d_cum + jnp.where(iota2((L, 1), 0) == L - 1, through, 0.0)
    d_log = mm_left(upper, d_cum, 2)
    d_step = sums[2 * L : 3 * L] + sums[3 * L :] - jnp.exp(rate_log) * d_log
    d_raw = d_step * sigmoid(raw)
    d_x = d_scaled * step_wide + skip * dy

    carry[...] = head_rows(cum_rows, L - 1) * d_state + mm(enter_dy, c_low, ((0,), (0,)))

    d_act = jnp.concatenate([d_b, d_c, d_x], axis=1)
    d_conv = d_act * (sig + act * (1.0 - sig))
    row = r0 + iota2((L + 8, 1), 0)
    longer = jnp.concatenate([d_conv, late[...]], axis=0)
    late[...] = d_conv[:8]
    d_xbc = jnp.zeros((L, XBC), F32)
    for k in range(CONV):
        ahead = CONV - 1 - k
        masked = longer
        if ahead:
            masked = longer * tap_mask(row, first_len, ahead)
        d_xbc = d_xbc + taps[k : k + 1] * masked[ahead : ahead + L]
        small[k : k + 1, :] += jnp.sum(
            masked[:L] * xbc[HALO - ahead : HALO - ahead + L], axis=0, keepdims=True
        )
    small[4:5, :] += jnp.sum(d_conv, axis=0, keepdims=True)
    small[5:6, :CH] += jnp.sum(dy * x, axis=0, keepdims=True)
    heads[0:1, :] += jnp.sum(d_raw, axis=0, keepdims=True)
    heads[1:2, :] += jnp.sum(d_log * log_decay, axis=0, keepdims=True)
    proj[pl.ds(pl.multiple_of(HALO + b * L, 16), L), CH:] = jnp.concatenate(
        [d_xbc, d_raw], axis=1
    ).astype(BF)


def finish_kernel(
    mixed_in, grad_in, gates_in, tail_in, outs_in, packed, mixed, grad, norm_grad, in_grad, conv_grad, bias_grad,
    dt_grad, rate_grad, skip_grad, gain_grad, out_grad,
    mixed_here, grad_here, gates, tail, outs, in_here, out_here, into, out,
):
    loads = [
        pltpu.make_async_copy(src, dst, into.at[at])
        for at, (src, dst) in enumerate(
            ((outs_in, outs), (gates_in, gates), (tail_in, tail), (mixed_in, mixed_here), (grad_in, grad_here))
        )
    ]
    for load in loads:
        load.start()
    stores = []

    def store(src, dst):
        stores.append(pltpu.make_async_copy(src, dst, out.at[len(stores)]))
        stores[-1].start()

    loads[0].wait()
    out_here[...] = outs[...].astype(F32)
    store(out_here, out_grad.at[0])
    loads[1].wait()
    loads[2].wait()
    for chunk in range(0, ROWS, PIECE):
        rows = slice(chunk, chunk + PIECE)
        in_here[rows, :INNER] = gates[rows, :].astype(F32)
        for s in range(SHARDS):
            begin = INNER + CH * s
            in_here[rows, begin : begin + 128] = tail[0, rows, BC + 128 * s : BC + 128 * s + 128].astype(F32)
            in_here[rows, begin + 128 : begin + CH] = tail[1, rows, 256 * s : 256 * s + 256].astype(F32)
        in_here[rows, 2 * INNER : 2 * INNER + BC] = tail[0, rows, :BC].astype(F32)
        in_here[rows, 2 * INNER + BC :] = tail[1, rows, 2048 : 2048 + HEADS].astype(F32)
        store(in_here.at[pl.ds(chunk, PIECE)], in_grad.at[0, pl.ds(chunk, PIECE)])
    loads[3].wait()
    store(mixed_here, mixed)
    loads[4].wait()
    store(grad_here, grad)
    parts = [packed[s] for s in range(SHARDS)]
    both = parts[0][:, :BC]
    for s in range(1, SHARDS):
        both = both + parts[s][:, :BC]
    conv_grad[0, :, INNER:] = both[:CONV]
    bias_grad[:, INNER:] = both[CONV : CONV + 1]
    heads = [jnp.zeros((8, 128), F32)] * 3
    for s in range(SHARDS):
        own = slice(CH * s, CH * s + CH)
        conv_grad[0, :, own] = parts[s][:CONV, BC:XBC]
        bias_grad[:, own] = parts[s][CONV : CONV + 1, BC:XBC]
        gain_grad[:, own] = parts[s][5:6, CH : 2 * CH]
        put = (iota2((128, 128), 1) == iota2((128, 128), 0) + s * OWN) & (iota2((128, 128), 0) < OWN)
        put_wide = iota2((CH, 128), 1) == iota2((CH, 128), 0) // HEAD_DIM + s * OWN
        rows = (
            (parts[s][5:6, 2 * CH : 2 * CH + 128], put),
            (parts[s][5:6, 2 * CH + 128 : 2 * CH + 256], put),
            (parts[s][5:6, :CH], put_wide),
        )
        for at, (row, to) in enumerate(rows):
            wide = jnp.broadcast_to(row, (8, row.shape[1]))
            heads[at] = heads[at] + mm_right(wide, to.astype(BF), 3)
    for at, ref in enumerate((dt_grad, rate_grad, skip_grad)):
        ref[...] = heads[at][0:1, :HEADS]
    total = parts[0][6:7]
    for s in range(1, SHARDS):
        total = total + parts[s][6:7]
    norm_grad[...] = total
    for copy in stores:
        copy.wait()


VM = pl.BlockSpec(memory_space=pltpu.VMEM)
SM = pl.BlockSpec(memory_space=pltpu.SMEM)
ANY = pl.BlockSpec(memory_space=pl.ANY)
LIMIT = 61 << 20


def local(
    resid,
    cotangent,
    first_length,
    norm_gain,
    in_weight,
    conv_weight,
    conv_bias,
    dt_bias,
    a_log,
    skip,
    gate_gain,
    out_weight,
):
    w = in_weight[0]
    narrow = lax.pad(w, jnp.zeros((), BF), ((0, 0, 0), (-2 * INNER, 4 * 128 - BC - HEADS, 0)))
    dma = pltpu.SemaphoreType.DMA
    outs = (
        ((TOK, MODEL), F32), ((TOK, MODEL), F32), ((ROWS, INNER), BF), ((2, ROWS, TAIL), BF),
        ((CH, MODEL), BF), ((SHARDS, 8, MODEL), F32),
    )
    scratch = (
        ((GROUP, MODEL), BF), ((GROUP, MODEL), BF), ((2, MODEL, HALF), BF),
        ((HALO + GROUP, COLS), BF), ((GROUP, CH), F32), ((NB + 1, CH, STATE), F32), ((GROUP, CH), BF),
        ((SHARDS, 2, NB, L), F32), ((CH, STATE), F32), ((2, TOK, MODEL), F32), ((CONV, XBC), F32),
        ((1, XBC), F32),
        ((2, NB, L), F32), ((GROUP, CH), BF), ((1, CH), F32), ((8, MODEL), F32), ((8, XBC), F32),
        ((8, 128), F32),
        ((8, XBC), F32), ((7, TOK, MODEL), BF), ((7, TOK, MODEL), BF),
        ((3, QUARTER, CH), BF), ((CH, HALF_OUT), BF), ((HALF_OUT, CH), BF), ((3, 96, HALF_OUT), BF),
        ((3, QUARTER // 2, CH), BF), ((96, HALF_OUT), BF), ((QUARTER // 2, CH), BF),
        ((96, HALF_OUT), BF), ((QUARTER // 2, CH), BF),
        ((QUARTER, CH), BF),
        ((ROWS, INNER), BF), ((CH, MODEL), BF),
        ((QUARTER, CH), BF),
        ((SHARDS, PIECE, CH), BF), ((2, ROWS, TAIL), BF),
        ((2, 8, MODEL), F32), ((2, 8, MODEL), F32), ((4, 8, MODEL), F32), ((SHARDS, 8, MODEL), F32),
    )
    mixed, grad, gates, tail, out_grad, packed = pl.pallas_call(
        layer_kernel,
        out_shape=tuple(jax.ShapeDtypeStruct(*shape) for shape in outs),
        in_specs=[SM, ANY, ANY, ANY, ANY] + [VM] * 8,
        out_specs=(ANY,) * 6,
        scratch_shapes=[pltpu.VMEM(*shape) for shape in scratch]
        + [dma((11,))] * 4 + [dma((SHARDS,))] * 2 + [dma((4,))] * 2 + [dma((1,))] * 2
        + [dma((2 * SHARDS,))] * 2 + [dma((11,))] + [dma((10,))] * 4 + [dma((60,))] * 2 + [dma((SHARDS,))] * 2
        + [pltpu.SemaphoreType.REGULAR] * 2,
        compiler_params=pltpu.CompilerParams(
            vmem_limit_bytes=LIMIT, collective_id=0, has_side_effects=True
        ),
    )(
        first_length, resid, cotangent, w, narrow, out_weight[0], norm_gain, conv_weight[0], conv_bias,
        dt_bias, a_log, skip, gate_gain,
    )
    wide = CONVCH
    shapes = (
        (TOK, MODEL), (TOK, MODEL), (1, MODEL), (1, ROWS, 2 * INNER + BC + HEADS), (1, CONV, wide), (1, wide),
        (1, HEADS), (1, HEADS), (1, HEADS), (1, INNER), (1, CH, MODEL),
    )
    return pl.pallas_call(
        finish_kernel,
        out_shape=tuple(jax.ShapeDtypeStruct(shape, F32) for shape in shapes),
        in_specs=[ANY] * 5 + [VM],
        out_specs=(ANY, ANY, VM, ANY) + (VM,) * 6 + (ANY,),
        scratch_shapes=[
            pltpu.VMEM((TOK, MODEL), F32), pltpu.VMEM((TOK, MODEL), F32), pltpu.VMEM((ROWS, INNER), BF),
            pltpu.VMEM((2, ROWS, TAIL), BF), pltpu.VMEM((CH, MODEL), BF),
            pltpu.VMEM((ROWS, 2 * INNER + BC + HEADS), F32), pltpu.VMEM((CH, MODEL), F32), dma((5,)), dma((7,)),
        ],
        compiler_params=pltpu.CompilerParams(vmem_limit_bytes=LIMIT),
    )(mixed, grad, gates, tail, out_grad, packed)


def solution(mesh):
    rows = P(("rep", "shard"), None)
    weight = P(None, "shard", None)
    return jax.shard_map(
        local,
        mesh=mesh,
        in_specs=(rows, rows, P("rep"), P(), weight, P(), P(), P(), P(), P(), P(), weight),
        out_specs=(rows, rows, P(), weight, P(), P(), P(), P(), P(), P(), weight),
        check_vma=False,
    )
```
